32 devices in a mesh: shot: 8 (over y, x, core), freq: 4 (over z).
Axes of the slice: x: 2, y: 2, z: 4, core: 2. Of those that a mesh axis runs over, the one named last changes fastest.
Arguments:
- traces: float32 [24, 256, 1024], P('shot', None, 'freq'), may hold values from -6 to 6
- live_mask: int32 [24, 256], P('shot'), may hold values 0 or 1
- offset_bin: int32 [24, 256, 1], P('shot'), may hold values from 0 to 31; in each aligned block of 768 rows (0 to 767, 768 to 1535, ..., all dimensions but the last counted through in order) at most 36 rows name the same one
- surface: float32 [128, 256, 512], P('shot', None, 'freq'), may hold values from -2.5 to 2.5
- block_owner: int32 [2], replicated, may hold values from 0 to 7
- point_column: int32 [2, 16], replicated, may hold values from 0 to 255
- filters: float32 [32, 31], P('shot'), may hold values from -1 to 1
Outputs:
- primaries: float32 [32, 288, 1024], P('shot', None, 'freq')
The draws below stay inside these ranges and needn't reach their ends.
Inputs may be any that keep to these rules, and one draw needn't show every extreme that they name: `offset_bin`: among the traces of one group of 3 consecutive shots (the rows of one device) no bin holds more than 36 traces, and in every draw some group has a bin with exactly 36; every bin holds some trace.
All inputs are finite; a program needn't handle non-finite values. No bound on the sum of `live_mask` on one device may be relied on, other than what follows from the above.
Results may differ from the reference program's by a relative error of at most 0.0003.
Values sent between devices are 32-bit elements; how exact they have to be, the bound alone decides.
No kernel may reach another device: no remote copies, remote signals or barrier semaphores. Data moves between devices by JAX's collectives and lax.ppermute only.
A program may use at most 64 MiB of HBM per device.

```python
import math
import jax
import jax.numpy as jnp
import numpy as np
from jax import lax

R = 256
NT = 1024
NF = 256
TAPS = 31
POINTS_BLK = 16
STEPS = 2
SHOT_DEV = 3
SHOTS = 24
POINTS = 128
NBINS = 32
MOST = 36
GROUP_SLOTS = 288
N_SHOT = 8
N_FREQ = 4


def with_ends(drawn, own_key, low, high):
    longest = drawn.shape.index(max(drawn.shape))
    spots = []
    for shift in (0, 1):
        where = [jax.random.randint(jax.random.fold_in(own_key, axis), (), 0, length) for axis, length in enumerate(drawn.shape)]
        where[longest] = (where[longest] + shift) % drawn.shape[longest]
        spots.append(tuple(where))
    return drawn.at[spots[0]].set(low).at[spots[1]].set(high)


def shard_levels(own_key, extent, shards, low, top_value):
    factor_of = 1.0
    for position, parts in shards:
        steps = jax.random.uniform(jax.random.fold_in(jax.random.fold_in(own_key, 6), position), (parts,), jnp.float32, low / len(shards), top_value / len(shards))
        factor_of = factor_of * jnp.repeat(jnp.exp(steps), extent[position] // parts).reshape((-1,) + (1,) * (len(extent) - 1 - position))
    return factor_of


def deal_out(own_key, own, number, rows, count, top, reach, lean):
    order = jax.random.permutation(own_key, count)
    crowded, ordinary = shares(count, rows * top, reach, lean, True), shares(count, rows * top, reach, lean, False)
    places = jnp.arange(count)

    def named(lengths, offset_by):
        used = int((lengths > 0).sum())
        fixed = max(1, used // 4)
        shifted = fixed + (places - fixed + offset_by * (used - fixed)) % max(1, count - fixed)
        return jnp.zeros((count,), jnp.int32).at[order[jnp.where(places < fixed, places, shifted)]].set(jnp.asarray(lengths, jnp.int32))

    lengths = jnp.where(number % 4 == 0, named(crowded, number // 4), named(ordinary, number - number // 4 - 1))
    mixed = jax.random.permutation(jax.random.fold_in(own, 3), count)
    source_of, taker = mixed[0:count // 2 * 2:2], mixed[1:count // 2 * 2:2]
    margin = jnp.minimum(lengths[source_of] - 1, reach - lengths[taker]) // 2
    margin = jnp.where((source_of == order[0]) | (taker == order[0]) | (lengths[taker] == 0), 0, jnp.maximum(margin, 0))
    shifted = jax.random.randint(jax.random.fold_in(own, 4), (count // 2,), 0, 1 << 20) % (margin + 1)
    lengths = lengths.at[source_of].add(-shifted).at[taker].add(shifted)
    members = jnp.searchsorted(jnp.cumsum(lengths), jnp.arange(rows * top), side="right").astype(jnp.int32)
    grid = members.reshape(top, rows).T
    grid = grid[jax.random.permutation(jax.random.fold_in(own, 1), rows)]
    offset_by = jax.random.randint(jax.random.fold_in(own, 2), (rows, 1), 0, top)
    return jnp.take_along_axis(grid, (jnp.arange(top)[None, :] + offset_by) % top, axis=1)


def shares(number_of, total, bound, slope, full):
    portions = [(1 << 20) // math.isqrt(rank ** slope) + 1 for rank in range(1, number_of + 1)]
    largest = bound if full else min(bound, max(-(-total // number_of), total * portions[0] // sum(portions)))
    least = 1 if total - largest >= number_of - 1 else 0
    counts, spare = [largest] + [least] * (number_of - 1), total - largest - least * (number_of - 1)
    while spare > 0:
        free = [i for i in range(1, number_of) if counts[i] < largest] or [i for i in range(1, number_of) if counts[i] < bound]
        pool, remaining = sum([portions[i] for i in free]), spare
        for i in free:
            extra = min(bound - counts[i], max(1, remaining * portions[i] // pool), spare)
            counts[i] = counts[i] + extra
            spare = spare - extra
    return np.array(counts)


def noise(own_key, dims, scale, limit, cuts=(), kind=jnp.bfloat16):
    result = jax.random.normal(own_key, dims, jnp.float32) * scale
    if len(cuts) > 0:
        result = shard_levels(own_key, dims, cuts, -0.22, 0.18) * result
    return jnp.clip(result, min=-limit, max=limit).astype(kind)


def setup_inputs(seed: int = 0) -> dict:
    splits = jax.random.split(jax.random.key(seed), 8)
    traces = noise(splits[0], (SHOTS, R, NT), 1.0, 6.0, ((0, 8), (2, 4)), jnp.float32)
    live_mask = with_ends((jax.random.randint(splits[1], (SHOTS, R), 0, 8) < 7).astype(jnp.int32), jax.random.fold_in(splits[1], 1), 0, 1)
    offset_bin_keys = jax.random.split(jax.random.fold_in(splits[2], 1), SHOTS * R // (SHOT_DEV * R))
    offset_bin_turns = jax.random.permutation(jax.random.fold_in(splits[2], 3), SHOTS * R // (SHOT_DEV * R))
    offset_bin = jax.vmap(lambda own, number: deal_out(jax.random.fold_in(splits[2], 2), own, number, SHOT_DEV * R, NBINS, 1, MOST, 1))(offset_bin_keys, offset_bin_turns).reshape((SHOTS, R, 1))
    surface = noise(splits[3], (POINTS, R, 2 * NF), ((NT / (4 * STEPS * POINTS_BLK * NF)) ** 0.5), 2.5, ((0, 8), (2, 4)), jnp.float32)
    block_owner = jax.random.randint(splits[4], (STEPS,), 0, N_SHOT).astype(jnp.int32)
    point_column = with_ends(jax.random.randint(splits[5], (STEPS, POINTS_BLK), 0, R), jax.random.fold_in(splits[5], 1), 0, R - 1).astype(jnp.int32)
    filters = noise(splits[6], (NBINS, TAPS), TAPS ** -0.5, 1.0, ((0, 8),), jnp.float32)
    return dict(traces=traces, live_mask=live_mask, offset_bin=offset_bin, surface=surface, block_owner=block_owner, point_column=point_column, filters=filters)


FULL_PRECISION = lax.Precision.HIGHEST


def wave_table(time_ids, comp_ids, band_width, period):
    mode_ids = (comp_ids // (2 * band_width)) * band_width + comp_ids % band_width
    phase_ids = ((mode_ids[None, :] + 1) * time_ids[:, None]) % period
    angles = phase_ids.astype(jnp.float32) * (2.0 * math.pi / period)
    real_part = (comp_ids % (2 * band_width)) < band_width
    return jnp.where(real_part[None, :], jnp.cos(angles), -jnp.sin(angles))


def cross_mix(left_side, right_side):
    return jnp.einsum("sjgb,jrgb->srgb", left_side, right_side, precision=FULL_PRECISION)


def shifted_sum(widened, tap_table, out_width):
    half_span = (tap_table.shape[-1] - 1) // 2
    summed = jnp.zeros(widened.shape[:-1] + (out_width,), jnp.float32)
    for tap_index in range(tap_table.shape[-1]):
        offset_start = 2 * half_span - tap_index
        window = lax.slice_in_dim(widened, offset_start, offset_start + out_width, axis=widened.ndim - 1)
        summed = summed + tap_table[..., tap_index:tap_index + 1] * window
    return summed


def group_ranks(group_bins):
    order_ids = jnp.arange(group_bins.shape[0])
    earlier = (group_bins[:, None] == group_bins[None, :]) & (order_ids[None, :] < order_ids[:, None])
    return jnp.sum(earlier.astype(jnp.int32), axis=1)


def reference(traces, live_mask, offset_bin, surface, block_owner, point_column, filters):
    band_width = NF // N_FREQ
    live_rows = live_mask.astype(jnp.float32)[:, :, None]
    live_traces = traces * live_rows
    columns = point_column.reshape(-1)
    picked = live_traces[:, columns, :]
    table_full = wave_table(jnp.arange(NT), jnp.arange(2 * NF), band_width, NT)
    spectra = jnp.einsum("sjt,tc->sjc", picked, table_full, precision=FULL_PRECISION)
    spectra = spectra.reshape(SHOTS, STEPS * POINTS_BLK, N_FREQ, 2, band_width)
    real_sum = jnp.zeros((SHOTS, R, N_FREQ, band_width), jnp.float32)
    imag_sum = jnp.zeros((SHOTS, R, N_FREQ, band_width), jnp.float32)
    for step_index in range(STEPS):
        first_point = (block_owner[step_index] * POINTS_BLK).astype(jnp.int32)
        surface_part = lax.dynamic_slice_in_dim(surface, first_point, POINTS_BLK, 0)
        surface_part = surface_part.reshape(POINTS_BLK, R, N_FREQ, 2, band_width)
        point_spectra = spectra[:, step_index * POINTS_BLK:(step_index + 1) * POINTS_BLK]
        data_real = point_spectra[:, :, :, 0]
        data_imag = point_spectra[:, :, :, 1]
        surf_real = surface_part[:, :, :, 0]
        surf_imag = surface_part[:, :, :, 1]
        real_sum = real_sum + (cross_mix(data_real, surf_real) - cross_mix(data_imag, surf_imag))
        imag_sum = imag_sum + (cross_mix(data_real, surf_imag) + cross_mix(data_imag, surf_real))
    prediction = jnp.stack([real_sum, imag_sum], axis=3).reshape(SHOTS, R, 2 * NF)
    inverse = table_full.T * (2.0 / NT)
    multiples = jnp.einsum("src,ct->srt", prediction, inverse, precision=FULL_PRECISION) * live_rows
    half_span = (TAPS - 1) // 2
    widened = jnp.pad(multiples, ((0, 0), (0, 0), (half_span, half_span)))
    bins_full = offset_bin[:, :, 0]
    trace_taps = filters[bins_full]
    cleaned = live_traces - shifted_sum(widened, trace_taps, NT)
    rank_ids = lax.map(group_ranks, bins_full.reshape(N_SHOT, SHOT_DEV * R)).reshape(SHOTS, R)
    group_ids = (jnp.arange(SHOTS) // SHOT_DEV)[:, None]
    slot_ids = group_ids * MOST + rank_ids
    return jnp.zeros((NBINS, GROUP_SLOTS, NT), jnp.float32).at[bins_full, slot_ids].set(cleaned)
```

```python
import functools
import math

import jax
import jax.numpy as jnp
import numpy as np
from jax import lax
from jax.experimental import pallas as pl
from jax.experimental.pallas import tpu as pltpu
from jax.sharding import PartitionSpec as P

NT = 1024
NF = 256
TAPS = 31
POINTS_BLK = 16
STEPS = 2
RIM = 16
PARTS = 2

FULL_PRECISION = lax.Precision.HIGHEST
VMEM = pl.BlockSpec(memory_space=pltpu.VMEM)
SMEM = pl.BlockSpec(memory_space=pltpu.SMEM)
ANY = pl.BlockSpec(memory_space=pl.ANY)


def wave_constant(bands):
    width = NF // bands
    comps = np.arange(2 * NF)
    modes = comps // (2 * width) * width + comps % width
    phases = (modes[None, :] + 1) * np.arange(NT)[:, None] % NT
    angles = phases * (2.0 * math.pi / NT)
    table = np.where((comps % (2 * width) < width)[None, :], np.cos(angles), -np.sin(angles))
    table = np.pad(table, ((RIM, RIM), (0, 0))).astype(np.float32)
    high = table.astype(jnp.bfloat16)
    low = (table - high.astype(np.float32)).astype(jnp.bfloat16)
    return high, low


def tap_constant(bands, lanes):
    high, low = wave_constant(bands)
    table = high.astype(np.float32) + low.astype(np.float32)
    shifts = (np.arange(TAPS) - (TAPS - 1) // 2) % NT
    return np.pad(table[RIM + shifts], ((0, lanes - TAPS), (0, 0)))


def split_two(value):
    high = value.astype(jnp.bfloat16)
    return high, (value - high.astype(jnp.float32)).astype(jnp.bfloat16)


def dot_nn(left, right):
    return lax.dot_general(left, right, (((1,), (0,)), ((), ())), preferred_element_type=jnp.float32)


def dot_nt(left, right):
    return lax.dot_general(left, right, (((1,), (1,)), ((), ())), preferred_element_type=jnp.float32)


def run_all(copies):
    for copy in copies:
        copy.start()
    for copy in copies:
        copy.wait()


def swap(value, axis, count, bit):
    return lax.ppermute(value, axis, [(i, i ^ bit) for i in range(count)])


def spectra_kernel(cols, live, traces, high, low, *rest):
    outs, (picked, tab_high, tab_low, part, sems) = rest[:4], rest[4:]
    shots, _, quarter = traces.shape
    z = lax.axis_index("freq")
    rows = pl.ds(pl.multiple_of(RIM + z * quarter, 16), quarter)
    loads = [
        pltpu.make_async_copy(high.at[rows], tab_high, sems.at[0]),
        pltpu.make_async_copy(low.at[rows], tab_low, sems.at[1]),
    ]
    for load in loads:
        load.start()
    per_block = cols.shape[1]
    points = cols.shape[0] * per_block
    for j in range(points):
        col = cols[j // per_block, j % per_block]
        for s in range(shots):
            row = traces[s, pl.ds(col, 1), :]
            picked[s * points + j : s * points + j + 1, :] = row * live[s, col].astype(jnp.float32)
    for load in loads:
        load.wait()
    left_high, left_low = split_two(picked[...])
    part[...] = (
        dot_nn(left_high, tab_high[...]) + dot_nn(left_low, tab_high[...]) + dot_nn(left_high, tab_low[...])
    )
    lanes = outs[0].shape[1]
    for k, out in enumerate(outs):
        out[...] = part[:, pl.ds(pl.multiple_of((z ^ k) * lanes, lanes), lanes)]


def sibling_kernel(surface, out, sem):
    half = out.shape[1]
    core = lax.axis_index("shot") % 2
    copy = pltpu.make_async_copy(surface.at[:, pl.ds(pl.multiple_of((1 - core) * half, 8), half)], out, sem)
    copy.start()
    copy.wait()


def pieces_kernel(surface, sibling, *outs):
    d = lax.axis_index("shot")
    chip, core = d // 2, d % 2
    half = sibling.shape[1]
    size = outs[0].shape[2]
    for k, out in enumerate(outs):
        to, part = chip ^ (1 + k // PARTS), k % PARTS
        first = to * (size * PARTS) + part * size
        out[core] = surface[:, pl.ds(pl.multiple_of(core * half + first, 8), size), :]
        out[1 - core] = sibling[:, pl.ds(pl.multiple_of(first, 8), size), :]


def prediction_kernel(part, owners, surface, sibling, *rest):
    sent, spectra, outs = rest[:3], rest[3:7], rest[7:11]
    chosen, real_side, imag_side, sems = rest[11:]
    d = lax.axis_index("shot")
    chip, core = d // 2, d % 2
    half = sibling.shape[1]
    size = chosen.shape[2]
    first = chip * (size * PARTS) + part * size
    for b in range(STEPS):
        owner = owners[b]
        step, owner_core = (owner // 2) ^ chip, owner % 2

        @pl.when((step == 0) & (owner_core == core))
        def _():
            rows = pl.ds(pl.multiple_of(core * half + first, 8), size)
            pltpu.make_async_copy(surface.at[:, rows], chosen.at[b], sems.at[b]).start()

        @pl.when((step == 0) & (owner_core != core))
        def _():
            rows = pl.ds(pl.multiple_of(first, 8), size)
            pltpu.make_async_copy(sibling.at[:, rows], chosen.at[b], sems.at[b]).start()

        for k in range(3):

            @pl.when(step == k + 1)
            def _():
                pltpu.make_async_copy(sent[k].at[owner_core], chosen.at[b], sems.at[b]).start()

    points = STEPS * POINTS_BLK
    rows = real_side.shape[1]
    shots = rows // points
    lanes = chosen.shape[3]
    lane = lax.broadcasted_iota(jnp.int32, (rows, lanes), 1)
    for q in range(4):
        for c in range(2):
            value = spectra[q][c, :rows, :]
            turned = pltpu.roll(value, lanes // 2, 1)
            real_side[2 * q + c] = jnp.where(lane < lanes // 2, value, turned)
            imag_side[2 * q + c] = jnp.where(lane < lanes // 2, turned, -value)
    for b in range(STEPS):
        pltpu.make_async_copy(sibling.at[:, pl.ds(0, size)], chosen.at[b], sems.at[b]).wait()

    for q in range(4):

        @pl.loop(0, 2)
        def _(rel):
            at = 2 * q + (core ^ rel)
            first_sum = [jnp.zeros((size, lanes), jnp.float32)] * shots
            second_sum = [jnp.zeros((size, lanes), jnp.float32)] * shots
            for j in range(points):
                block = chosen[j // POINTS_BLK, j % POINTS_BLK]
                for s in range(shots):
                    row = s * points + j
                    first_sum[s] = first_sum[s] + real_side[at, row : row + 1, :] * block
                    second_sum[s] = second_sum[s] + imag_side[at, row : row + 1, :] * block
            for s in range(shots):
                outs[q][rel * shots + s] = first_sum[s] + pltpu.roll(second_sum[s], lanes // 2, 1)


def arrange_kernel(own, first, second, third, out):
    chip = lax.axis_index("shot") // 2
    for q, piece in enumerate((own, first, second, third)):
        out[:, chip ^ q] = piece[...]


def slots_kernel(most, bins, live, places):
    total = bins.shape[1]
    bins_total = places.shape[0] // most
    member = (lax.broadcasted_iota(jnp.int32, (bins_total, total), 0) == bins[...]).astype(jnp.float32)
    before = lax.broadcasted_iota(jnp.int32, (total, total), 0) < lax.broadcasted_iota(jnp.int32, (total, total), 1)
    counts = dot_nn(member.astype(jnp.bfloat16), before.astype(jnp.float32).astype(jnp.bfloat16))
    rank = jnp.sum(counts * member, axis=0, keepdims=True)
    slot = bins[...] * most + rank.astype(jnp.int32)
    slot = jnp.where(live[...] != 0, slot, -1)
    at = lax.broadcasted_iota(jnp.int32, places.shape, 0)
    places[...] = (at == slot).astype(jnp.float32).astype(jnp.bfloat16)


def response_kernel(own_bins, bins, waves, *rest):
    spectra, (taps, same_side, cross_side, filters) = rest[:4], rest[4:]
    chip = lax.axis_index("shot") // 2
    z = lax.axis_index("freq")
    lines = spectra[0].shape[1]
    for q in range(4):
        for c in range(2):
            filters[(chip ^ q) * 2 + c] = spectra[q][c, lines - 8 :, :]
    devices, padded, lanes = filters.shape
    shape = (devices * padded, bins.shape[1])
    row = lax.broadcasted_iota(jnp.int32, shape, 0)
    bin_of_row = jnp.where(row % padded < own_bins, row // padded * own_bins + row % padded, -1)
    member = (bin_of_row == bins[...]).astype(jnp.float32).astype(jnp.bfloat16)

    def per_trace(table):
        high, low = split_two(table)
        dims = (((0,), (0,)), ((), ()))
        return lax.dot_general(member, high, dims, preferred_element_type=jnp.float32) + lax.dot_general(
            member, low, dims, preferred_element_type=jnp.float32
        )

    table = filters[...].reshape(devices * padded, lanes)
    taps[...] = per_trace(table)
    lane = lax.broadcasted_iota(jnp.int32, (devices * padded, lanes), 1)
    for slot, step in enumerate((0, 3, 1, 2)):
        cols = pl.ds(pl.multiple_of((z + step) % 4 * lanes, lanes), lanes)
        answer = jnp.dot(table, waves[:, cols], precision=FULL_PRECISION, preferred_element_type=jnp.float32)
        turned = pltpu.roll(answer, lanes // 2, 1)
        into = slice(slot * lanes, (slot + 1) * lanes)
        same_side[:, into] = per_trace(jnp.where(lane < lanes // 2, answer, turned))
        cross_side[:, into] = per_trace(jnp.where(lane < lanes // 2, -turned, answer))


def clean_kernel(keep, got, traces, places, out, high, low):
    core = lax.axis_index("shot") % 2
    shots, receivers, _ = traces.shape
    half = keep.shape[1]
    for source, side in ((keep, core), (got, 1 - core)):
        for s in range(shots):
            first = pl.multiple_of(side * half, half)
            flat = pl.ds(pl.multiple_of(s * receivers + first, half), half)
            clean_high, clean_low = split_two(traces[s, pl.ds(first, half), :] - source[s])
            high[flat, :] = clean_high
            low[flat, :] = clean_low
    out[...] = dot_nn(places[...], high[...]) + dot_nn(places[...], low[...])


def inverse_kernel(high, low, taps, same_side, cross_side, *rest):
    bands = [rest[5 * p : 5 * p + 5] for p in range(PARTS)]
    keep, send = rest[5 * PARTS : 5 * PARTS + 2]
    gathered, tab_high, tab_low, end_high, end_low, sems, tab_sems = rest[5 * PARTS + 2 :]
    z = lax.axis_index("freq")
    lanes = bands[0][0].shape[3]
    quarter = tab_high.shape[0]
    loads = []
    rows = pl.ds(pl.multiple_of(RIM + z * quarter, 16), quarter)
    end_rows = pl.ds(pl.multiple_of(jnp.where(z == 0, NT, RIM), 16), RIM)
    for slot, step in enumerate((0, 3, 1, 2)):
        cols = pl.ds(pl.multiple_of((z + step) % 4 * lanes, lanes), lanes)
        into = pl.ds(slot * lanes, lanes)
        pairs = ((high, rows, tab_high), (low, rows, tab_low), (high, end_rows, end_high), (low, end_rows, end_low))
        for i, (table, some, scratch) in enumerate(pairs):
            loads.append(pltpu.make_async_copy(table.at[some, cols], scratch.at[:, into], tab_sems.at[4 * slot + i]))
    for load in loads:
        load.start()

    def fetch(source, p, slot):
        into = gathered.at[:, :, p, :, pl.ds(slot * lanes, lanes)]
        return pltpu.make_async_copy(source, into, sems.at[4 * p + slot])

    for p in range(PARTS):
        own, right, left, across, forward = bands[p]
        fetch(own, p, 0).start()
        fetch(across, p, 3).start()

        @pl.when(z > 0)
        def _():
            fetch(right, p, 1).start()

        @pl.when(z == 0)
        def _():
            fetch(forward, p, 1).start()

        @pl.when(z < 3)
        def _():
            fetch(left, p, 2).start()

        @pl.when(z == 3)
        def _():
            fetch(forward, p, 2).start()

    for load in loads:
        load.wait()
    for p in range(PARTS):
        for slot in range(4):
            fetch(bands[p][0], p, slot).wait()
    shots, count, _ = keep.shape

    def transform(value, into_high, into_low):
        left_high, left_low = split_two(value)
        full = dot_nt(left_high, into_high[...]) + dot_nt(left_low, into_high[...]) + dot_nt(left_high, into_low[...])
        return full * (2.0 / NT)

    for s in range(2 * shots):
        value = gathered[s].reshape(count, 4 * lanes)
        rolled = [pltpu.roll(value[:, i * lanes : (i + 1) * lanes], lanes // 2, 1) for i in range(4)]
        turned = jnp.concatenate(rolled, axis=1)
        some = slice(s * count, (s + 1) * count)
        answer = value * same_side[some, :] + turned * cross_side[some, :]
        target, at = (keep, s) if s < shots else (send, s - shots)
        target[at] = transform(answer, tab_high, tab_low)

        @pl.when((z == 0) | (z == 3))
        def _(value=value, some=some, target=target, at=at):
            ends = transform(value, end_high, end_low)
            lane = lax.broadcasted_iota(jnp.int32, (count, lanes), 1)
            moved = pltpu.roll(taps[some, :], jnp.where(z == 0, lanes - 2 * RIM + 1, lanes - RIM + 1), 1)
            total = jnp.zeros((count, lanes), jnp.float32)
            for k in range(RIM):
                total = total + ends[:, k : k + 1] * moved
                moved = pltpu.roll(moved, 1, 1)
            cols = pl.ds(pl.multiple_of(jnp.where(z == 0, 0, quarter - lanes), lanes), lanes)
            touched = (lane < RIM) == (z == 0)
            touched = touched & ((lane < RIM) | (lane >= lanes - RIM))
            target[at, :, cols] = target[at, :, cols] - jnp.where(touched, total, 0.0)


def unpack_kernel(most, slots, out):
    devices = slots.shape[0]
    for b in range(out.shape[0]):
        for d in range(devices):
            out[b, d * most : (d + 1) * most, :] = slots[d, b * most : (b + 1) * most, :]


def f32(*shape):
    return jax.ShapeDtypeStruct(shape, jnp.float32)


def kernel_call(body, out_shape, in_specs, out_specs, scratch, flops=0, moved=0, vmem=None):
    return pl.pallas_call(
        body,
        name=getattr(body, "func", body).__name__,
        out_shape=out_shape,
        in_specs=in_specs,
        out_specs=out_specs,
        scratch_shapes=scratch,
        compiler_params=pltpu.CompilerParams(vmem_limit_bytes=vmem),
        cost_estimate=pl.CostEstimate(flops=flops, bytes_accessed=moved, transcendentals=0),
    )


def plane_device(traces, live_mask, offset_bin, surface, block_owner, point_column, filters):
    shots, receivers, quarter = traces.shape
    devices = lax.axis_size("shot")
    points = STEPS * POINTS_BLK
    rows = shots * receivers
    bins_total = filters.shape[0] * devices
    most = max(2, 3 * rows // (2 * bins_total))
    lanes = surface.shape[2]
    half = receivers // 2
    chunk = receivers // devices
    size = chunk // PARTS
    core = lax.axis_index("shot") % 2
    high, low = (jnp.asarray(x) for x in wave_constant(lax.axis_size("freq")))
    dma = pltpu.SemaphoreType.DMA

    to_sibling = kernel_call(
        sibling_kernel, f32(POINTS_BLK, half, lanes), [ANY], VMEM, [dma], moved=2 << 20, vmem=8 << 20
    )(surface)
    sibling = swap(to_sibling, "shot", devices, 1)

    bands = kernel_call(
        spectra_kernel,
        [f32(shots * points, lanes)] * 4,
        [SMEM, SMEM, VMEM, ANY, ANY],
        [VMEM] * 4,
        [
            pltpu.VMEM((shots * points, quarter), jnp.float32),
            pltpu.VMEM((quarter, 2 * NF), jnp.bfloat16),
            pltpu.VMEM((quarter, 2 * NF), jnp.bfloat16),
            pltpu.VMEM((shots * points, 2 * NF), jnp.float32),
            dma((2,)),
        ],
        moved=1 << 21,
        vmem=16 << 20,
    )(point_column, live_mask, traces, high, low)
    spectra = bands[0]
    for k in range(1, 4):
        spectra = spectra + swap(bands[k], "freq", 4, k)

    pieces = kernel_call(
        pieces_kernel,
        [f32(2, POINTS_BLK, size, lanes)] * (3 * PARTS),
        [VMEM, VMEM],
        [VMEM] * (3 * PARTS),
        [],
        moved=5 << 20,
        vmem=24 << 20,
    )(surface, sibling)
    sent = [swap(piece, "shot", devices, 2 * (1 + k // PARTS)) for k, piece in enumerate(pieces)]

    own_filters = jnp.pad(filters, ((0, 8 - filters.shape[0]), (0, lanes - filters.shape[1])))
    shared = jnp.concatenate([spectra, own_filters], axis=0)
    paired = swap(shared, "shot", devices, 1)
    paired = jnp.where(core == 0, jnp.stack([shared, paired]), jnp.stack([paired, shared]))
    every = [paired] + [swap(paired, "shot", devices, 2 * q) for q in (1, 2, 3)]

    places = kernel_call(
        functools.partial(slots_kernel, most),
        jax.ShapeDtypeStruct((bins_total * most, rows), jnp.bfloat16),
        [VMEM] * 2,
        VMEM,
        [],
        flops=rows * rows * 100,
        moved=1 << 21,
        vmem=24 << 20,
    )(offset_bin.reshape(1, rows), live_mask.reshape(1, rows))

    bins = offset_bin.reshape(shots, receivers)
    bins_here = lax.dynamic_slice_in_dim(bins, core * half, half, axis=1)
    bins_there = lax.dynamic_slice_in_dim(bins, (1 - core) * half, half, axis=1)
    bins_both = jnp.concatenate([bins_here, swap(bins_there, "shot", devices, 1)]).reshape(1, rows)
    waves = jnp.asarray(tap_constant(lax.axis_size("freq"), lanes))
    taps, same_side, cross_side = kernel_call(
        functools.partial(response_kernel, filters.shape[0]),
        [f32(rows, lanes), f32(rows, 4 * lanes), f32(rows, 4 * lanes)],
        [VMEM] * 6,
        [VMEM] * 3,
        [pltpu.VMEM((devices, 8, lanes), jnp.float32)],
        flops=rows * 64 * 4 * 1152,
        moved=1 << 22,
        vmem=24 << 20,
    )(bins_both, waves, *every)

    gathered = []
    for part in range(PARTS):
        outs = kernel_call(
            functools.partial(prediction_kernel, part),
            [f32(2 * shots, size, lanes)] * 4,
            [SMEM, ANY, ANY, ANY, ANY, ANY] + [VMEM] * 4,
            [VMEM] * 4,
            [
                pltpu.VMEM((STEPS, POINTS_BLK, size, lanes), jnp.float32),
                pltpu.VMEM((8, shots * points, lanes), jnp.float32),
                pltpu.VMEM((8, shots * points, lanes), jnp.float32),
                dma((STEPS,)),
            ],
            flops=devices * shots * size * points * lanes * 4,
            moved=1 << 20,
            vmem=16 << 20,
        )(block_owner, surface, sibling, *sent[part::PARTS], *every)
        turned = [outs[0]] + [swap(outs[q], "shot", devices, 2 * q) for q in (1, 2, 3)]
        own = kernel_call(
            arrange_kernel,
            f32(2 * shots, 4, size, lanes),
            [VMEM] * 4,
            VMEM,
            [],
            moved=1 << 19,
            vmem=8 << 20,
        )(*turned)
        right = lax.ppermute(own, "freq", [(0, 1), (1, 2), (2, 3)])
        left = lax.ppermute(own, "freq", [(1, 0), (2, 1), (3, 2)])
        across = swap(own, "freq", 4, 2)
        forward = lax.ppermute(across, "freq", [(2, 3), (1, 0)])
        gathered += [own, right, left, across, forward]

    keep, send = kernel_call(
        inverse_kernel,
        [f32(shots, half, quarter)] * 2,
        [ANY, ANY, VMEM, VMEM, VMEM] + [ANY] * (5 * PARTS),
        [VMEM] * 2,
        [
            pltpu.VMEM((2 * shots, 4, PARTS, size, 4 * lanes), jnp.float32),
            pltpu.VMEM((quarter, 4 * lanes), jnp.bfloat16),
            pltpu.VMEM((quarter, 4 * lanes), jnp.bfloat16),
            pltpu.VMEM((RIM, 4 * lanes), jnp.bfloat16),
            pltpu.VMEM((RIM, 4 * lanes), jnp.bfloat16),
            dma((4 * PARTS,)),
            dma((16,)),
        ],
        flops=6 * rows * 4 * lanes * quarter,
        moved=4 << 20,
        vmem=32 << 20,
    )(high, low, taps, same_side, cross_side, *gathered)
    got = swap(send, "shot", devices, 1)

    packed = kernel_call(
        clean_kernel,
        f32(bins_total * most, quarter),
        [VMEM] * 4,
        VMEM,
        [pltpu.VMEM((rows, quarter), jnp.bfloat16)] * 2,
        flops=4 * rows * bins_total * most * quarter,
        moved=6 << 20,
        vmem=32 << 20,
    )(keep, got, traces, places)

    slots = packed.reshape(devices, filters.shape[0] * most, quarter)
    slots = lax.all_to_all(slots, "shot", split_axis=0, concat_axis=0, tiled=True)
    return kernel_call(
        functools.partial(unpack_kernel, most),
        f32(filters.shape[0], devices * most, quarter),
        [VMEM],
        VMEM,
        [],
        moved=3 << 20,
        vmem=16 << 20,
    )(slots)


def with_halo(cells, sides, width):
    for axis, dim in sides:
        count = lax.axis_size(axis)
        ends = count - 1
        head = lax.slice_in_dim(cells, 0, width, axis=dim)
        tail = lax.slice_in_dim(cells, cells.shape[dim] - width, cells.shape[dim], axis=dim)
        cells = jnp.concatenate(
            [
                lax.ppermute(tail, axis, [(i, (i + 1) % count) for i in range(ends)]),
                cells,
                lax.ppermute(head, axis, [((i + 1) % count, i) for i in range(ends)]),
            ],
            axis=dim,
        )
    return cells


def broadcast(value, axis, source):
    kept = jnp.where(lax.axis_index(axis) == source, value, 0).astype(value.dtype)
    return lax.psum(kept, axis)


def wave_table(time_ids, comp_ids, band_width, period):
    mode_ids = comp_ids // (2 * band_width) * band_width + comp_ids % band_width
    phase_ids = (mode_ids[None, :] + 1) * time_ids[:, None] % period
    angles = phase_ids.astype(jnp.float32) * (2.0 * math.pi / period)
    real_part = comp_ids % (2 * band_width) < band_width
    return jnp.where(real_part[None, :], jnp.cos(angles), -jnp.sin(angles))


def cross_mix(left_side, right_side):
    return jnp.einsum("bsj,jrb->srb", left_side, right_side, precision=FULL_PRECISION)


def shifted_sum(widened, tap_table, out_width):
    half_span = (tap_table.shape[-1] - 1) // 2
    summed = jnp.zeros(widened.shape[:-1] + (out_width,), jnp.float32)
    for tap_index in range(tap_table.shape[-1]):
        offset_start = 2 * half_span - tap_index
        window = lax.slice_in_dim(
            widened, offset_start, offset_start + out_width, axis=widened.ndim - 1
        )
        summed = summed + tap_table[..., tap_index : tap_index + 1] * window
    return summed


def widened_rims(values):
    half_span = (TAPS - 1) // 2
    return with_halo(values, (("freq", 2),), half_span)


def pack_rows(values, slot_ids, total_slots):
    return jnp.zeros((total_slots, values.shape[-1]), jnp.float32).at[slot_ids].set(values)


def any_device(traces, live_mask, offset_bin, surface, block_owner, point_column, filters):
    shots_here, receivers, quarter = traces.shape
    freq_count = lax.axis_size("freq")
    shot_count = lax.axis_size("shot")
    band_width = NF // freq_count
    rows_here = shots_here * receivers
    bins_total = filters.shape[0] * shot_count
    most_slots = max(2, 3 * rows_here // (2 * bins_total))
    total_slots = bins_total * most_slots
    live_rows = live_mask.astype(jnp.float32)[:, :, None]
    live_traces = traces * live_rows
    columns = point_column.reshape(-1)
    picked = jnp.take(live_traces, columns, axis=1).reshape(shots_here * columns.shape[0], quarter)
    freq_index = lax.axis_index("freq")
    time_ids = freq_index * quarter + jnp.arange(quarter)
    band_ids = freq_index * 2 * band_width + jnp.arange(2 * band_width)
    wave_rows = wave_table(
        time_ids, jnp.arange(2 * band_width * lax.axis_size("freq")), band_width, NT
    )
    spectra = lax.psum_scatter(
        lax.dot_general(wave_rows, picked, (((0,), (1,)), ((), ())), precision=FULL_PRECISION),
        "freq",
        scatter_dimension=0,
        tiled=True,
    )
    spectra = spectra.reshape(2 * band_width, shots_here, columns.shape[0])
    real_sum = jnp.zeros((shots_here, receivers, band_width), jnp.float32)
    imag_sum = jnp.zeros((shots_here, receivers, band_width), jnp.float32)
    for step_index in range(STEPS):
        surface_part = broadcast(surface, "shot", block_owner[step_index])
        point_spectra = spectra[:, :, step_index * POINTS_BLK : (step_index + 1) * POINTS_BLK]
        data_real = point_spectra[:band_width]
        data_imag = point_spectra[band_width:]
        surf_real = surface_part[:, :, :band_width]
        surf_imag = surface_part[:, :, band_width:]
        real_sum = real_sum + (cross_mix(data_real, surf_real) - cross_mix(data_imag, surf_imag))
        imag_sum = imag_sum + (cross_mix(data_real, surf_imag) + cross_mix(data_imag, surf_real))
    prediction = jnp.concatenate([real_sum, imag_sum], axis=2).reshape(rows_here, 2 * band_width)
    inverse = wave_table(jnp.arange(NT), band_ids, band_width, NT).T * (2.0 / NT)
    partial_value = jnp.dot(prediction, inverse, precision=FULL_PRECISION)
    multiples = lax.psum_scatter(partial_value, "freq", scatter_dimension=1, tiled=True)
    multiples = multiples.reshape(shots_here, receivers, quarter) * live_rows
    bins_flat = offset_bin.reshape(rows_here)
    order_ids = jnp.arange(rows_here)
    earlier = (bins_flat[:, None] == bins_flat[None, :]) & (order_ids[None, :] < order_ids[:, None])
    rank_ids = jnp.sum(earlier.astype(jnp.int32), axis=1)
    slot_ids = bins_flat * most_slots + rank_ids
    every_filter = lax.all_gather(filters, "shot", axis=0, tiled=True)
    trace_taps = jnp.take(every_filter, bins_flat, axis=0).reshape(
        shots_here, receivers, every_filter.shape[1]
    )
    widened = widened_rims(multiples)
    cleaned = live_traces - shifted_sum(widened, trace_taps, quarter)
    cleaned_slots = pack_rows(cleaned.reshape(rows_here, quarter), slot_ids, total_slots)
    cleaned_slots = cleaned_slots.reshape(bins_total, most_slots, quarter)
    return lax.all_to_all(cleaned_slots, "shot", split_axis=0, concat_axis=1, tiled=True)


def on_device(traces, live_mask, offset_bin, surface, block_owner, point_column, filters):
    devices = lax.axis_size("shot")
    in_plane = devices == 8 and lax.axis_size("freq") == 4
    whole_tiles = traces.shape[1] % (8 * PARTS * devices) == 0 and filters.shape[0] <= 8
    plan = plane_device if in_plane and whole_tiles else any_device
    return plan(traces, live_mask, offset_bin, surface, block_owner, point_column, filters)


def solution(mesh):
    return jax.shard_map(
        on_device,
        mesh=mesh,
        in_specs=(
            P("shot", None, "freq"),
            P("shot", None),
            P("shot", None, None),
            P("shot", None, "freq"),
            P(),
            P(),
            P("shot", None),
        ),
        out_specs=P("shot", None, "freq"),
        check_vma=False,
    )
```

```python
import functools
import math

import jax
import jax.numpy as jnp
import numpy as np
from jax import lax
from jax.experimental import pallas as pl
from jax.experimental.pallas import tpu as pltpu
from jax.sharding import PartitionSpec as P

NT = 1024
NF = 256
TAPS = 31
POINTS_BLK = 16
STEPS = 2
RIM = 16
PARTS = 1

FULL_PRECISION = lax.Precision.HIGHEST
VMEM = pl.BlockSpec(memory_space=pltpu.VMEM)
SMEM = pl.BlockSpec(memory_space=pltpu.SMEM)
ANY = pl.BlockSpec(memory_space=pl.ANY)


def wave_constant(bands):
    width = NF // bands
    comps = np.arange(2 * NF)
    modes = comps // (2 * width) * width + comps % width
    phases = (modes[None, :] + 1) * np.arange(NT)[:, None] % NT
    angles = phases * (2.0 * math.pi / NT)
    table = np.where((comps % (2 * width) < width)[None, :], np.cos(angles), -np.sin(angles))
    table = np.pad(table, ((RIM, RIM), (0, 0))).astype(np.float32)
    high = table.astype(jnp.bfloat16)
    low = (table - high.astype(np.float32)).astype(jnp.bfloat16)
    return high, low


def tap_constant(bands, lanes):
    high, low = wave_constant(bands)
    table = high.astype(np.float32) + low.astype(np.float32)
    shifts = (np.arange(TAPS) - (TAPS - 1) // 2) % NT
    return np.pad(table[RIM + shifts], ((0, lanes - TAPS), (0, 0)))


def end_constants(bands, lanes):
    high, low = wave_constant(bands)
    k, t = np.divmod(np.arange(RIM * RIM), RIM)
    waves = [np.stack([part[NT + k], part[RIM + k]]).reshape(2 * RIM * RIM, -1) for part in (high, low)]
    half_span = (TAPS - 1) // 2
    picks = np.zeros((2, lanes, RIM * RIM), np.float32)
    sums = np.zeros((2, RIM * RIM, lanes), np.float32)
    for side, tap, lane in ((0, t + RIM - k + half_span, t), (1, t - 1 - k, lanes - RIM + t)):
        fits = (tap >= 0) & (tap < TAPS)
        picks[side, tap[fits], np.arange(RIM * RIM)[fits]] = 1
        sums[side, np.arange(RIM * RIM), lane] = 1
    return *waves, picks, sums.reshape(2 * RIM * RIM, lanes).astype(jnp.bfloat16)


def split_two(value):
    high = value.astype(jnp.bfloat16)
    return high, (value - high.astype(jnp.float32)).astype(jnp.bfloat16)


def dot_nn(left, right):
    return lax.dot_general(left, right, (((1,), (0,)), ((), ())), preferred_element_type=jnp.float32)


def dot_nt(left, right):
    return lax.dot_general(left, right, (((1,), (1,)), ((), ())), preferred_element_type=jnp.float32)


def run_all(copies):
    for copy in copies:
        copy.start()
    for copy in copies:
        copy.wait()


def swap(value, axis, count, bit):
    return lax.ppermute(value, axis, [(i, i ^ bit) for i in range(count)])


def spectra_kernel(cols, live, traces, bins, filters, high, low, *rest):
    outs, (picked, tab_high, tab_low, part, sems) = rest[:4], rest[4:]
    shots, _, quarter = traces.shape
    z = lax.axis_index("freq")
    rows = pl.ds(pl.multiple_of(RIM + z * quarter, 16), quarter)
    loads = [
        pltpu.make_async_copy(high.at[rows], tab_high, sems.at[0]),
        pltpu.make_async_copy(low.at[rows], tab_low, sems.at[1]),
    ]
    for load in loads:
        load.start()
    per_block = cols.shape[1]
    points = cols.shape[0] * per_block
    for j in range(points):
        col = cols[j // per_block, j % per_block]
        for s in range(shots):
            row = traces[s, pl.ds(col, 1), :]
            picked[s * points + j : s * points + j + 1, :] = row * live[s, col].astype(jnp.float32)
    for load in loads:
        load.wait()
    left_high, left_low = split_two(picked[...])
    part[...] = (
        dot_nn(left_high, tab_high[...]) + dot_nn(left_low, tab_high[...]) + dot_nn(left_high, tab_low[...])
    )
    lines, lanes = outs[0].shape
    rows = shots * points
    for k, out in enumerate(outs):
        out[:rows] = part[:, pl.ds(pl.multiple_of((z ^ k) * lanes, lanes), lanes)]
        out[rows:] = jnp.zeros((lines - rows, lanes), jnp.float32)
    own = filters.shape[0]
    outs[0][rows : rows + own, : filters.shape[1]] = filters[...]
    half = bins.shape[1] // 2
    other = 1 - lax.axis_index("shot") % 2
    there = bins[:, pl.ds(pl.multiple_of(other * half, half), half)]
    outs[0][rows + own : rows + own + shots, :half] = there.astype(jnp.float32)


def sibling_kernel(surface, out, sem):
    half = out.shape[1]
    core = lax.axis_index("shot") % 2
    copy = pltpu.make_async_copy(surface.at[:, pl.ds(pl.multiple_of((1 - core) * half, 8), half)], out, sem)
    copy.start()
    copy.wait()


def pieces_kernel(step, owners, surface, sibling, *outs):
    d = lax.axis_index("shot")
    chip, core = d // 2, d % 2
    half = sibling.shape[1]
    chunk = outs[0].shape[1]
    first_owner, other_owner = owners[step], owners[1 - step]
    owner_core = jnp.where(first_owner // 2 == chip, first_owner % 2, other_owner % 2)
    for source, base, wanted in ((surface, core * half, owner_core == core), (sibling, 0, owner_core != core)):

        @pl.when(wanted)
        def _(source=source, base=base):
            for k, out in enumerate(outs):
                first = base + (chip ^ (k + 1)) * chunk
                out[...] = source[:, pl.ds(pl.multiple_of(first, 8), chunk), :]


def choose_kernel(extra, owners, surface, sibling, *rest):
    sent, (chosen, sems) = rest[:-2], rest[-2:]
    d = lax.axis_index("shot")
    chip, core = d // 2, d % 2
    half = sibling.shape[1]
    chunk = chosen.shape[2]
    for b in range(STEPS):
        owner = owners[b]
        step, owner_core = (owner // 2) ^ chip, owner % 2

        @pl.when((step == 0) & (owner_core == core))
        def _():
            rows = pl.ds(pl.multiple_of(core * half + chip * chunk, 8), chunk)
            pltpu.make_async_copy(surface.at[:, rows], chosen.at[b], sems.at[b]).start()

        @pl.when((step == 0) & (owner_core != core))
        def _():
            rows = pl.ds(pl.multiple_of(chip * chunk, 8), chunk)
            pltpu.make_async_copy(sibling.at[:, rows], chosen.at[b], sems.at[b]).start()

        for k in range(3):

            @pl.when(step == k + 1)
            def _():
                source = sent[3 + k] if extra and b == 1 else sent[k]
                pltpu.make_async_copy(source, chosen.at[b], sems.at[b]).start()

    for b in range(STEPS):
        pltpu.make_async_copy(sibling.at[:, pl.ds(0, chunk)], chosen.at[b], sems.at[b]).wait()


def prediction_kernel(part, chosen, *rest):
    spectra, outs, (real_side, imag_side) = rest[:2], rest[2:6], rest[6:]
    size = outs[0].shape[1]
    points = STEPS * POINTS_BLK
    rows = real_side.shape[1]
    shots = rows // points
    lanes = chosen.shape[3]
    lane = lax.broadcasted_iota(jnp.int32, (rows, lanes), 1)
    for q in range(4):
        for c in range(2):
            value = spectra[c][q, :rows, :]
            turned = pltpu.roll(value, lanes // 2, 1)
            real_side[2 * q + c] = jnp.where(lane < lanes // 2, value, turned)
            imag_side[2 * q + c] = jnp.where(lane < lanes // 2, turned, -value)
    some = slice(part * size, (part + 1) * size)
    for q in range(4):

        @pl.loop(0, 2)
        def _(rel):
            at = 2 * q + rel
            first_sum = [jnp.zeros((size, lanes), jnp.float32)] * shots
            second_sum = [jnp.zeros((size, lanes), jnp.float32)] * shots
            for j in range(points):
                block = chosen[j // POINTS_BLK, j % POINTS_BLK, some, :]
                for s in range(shots):
                    row = s * points + j
                    first_sum[s] = first_sum[s] + real_side[at, row : row + 1, :] * block
                    second_sum[s] = second_sum[s] + imag_side[at, row : row + 1, :] * block
            for s in range(shots):
                outs[q][rel * shots + s] = first_sum[s] + pltpu.roll(second_sum[s], lanes // 2, 1)


def arrange_kernel(own, first, second, third, out):
    chip = lax.axis_index("shot") // 2
    for q, piece in enumerate((own, first, second, third)):
        out[:, chip ^ q] = piece[...]


def slots_kernel(most, bins, live, places):
    total = bins.shape[1]
    bins_total = places.shape[0] // most
    member = (lax.broadcasted_iota(jnp.int32, (bins_total, total), 0) == bins[...]).astype(jnp.float32)
    before = lax.broadcasted_iota(jnp.int32, (total, total), 0) < lax.broadcasted_iota(jnp.int32, (total, total), 1)
    counts = dot_nn(member.astype(jnp.bfloat16), before.astype(jnp.float32).astype(jnp.bfloat16))
    rank = jnp.sum(counts * member, axis=0, keepdims=True)
    slot = bins[...] * most + rank.astype(jnp.int32)
    slot = jnp.where(live[...] != 0, slot, -1)
    at = lax.broadcasted_iota(jnp.int32, places.shape, 0)
    places[...] = (at == slot).astype(jnp.float32).astype(jnp.bfloat16)


def response_kernel(own_bins, bins, waves, picks, *rest):
    spectra, (taps, same_side, cross_side, filters) = rest[:2], rest[2:]
    d = lax.axis_index("shot")
    z = lax.axis_index("freq")
    lines = spectra[0].shape[1]
    for q in range(4):
        for c in range(2):
            filters[d ^ (2 * q + c)] = spectra[c][q, lines - 8 :, :]
    devices, padded, lanes = filters.shape
    shots, receivers = bins.shape
    half = receivers // 2
    here = bins[:, pl.ds(pl.multiple_of(d % 2 * half, half), half)]
    first = lines - 8 + own_bins
    there = spectra[1][0, first : first + shots, :half].astype(jnp.int32)
    lists = [some[s : s + 1] for some in (here, there) for s in range(shots)]
    bin_row = jnp.concatenate(lists, axis=1)
    shape = (devices * padded, shots * receivers)
    row = lax.broadcasted_iota(jnp.int32, shape, 0)
    bin_of_row = jnp.where(row % padded < own_bins, row // padded * own_bins + row % padded, -1)
    member = (bin_of_row == bin_row).astype(jnp.float32).astype(jnp.bfloat16)

    def per_trace(table):
        high, low = split_two(table)
        dims = (((0,), (0,)), ((), ()))
        return lax.dot_general(member, high, dims, preferred_element_type=jnp.float32) + lax.dot_general(
            member, low, dims, preferred_element_type=jnp.float32
        )

    table = filters[...].reshape(devices * padded, lanes)
    side = picks[(z + 1) // 4]
    taps[...] = per_trace(jnp.dot(table, side, precision=FULL_PRECISION, preferred_element_type=jnp.float32))
    lane = lax.broadcasted_iota(jnp.int32, (devices * padded, lanes), 1)
    for slot, step in enumerate((0, 3, 1, 2)):
        cols = pl.ds(pl.multiple_of((z + step) % 4 * lanes, lanes), lanes)
        answer = jnp.dot(table, waves[:, cols], precision=FULL_PRECISION, preferred_element_type=jnp.float32)
        turned = pltpu.roll(answer, lanes // 2, 1)
        into = slice(slot * lanes, (slot + 1) * lanes)
        same_side[:, into] = per_trace(jnp.where(lane < lanes // 2, answer, turned))
        cross_side[:, into] = per_trace(jnp.where(lane < lanes // 2, -turned, answer))


def clean_kernel(keep, got, traces, places, *rest):
    outs, (high, low, packed) = rest[:-3], rest[-3:]
    d = lax.axis_index("shot")
    core = d % 2
    shots, receivers, _ = traces.shape
    half = keep.shape[1]
    for source, side in ((keep, core), (got, 1 - core)):
        for s in range(shots):
            first = pl.multiple_of(side * half, half)
            flat = pl.ds(pl.multiple_of(s * receivers + first, half), half)
            clean_high, clean_low = split_two(traces[s, pl.ds(first, half), :] - source[s])
            high[flat, :] = clean_high
            low[flat, :] = clean_low
    packed[...] = dot_nn(places[...], high[...]) + dot_nn(places[...], low[...])
    count = outs[0].shape[0]
    for k, out in enumerate(outs):
        out[...] = packed[pl.ds(pl.multiple_of((d ^ k) * count, 8), count), :]


def inverse_kernel(high, low, end_high, end_low, sums, taps, same_side, cross_side, *rest):
    bands = [rest[5 * p : 5 * p + 5] for p in range(PARTS)]
    keep, send = rest[5 * PARTS : 5 * PARTS + 2]
    gathered, tab_high, tab_low, tab_end_high, tab_end_low, end_sums, sems, tab_sems = rest[5 * PARTS + 2 :]
    z = lax.axis_index("freq")
    lanes = bands[0][0].shape[3]
    quarter = tab_high.shape[0]
    at_end = (z == 0) | (z == 3)
    rows = pl.ds(pl.multiple_of(RIM + z * quarter, 16), quarter)
    end_size = RIM * RIM
    end_rows = pl.ds(pl.multiple_of((z + 1) // 4 * end_size, 16), end_size)
    loads = []
    end_loads = [pltpu.make_async_copy(sums.at[end_rows], end_sums, tab_sems.at[16])]
    for slot, step in enumerate((0, 3, 1, 2)):
        cols = pl.ds(pl.multiple_of((z + step) % 4 * lanes, lanes), lanes)
        into = pl.ds(slot * lanes, lanes)
        for i, (table, scratch) in enumerate(((high, tab_high), (low, tab_low))):
            loads.append(pltpu.make_async_copy(table.at[rows, cols], scratch.at[:, into], tab_sems.at[4 * slot + i]))
        for i, (table, scratch) in enumerate(((end_high, tab_end_high), (end_low, tab_end_low))):
            copy = pltpu.make_async_copy(table.at[end_rows, cols], scratch.at[:, into], tab_sems.at[4 * slot + 2 + i])
            end_loads.append(copy)
    for load in loads:
        load.start()

    @pl.when(at_end)
    def _():
        for load in end_loads:
            load.start()

    def fetch(source, p, slot):
        into = gathered.at[:, :, p, :, pl.ds(slot * lanes, lanes)]
        return pltpu.make_async_copy(source, into, sems.at[4 * p + slot])

    for p in range(PARTS):
        own, right, left, across, forward = bands[p]
        fetch(own, p, 0).start()
        fetch(across, p, 3).start()

        @pl.when(z > 0)
        def _():
            fetch(right, p, 1).start()

        @pl.when(z == 0)
        def _():
            fetch(forward, p, 1).start()

        @pl.when(z < 3)
        def _():
            fetch(left, p, 2).start()

        @pl.when(z == 3)
        def _():
            fetch(forward, p, 2).start()

    for load in loads:
        load.wait()
    for p in range(PARTS):
        for slot in range(4):
            fetch(bands[p][0], p, slot).wait()
    shots, count, _ = keep.shape
    total = 2 * shots * count
    value = gathered[...].reshape(total, 4 * lanes)
    rolled = [pltpu.roll(value[:, i * lanes : (i + 1) * lanes], lanes // 2, 1) for i in range(4)]
    answer = value * same_side[...] + jnp.concatenate(rolled, axis=1) * cross_side[...]

    def transform(value, into_high, into_low):
        left_high, left_low = split_two(value)
        full = dot_nt(left_high, into_high[...]) + dot_nt(left_low, into_high[...]) + dot_nt(left_high, into_low[...])
        return full * (2.0 / NT)

    result = transform(answer, tab_high, tab_low).reshape(2 * shots, count, quarter)
    keep[...] = result[:shots]
    send[...] = result[shots:]

    @pl.when(at_end)
    def _():
        for load in end_loads:
            load.wait()
        beyond = transform(gathered[...].reshape(total, 4 * lanes), tab_end_high, tab_end_low) * taps[...]
        beyond_high, beyond_low = split_two(beyond)
        wrapped = dot_nn(beyond_high, end_sums[...]) + dot_nn(beyond_low, end_sums[...])
        wrapped = wrapped.reshape(2 * shots, count, lanes)
        cols = pl.ds(pl.multiple_of(jnp.where(z == 0, 0, quarter - lanes), lanes), lanes)
        keep[:, :, cols] = keep[:, :, cols] - wrapped[:shots]
        send[:, :, cols] = send[:, :, cols] - wrapped[shots:]


def unpack_kernel(most, *rest):
    slots, out = rest[:-1], rest[-1]
    d = lax.axis_index("shot")
    chip, core = d // 2, d % 2
    for q in range(len(slots) // 2):
        own, other = slots[2 * q][...], slots[2 * q + 1][...]
        first, second = jnp.where(core == 0, own, other), jnp.where(core == 0, other, own)
        rows = pl.ds(pl.multiple_of((chip ^ q) * (2 * most), 8), 2 * most)
        for b in range(out.shape[0]):
            some = slice(b * most, (b + 1) * most)
            out[b, rows, :] = jnp.concatenate([first[some], second[some]], axis=0)


def f32(*shape):
    return jax.ShapeDtypeStruct(shape, jnp.float32)


def kernel_call(body, out_shape, in_specs, out_specs, scratch, flops=0, moved=0, vmem=None):
    return pl.pallas_call(
        body,
        name=getattr(body, "func", body).__name__,
        out_shape=out_shape,
        in_specs=in_specs,
        out_specs=out_specs,
        scratch_shapes=scratch,
        compiler_params=pltpu.CompilerParams(vmem_limit_bytes=vmem),
        cost_estimate=pl.CostEstimate(flops=flops, bytes_accessed=moved, transcendentals=0),
    )


def plane_device(traces, live_mask, offset_bin, surface, block_owner, point_column, filters):
    shots, receivers, quarter = traces.shape
    devices = lax.axis_size("shot")
    points = STEPS * POINTS_BLK
    rows = shots * receivers
    bins_total = filters.shape[0] * devices
    most = max(2, 3 * rows // (2 * bins_total))
    lanes = surface.shape[2]
    half = receivers // 2
    chunk = receivers // devices
    size = chunk // PARTS
    core = lax.axis_index("shot") & 1
    high, low = (jnp.asarray(x) for x in wave_constant(lax.axis_size("freq")))
    dma = pltpu.SemaphoreType.DMA

    to_sibling = kernel_call(
        sibling_kernel, f32(POINTS_BLK, half, lanes), [ANY], VMEM, [dma], moved=2 << 20, vmem=8 << 20
    )(surface)
    sibling = swap(to_sibling, "shot", devices, 1)

    bins = offset_bin.reshape(shots, receivers)
    bands = kernel_call(
        spectra_kernel,
        [f32(shots * points + 8, lanes)] * 4,
        [SMEM, SMEM, VMEM, VMEM, VMEM, ANY, ANY],
        [VMEM] * 4,
        [
            pltpu.VMEM((shots * points, quarter), jnp.float32),
            pltpu.VMEM((quarter, 2 * NF), jnp.bfloat16),
            pltpu.VMEM((quarter, 2 * NF), jnp.bfloat16),
            pltpu.VMEM((shots * points, 2 * NF), jnp.float32),
            dma((2,)),
        ],
        moved=1 << 21,
        vmem=16 << 20,
    )(point_column, live_mask, traces, bins, filters, high, low)
    def scatter(step):
        pieces = kernel_call(
            functools.partial(pieces_kernel, step),
            [f32(POINTS_BLK, chunk, lanes)] * 3,
            [SMEM, VMEM, VMEM],
            [VMEM] * 3,
            [],
            moved=4 << 20,
            vmem=24 << 20,
        )(block_owner, surface, sibling)
        return [swap(piece, "shot", devices, 2 * (k + 1)) for k, piece in enumerate(pieces)]

    def choose(*sent):
        return kernel_call(
            functools.partial(choose_kernel, len(sent) > 3),
            f32(STEPS, POINTS_BLK, chunk, lanes),
            [SMEM] + [ANY] * (2 + len(sent)),
            VMEM,
            [dma((STEPS,))],
            moved=1 << 20,
            vmem=8 << 20,
        )(block_owner, surface, sibling, *sent)

    sent = scatter(0)

    spectra = bands[0]
    for k in range(1, 4):
        spectra = spectra + swap(bands[k], "freq", 4, k)
    every = jnp.stack([spectra] + [swap(spectra, "shot", devices, 2 * q) for q in (1, 2, 3)])
    every = [every, swap(every, "shot", devices, 1)]

    places = kernel_call(
        functools.partial(slots_kernel, most),
        jax.ShapeDtypeStruct((bins_total * most, rows), jnp.bfloat16),
        [VMEM] * 2,
        VMEM,
        [],
        flops=rows * rows * 100,
        moved=1 << 21,
        vmem=24 << 20,
    )(offset_bin.reshape(1, rows), live_mask.reshape(1, rows))

    waves = jnp.asarray(tap_constant(lax.axis_size("freq"), lanes))
    end_high, end_low, picks, sums = (jnp.asarray(x) for x in end_constants(lax.axis_size("freq"), lanes))
    taps, same_side, cross_side = kernel_call(
        functools.partial(response_kernel, filters.shape[0]),
        [f32(rows, RIM * RIM), f32(rows, 4 * lanes), f32(rows, 4 * lanes)],
        [VMEM] * 5,
        [VMEM] * 3,
        [pltpu.VMEM((devices, 8, lanes), jnp.float32)],
        flops=rows * 64 * 4 * 1152,
        moved=1 << 22,
        vmem=24 << 20,
    )(bins, waves, picks, *every)

    both = (block_owner[0] ^ block_owner[1]) == 1
    sent, every = lax.optimization_barrier((sent, every))
    chosen = lax.cond(both, lambda *sent: choose(*sent, *scatter(1)), choose, *sent)

    gathered = []
    for part in range(PARTS):
        outs = kernel_call(
            functools.partial(prediction_kernel, part),
            [f32(2 * shots, size, lanes)] * 4,
            [VMEM] * 3,
            [VMEM] * 4,
            [pltpu.VMEM((8, shots * points, lanes), jnp.float32)] * 2,
            flops=devices * shots * size * points * lanes * 4,
            moved=1 << 20,
            vmem=16 << 20,
        )(chosen, *every)
        if gathered:
            outs, gathered[0] = lax.optimization_barrier((outs, gathered[0]))
        turned = [outs[0]] + [swap(outs[q], "shot", devices, 2 * q) for q in (1, 2, 3)]
        own = kernel_call(
            arrange_kernel,
            f32(2 * shots, 4, size, lanes),
            [VMEM] * 4,
            VMEM,
            [],
            moved=1 << 19,
            vmem=8 << 20,
        )(*turned)
        right = lax.ppermute(own, "freq", [(0, 1), (1, 2), (2, 3)])
        left = lax.ppermute(own, "freq", [(1, 0), (2, 1), (3, 2)])
        across = swap(own, "freq", 4, 2)
        forward = lax.ppermute(across, "freq", [(2, 3), (1, 0)])
        gathered += [own, right, left, across, forward]

    keep, send = kernel_call(
        inverse_kernel,
        [f32(shots, half, quarter)] * 2,
        [ANY] * 5 + [VMEM] * 3 + [ANY] * (5 * PARTS),
        [VMEM] * 2,
        [
            pltpu.VMEM((2 * shots, 4, PARTS, size, 4 * lanes), jnp.float32),
            pltpu.VMEM((quarter, 4 * lanes), jnp.bfloat16),
            pltpu.VMEM((quarter, 4 * lanes), jnp.bfloat16),
            pltpu.VMEM((RIM * RIM, 4 * lanes), jnp.bfloat16),
            pltpu.VMEM((RIM * RIM, 4 * lanes), jnp.bfloat16),
            pltpu.VMEM((RIM * RIM, lanes), jnp.bfloat16),
            dma((4 * PARTS,)),
            dma((17,)),
        ],
        flops=6 * rows * 4 * lanes * quarter,
        moved=4 << 20,
        vmem=32 << 20,
    )(high, low, end_high, end_low, sums, taps, same_side, cross_side, *gathered)
    got = swap(send, "shot", devices, 1)

    bin_slots = filters.shape[0] * most
    slots = kernel_call(
        clean_kernel,
        [f32(bin_slots, quarter)] * devices,
        [VMEM] * 4,
        [VMEM] * devices,
        [pltpu.VMEM((rows, quarter), jnp.bfloat16)] * 2 + [pltpu.VMEM((devices * bin_slots, quarter), jnp.float32)],
        flops=4 * rows * bins_total * most * quarter,
        moved=6 << 20,
        vmem=32 << 20,
    )(keep, got, traces, places)
    slots = [slots[0]] + [swap(slots[k], "shot", devices, k) for k in range(1, devices)]
    return kernel_call(
        functools.partial(unpack_kernel, most),
        f32(filters.shape[0], devices * most, quarter),
        [VMEM] * devices,
        VMEM,
        [],
        moved=3 << 20,
        vmem=16 << 20,
    )(*slots)


def with_halo(cells, sides, width):
    for axis, dim in sides:
        count = lax.axis_size(axis)
        ends = count - 1
        head = lax.slice_in_dim(cells, 0, width, axis=dim)
        tail = lax.slice_in_dim(cells, cells.shape[dim] - width, cells.shape[dim], axis=dim)
        cells = jnp.concatenate(
            [
                lax.ppermute(tail, axis, [(i, (i + 1) % count) for i in range(ends)]),
                cells,
                lax.ppermute(head, axis, [((i + 1) % count, i) for i in range(ends)]),
            ],
            axis=dim,
        )
    return cells


def broadcast(value, axis, source):
    kept = jnp.where(lax.axis_index(axis) == source, value, 0).astype(value.dtype)
    return lax.psum(kept, axis)


def wave_table(time_ids, comp_ids, band_width, period):
    mode_ids = comp_ids // (2 * band_width) * band_width + comp_ids % band_width
    phase_ids = (mode_ids[None, :] + 1) * time_ids[:, None] % period
    angles = phase_ids.astype(jnp.float32) * (2.0 * math.pi / period)
    real_part = comp_ids % (2 * band_width) < band_width
    return jnp.where(real_part[None, :], jnp.cos(angles), -jnp.sin(angles))


def cross_mix(left_side, right_side):
    return jnp.einsum("bsj,jrb->srb", left_side, right_side, precision=FULL_PRECISION)


def shifted_sum(widened, tap_table, out_width):
    half_span = (tap_table.shape[-1] - 1) // 2
    summed = jnp.zeros(widened.shape[:-1] + (out_width,), jnp.float32)
    for tap_index in range(tap_table.shape[-1]):
        offset_start = 2 * half_span - tap_index
        window = lax.slice_in_dim(
            widened, offset_start, offset_start + out_width, axis=widened.ndim - 1
        )
        summed = summed + tap_table[..., tap_index : tap_index + 1] * window
    return summed


def widened_rims(values):
    half_span = (TAPS - 1) // 2
    return with_halo(values, (("freq", 2),), half_span)


def pack_rows(values, slot_ids, total_slots):
    return jnp.zeros((total_slots, values.shape[-1]), jnp.float32).at[slot_ids].set(values)


def any_device(traces, live_mask, offset_bin, surface, block_owner, point_column, filters):
    shots_here, receivers, quarter = traces.shape
    freq_count = lax.axis_size("freq")
    shot_count = lax.axis_size("shot")
    band_width = NF // freq_count
    rows_here = shots_here * receivers
    bins_total = filters.shape[0] * shot_count
    most_slots = max(2, 3 * rows_here // (2 * bins_total))
    total_slots = bins_total * most_slots
    live_rows = live_mask.astype(jnp.float32)[:, :, None]
    live_traces = traces * live_rows
    columns = point_column.reshape(-1)
    picked = jnp.take(live_traces, columns, axis=1).reshape(shots_here * columns.shape[0], quarter)
    freq_index = lax.axis_index("freq")
    time_ids = freq_index * quarter + jnp.arange(quarter)
    band_ids = freq_index * 2 * band_width + jnp.arange(2 * band_width)
    wave_rows = wave_table(
        time_ids, jnp.arange(2 * band_width * lax.axis_size("freq")), band_width, NT
    )
    spectra = lax.psum_scatter(
        lax.dot_general(wave_rows, picked, (((0,), (1,)), ((), ())), precision=FULL_PRECISION),
        "freq",
        scatter_dimension=0,
        tiled=True,
    )
    spectra = spectra.reshape(2 * band_width, shots_here, columns.shape[0])
    real_sum = jnp.zeros((shots_here, receivers, band_width), jnp.float32)
    imag_sum = jnp.zeros((shots_here, receivers, band_width), jnp.float32)
    for step_index in range(STEPS):
        surface_part = broadcast(surface, "shot", block_owner[step_index])
        point_spectra = spectra[:, :, step_index * POINTS_BLK : (step_index + 1) * POINTS_BLK]
        data_real = point_spectra[:band_width]
        data_imag = point_spectra[band_width:]
        surf_real = surface_part[:, :, :band_width]
        surf_imag = surface_part[:, :, band_width:]
        real_sum = real_sum + (cross_mix(data_real, surf_real) - cross_mix(data_imag, surf_imag))
        imag_sum = imag_sum + (cross_mix(data_real, surf_imag) + cross_mix(data_imag, surf_real))
    prediction = jnp.concatenate([real_sum, imag_sum], axis=2).reshape(rows_here, 2 * band_width)
    inverse = wave_table(jnp.arange(NT), band_ids, band_width, NT).T * (2.0 / NT)
    partial_value = jnp.dot(prediction, inverse, precision=FULL_PRECISION)
    multiples = lax.psum_scatter(partial_value, "freq", scatter_dimension=1, tiled=True)
    multiples = multiples.reshape(shots_here, receivers, quarter) * live_rows
    bins_flat = offset_bin.reshape(rows_here)
    order_ids = jnp.arange(rows_here)
    earlier = (bins_flat[:, None] == bins_flat[None, :]) & (order_ids[None, :] < order_ids[:, None])
    rank_ids = jnp.sum(earlier.astype(jnp.int32), axis=1)
    slot_ids = bins_flat * most_slots + rank_ids
    every_filter = lax.all_gather(filters, "shot", axis=0, tiled=True)
    trace_taps = jnp.take(every_filter, bins_flat, axis=0).reshape(
        shots_here, receivers, every_filter.shape[1]
    )
    widened = widened_rims(multiples)
    cleaned = live_traces - shifted_sum(widened, trace_taps, quarter)
    cleaned_slots = pack_rows(cleaned.reshape(rows_here, quarter), slot_ids, total_slots)
    cleaned_slots = cleaned_slots.reshape(bins_total, most_slots, quarter)
    return lax.all_to_all(cleaned_slots, "shot", split_axis=0, concat_axis=1, tiled=True)


def on_device(traces, live_mask, offset_bin, surface, block_owner, point_column, filters):
    devices = lax.axis_size("shot")
    in_plane = devices == 8 and lax.axis_size("freq") == 4
    whole_tiles = traces.shape[1] % (8 * PARTS * devices) == 0 and filters.shape[0] <= 8
    plan = plane_device if in_plane and whole_tiles else any_device
    return plan(traces, live_mask, offset_bin, surface, block_owner, point_column, filters)


def solution(mesh):
    return jax.shard_map(
        on_device,
        mesh=mesh,
        in_specs=(
            P("shot", None, "freq"),
            P("shot", None),
            P("shot", None, None),
            P("shot", None, "freq"),
            P(),
            P(),
            P("shot", None),
        ),
        out_specs=P("shot", None, "freq"),
        check_vma=False,
    )
```

```python
import functools
import math

import jax
import jax.numpy as jnp
import numpy as np
from jax import lax
from jax.experimental import pallas as pl
from jax.experimental.pallas import tpu as pltpu
from jax.sharding import PartitionSpec as P

NT = 1024
NF = 256
TAPS = 31
POINTS_BLK = 16
STEPS = 2
RIM = 16

FULL_PRECISION = lax.Precision.HIGHEST
VMEM = pl.BlockSpec(memory_space=pltpu.VMEM)
SMEM = pl.BlockSpec(memory_space=pltpu.SMEM)
ANY = pl.BlockSpec(memory_space=pl.ANY)


def wave_constant(bands):
    width = NF // bands
    comps = np.arange(2 * NF)
    modes = comps // (2 * width) * width + comps % width
    phases = (modes[None, :] + 1) * np.arange(NT)[:, None] % NT
    angles = phases * (2.0 * math.pi / NT)
    table = np.where((comps % (2 * width) < width)[None, :], np.cos(angles), -np.sin(angles))
    table = np.pad(table, ((RIM, RIM), (0, 0))).astype(np.float32)
    high = table.astype(jnp.bfloat16)
    low = (table - high.astype(np.float32)).astype(jnp.bfloat16)
    return high, low


def tap_constant(bands, lanes):
    high, low = wave_constant(bands)
    table = high.astype(np.float32) + low.astype(np.float32)
    shifts = (np.arange(TAPS) - (TAPS - 1) // 2) % NT
    return np.pad(table[RIM + shifts], ((0, lanes - TAPS), (0, 0)))


def end_constants(bands, lanes):
    high, low = wave_constant(bands)
    k, t = np.divmod(np.arange(RIM * RIM), RIM)
    waves = [np.stack([part[NT + k], part[RIM + k]]).reshape(2 * RIM * RIM, -1) for part in (high, low)]
    half_span = (TAPS - 1) // 2
    picks = np.zeros((2, lanes, RIM * RIM), np.float32)
    sums = np.zeros((2, RIM * RIM, lanes), np.float32)
    for side, tap, lane in ((0, t + RIM - k + half_span, t), (1, t - 1 - k, lanes - RIM + t)):
        fits = (tap >= 0) & (tap < TAPS)
        picks[side, tap[fits], np.arange(RIM * RIM)[fits]] = 1
        sums[side, np.arange(RIM * RIM), lane] = 1
    return *waves, picks, sums.reshape(2 * RIM * RIM, lanes).astype(jnp.bfloat16)


def split_two(value):
    high = value.astype(jnp.bfloat16)
    return high, (value - high.astype(jnp.float32)).astype(jnp.bfloat16)


def dot_nn(left, right):
    return lax.dot_general(left, right, (((1,), (0,)), ((), ())), preferred_element_type=jnp.float32)


def dot_nt(left, right):
    return lax.dot_general(left, right, (((1,), (1,)), ((), ())), preferred_element_type=jnp.float32)


def run_all(copies):
    for copy in copies:
        copy.start()
    for copy in copies:
        copy.wait()


def swap(value, axis, count, bit):
    return lax.ppermute(value, axis, [(i, i ^ bit) for i in range(count)])


def spectra_kernel(cols, live, traces, bins, filters, high, low, *rest):
    outs, (picked, tab_high, tab_low, part, sems) = rest[:4], rest[4:]
    shots, _, quarter = traces.shape
    z = lax.axis_index("freq")
    rows = pl.ds(pl.multiple_of(RIM + z * quarter, 16), quarter)
    loads = [
        pltpu.make_async_copy(high.at[rows], tab_high, sems.at[0]),
        pltpu.make_async_copy(low.at[rows], tab_low, sems.at[1]),
    ]
    for load in loads:
        load.start()
    per_block = cols.shape[1]
    points = cols.shape[0] * per_block
    for j in range(points):
        col = cols[j // per_block, j % per_block]
        for s in range(shots):
            row = traces[s, pl.ds(col, 1), :]
            picked[s * points + j : s * points + j + 1, :] = row * live[s, col].astype(jnp.float32)
    for load in loads:
        load.wait()
    left_high, left_low = split_two(picked[...])
    part[...] = (
        dot_nn(left_high, tab_high[...]) + dot_nn(left_low, tab_high[...]) + dot_nn(left_high, tab_low[...])
    )
    lines, lanes = outs[0].shape
    rows = shots * points
    for k, out in enumerate(outs):
        out[:rows] = part[:, pl.ds(pl.multiple_of((z ^ k) * lanes, lanes), lanes)]
        out[rows:] = jnp.zeros((lines - rows, lanes), jnp.float32)
    own = filters.shape[0]
    outs[0][rows : rows + own, : filters.shape[1]] = filters[...]
    half = bins.shape[1] // 2
    other = 1 - lax.axis_index("shot") % 2
    there = bins[:, pl.ds(pl.multiple_of(other * half, half), half)]
    outs[0][rows + own : rows + own + shots, :half] = there.astype(jnp.float32)


def sibling_kernel(surface, out, sem):
    half = out.shape[1]
    core = lax.axis_index("shot") % 2
    copy = pltpu.make_async_copy(surface.at[:, pl.ds(pl.multiple_of((1 - core) * half, 8), half)], out, sem)
    copy.start()
    copy.wait()


def pieces_kernel(step, owners, surface, sibling, *outs):
    d = lax.axis_index("shot")
    chip, core = d // 2, d % 2
    half = sibling.shape[1]
    chunk = outs[0].shape[1]
    first_owner, other_owner = owners[step], owners[1 - step]
    owner_core = jnp.where(first_owner // 2 == chip, first_owner % 2, other_owner % 2)
    for source, base, wanted in ((surface, core * half, owner_core == core), (sibling, 0, owner_core != core)):

        @pl.when(wanted)
        def _(source=source, base=base):
            for k, out in enumerate(outs):
                first = base + (chip ^ (k + 1)) * chunk
                out[...] = source[:, pl.ds(pl.multiple_of(first, 8), chunk), :]


def predict(chosen, spectra, real_side, imag_side, outs):
    points = STEPS * POINTS_BLK
    rows = real_side.shape[1]
    shots = rows // points
    size, lanes = chosen.shape[2:]
    lane = lax.broadcasted_iota(jnp.int32, (rows, lanes), 1)
    for q in outs:
        for c in range(2):
            value = spectra[c][q, :rows, :]
            turned = pltpu.roll(value, lanes // 2, 1)
            real_side[2 * q + c] = jnp.where(lane < lanes // 2, value, turned)
            imag_side[2 * q + c] = jnp.where(lane < lanes // 2, turned, -value)
    yield
    for q, out in outs.items():

        @pl.loop(0, 2)
        def _(rel, q=q, out=out):
            at = 2 * q + rel
            first_sum = [jnp.zeros((size, lanes), jnp.float32)] * shots
            second_sum = [jnp.zeros((size, lanes), jnp.float32)] * shots
            for j in range(points):
                block = chosen[j // POINTS_BLK, j % POINTS_BLK]
                for s in range(shots):
                    row = s * points + j
                    first_sum[s] = first_sum[s] + real_side[at, row : row + 1, :] * block
                    second_sum[s] = second_sum[s] + imag_side[at, row : row + 1, :] * block
            for s in range(shots):
                out[rel * shots + s] = first_sum[s] + pltpu.roll(second_sum[s], lanes // 2, 1)


def others_kernel(extra, owners, surface, sibling, *rest):
    sent, spectra, outs, (chosen, real_side, imag_side, sems) = rest[:-9], rest[-9:-7], rest[-7:-4], rest[-4:]
    d = lax.axis_index("shot")
    chip, core = d // 2, d % 2
    half = sibling.shape[1]
    chunk = chosen.shape[2]
    for b in range(STEPS):
        owner = owners[b]
        step, owner_core = (owner // 2) ^ chip, owner % 2

        @pl.when((step == 0) & (owner_core == core))
        def _():
            rows = pl.ds(pl.multiple_of(core * half + chip * chunk, 8), chunk)
            pltpu.make_async_copy(surface.at[:, rows], chosen.at[b], sems.at[b]).start()

        @pl.when((step == 0) & (owner_core != core))
        def _():
            rows = pl.ds(pl.multiple_of(chip * chunk, 8), chunk)
            pltpu.make_async_copy(sibling.at[:, rows], chosen.at[b], sems.at[b]).start()

        for k in range(3):

            @pl.when(step == k + 1)
            def _():
                source = sent[3 + k] if extra and b == 1 else sent[k]
                pltpu.make_async_copy(source, chosen.at[b], sems.at[b]).start()

    steps = predict(chosen, spectra, real_side, imag_side, dict(zip((1, 2, 3), outs)))
    next(steps)
    for b in range(STEPS):
        pltpu.make_async_copy(sibling.at[:, pl.ds(0, chunk)], chosen.at[b], sems.at[b]).wait()
    for _ in steps:
        pass


def own_kernel(chosen, own, other, out, real_side, imag_side):
    for _ in predict(chosen, (own, other), real_side, imag_side, {0: out}):
        pass


def arrange_kernel(own, first, second, third, out):
    chip = lax.axis_index("shot") // 2
    for q, piece in enumerate((own, first, second, third)):
        out[:, chip ^ q] = piece[...]


def slots_kernel(most, bins, live, places):
    total = bins.shape[1]
    bins_total = places.shape[0] // most
    member = (lax.broadcasted_iota(jnp.int32, (bins_total, total), 0) == bins[...]).astype(jnp.float32)
    before = lax.broadcasted_iota(jnp.int32, (total, total), 0) < lax.broadcasted_iota(jnp.int32, (total, total), 1)
    counts = dot_nn(member.astype(jnp.bfloat16), before.astype(jnp.float32).astype(jnp.bfloat16))
    rank = jnp.sum(counts * member, axis=0, keepdims=True)
    slot = bins[...] * most + rank.astype(jnp.int32)
    slot = jnp.where(live[...] != 0, slot, -1)
    at = lax.broadcasted_iota(jnp.int32, places.shape, 0)
    places[...] = (at == slot).astype(jnp.float32).astype(jnp.bfloat16)


def response_kernel(own_bins, bins, waves, picks, *rest):
    spectra, (taps, same_side, cross_side, filters) = rest[:2], rest[2:]
    d = lax.axis_index("shot")
    z = lax.axis_index("freq")
    lines = spectra[0].shape[1]
    for q in range(4):
        for c in range(2):
            filters[d ^ (2 * q + c)] = spectra[c][q, lines - 8 :, :]
    devices, padded, lanes = filters.shape
    shots, receivers = bins.shape
    half = receivers // 2
    here = bins[:, pl.ds(pl.multiple_of(d % 2 * half, half), half)]
    first = lines - 8 + own_bins
    there = spectra[1][0, first : first + shots, :half].astype(jnp.int32)
    lists = [some[s : s + 1] for some in (here, there) for s in range(shots)]
    bin_row = jnp.concatenate(lists, axis=1)
    shape = (devices * padded, shots * receivers)
    row = lax.broadcasted_iota(jnp.int32, shape, 0)
    bin_of_row = jnp.where(row % padded < own_bins, row // padded * own_bins + row % padded, -1)
    member = (bin_of_row == bin_row).astype(jnp.float32).astype(jnp.bfloat16)

    def per_trace(table):
        high, low = split_two(table)
        dims = (((0,), (0,)), ((), ()))
        return lax.dot_general(member, high, dims, preferred_element_type=jnp.float32) + lax.dot_general(
            member, low, dims, preferred_element_type=jnp.float32
        )

    table = filters[...].reshape(devices * padded, lanes)
    side = picks[(z + 1) // 4]
    taps[...] = per_trace(jnp.dot(table, side, precision=FULL_PRECISION, preferred_element_type=jnp.float32))
    lane = lax.broadcasted_iota(jnp.int32, (devices * padded, lanes), 1)
    for slot, step in enumerate((0, 3, 1, 2)):
        cols = pl.ds(pl.multiple_of((z + step) % 4 * lanes, lanes), lanes)
        answer = jnp.dot(table, waves[:, cols], precision=FULL_PRECISION, preferred_element_type=jnp.float32)
        turned = pltpu.roll(answer, lanes // 2, 1)
        into = slice(slot * lanes, (slot + 1) * lanes)
        same_side[:, into] = per_trace(jnp.where(lane < lanes // 2, answer, turned))
        cross_side[:, into] = per_trace(jnp.where(lane < lanes // 2, -turned, answer))


def clean_kernel(keep, got, traces, places, *rest):
    outs, (high, low, packed) = rest[:-3], rest[-3:]
    d = lax.axis_index("shot")
    core = d % 2
    shots, receivers, _ = traces.shape
    half = keep.shape[1]
    for source, side in ((keep, core), (got, 1 - core)):
        for s in range(shots):
            first = pl.multiple_of(side * half, half)
            flat = pl.ds(pl.multiple_of(s * receivers + first, half), half)
            clean_high, clean_low = split_two(traces[s, pl.ds(first, half), :] - source[s])
            high[flat, :] = clean_high
            low[flat, :] = clean_low
    packed[...] = dot_nn(places[...], high[...]) + dot_nn(places[...], low[...])
    count = outs[0].shape[0]
    for k, out in enumerate(outs):
        out[...] = packed[pl.ds(pl.multiple_of((d ^ k) * count, 8), count), :]


def transform(value, into_high, into_low):
    left_high, left_low = split_two(value)
    full = dot_nt(left_high, into_high[...]) + dot_nt(left_low, into_high[...]) + dot_nt(left_high, into_low[...])
    return full * (2.0 / NT)


def respond(value, same_side, cross_side):
    lanes = 2 * NF // 4
    bands = [value[:, i : i + lanes] for i in range(0, value.shape[1], lanes)]
    turned = jnp.concatenate([pltpu.roll(band, lanes // 2, 1) for band in bands], axis=1)
    return value * same_side + turned * cross_side


def wrapped_ends(value, end_high, end_low, end_sums, taps):
    beyond_high, beyond_low = split_two(transform(value, end_high, end_low) * taps[...])
    return dot_nn(beyond_high, end_sums[...]) + dot_nn(beyond_low, end_sums[...])


def inverse_kernel(high, low, end_high, end_low, sums, taps, same_side, cross_side, *rest):
    own, right, left, across, out, gathered, tab_high, tab_low, tab_end_high, tab_end_low, end_sums, sems, tab_sems = rest
    z = lax.axis_index("freq")
    lanes = own.shape[3]
    quarter = tab_high.shape[0]
    at_end = (z == 0) | (z == 3)
    rows = pl.ds(pl.multiple_of(RIM + z * quarter, 16), quarter)
    end_size = RIM * RIM
    end_rows = pl.ds(pl.multiple_of((z + 1) // 4 * end_size, 16), end_size)
    loads = []
    end_loads = [pltpu.make_async_copy(sums.at[end_rows], end_sums, tab_sems.at[16])]
    for slot, step in enumerate((0, 3, 1, 2)):
        cols = pl.ds(pl.multiple_of((z + step) % 4 * lanes, lanes), lanes)
        into = pl.ds(slot * lanes, lanes)
        for i, (table, scratch) in enumerate(((high, tab_high), (low, tab_low))):
            loads.append(pltpu.make_async_copy(table.at[rows, cols], scratch.at[:, into], tab_sems.at[4 * slot + i]))
        for i, (table, scratch) in enumerate(((end_high, tab_end_high), (end_low, tab_end_low))):
            copy = pltpu.make_async_copy(table.at[end_rows, cols], scratch.at[:, into], tab_sems.at[4 * slot + 2 + i])
            end_loads.append(copy)
    for load in loads:
        load.start()

    @pl.when(at_end)
    def _():
        for load in end_loads:
            load.start()

    def fetch(source, slot):
        return pltpu.make_async_copy(source, gathered.at[:, :, :, pl.ds(slot * lanes, lanes)], sems.at[slot])

    fetch(own, 0).start()
    fetch(across, 3).start()
    for slot, source, there in ((1, right, z > 0), (2, left, z < 3)):

        @pl.when(there)
        def _(slot=slot, source=source):
            fetch(source, slot).start()
            fetch(source, slot).wait()

        @pl.when(jnp.logical_not(there))
        def _(slot=slot):
            gathered[:, :, :, slot * lanes : (slot + 1) * lanes] = jnp.zeros(own.shape, jnp.float32)

    for load in loads:
        load.wait()
    fetch(own, 0).wait()
    fetch(across, 3).wait()
    total = math.prod(own.shape[:3])
    value = gathered[...].reshape(total, 4 * lanes)
    out[...] = transform(respond(value, same_side[...], cross_side[...]), tab_high, tab_low)

    @pl.when(at_end)
    def _():
        for load in end_loads:
            load.wait()
        wrapped = wrapped_ends(gathered[...].reshape(total, 4 * lanes), tab_end_high, tab_end_low, end_sums, taps)
        cols = pl.ds(pl.multiple_of(jnp.where(z == 0, 0, quarter - lanes), lanes), lanes)
        out[:, cols] = out[:, cols] - wrapped


def forward_kernel(high, low, end_high, end_low, sums, taps, same_side, cross_side, partial, forward, *rest):
    keep, send, tab_high, tab_low, tab_end_high, tab_end_low, end_sums, result, sems = rest
    z = lax.axis_index("freq")
    lanes = forward.shape[3]
    total, quarter = partial.shape
    at_end = (z == 0) | (z == 3)

    @pl.when(at_end)
    def _():
        rows = pl.ds(pl.multiple_of(RIM + z * quarter, 16), quarter)
        end_size = RIM * RIM
        end_rows = pl.ds(pl.multiple_of((z + 1) // 4 * end_size, 16), end_size)
        cols = pl.ds(pl.multiple_of((3 - z) * lanes, lanes), lanes)
        loads = [
            pltpu.make_async_copy(high.at[rows, cols], tab_high, sems.at[0]),
            pltpu.make_async_copy(low.at[rows, cols], tab_low, sems.at[1]),
            pltpu.make_async_copy(end_high.at[end_rows, cols], tab_end_high, sems.at[2]),
            pltpu.make_async_copy(end_low.at[end_rows, cols], tab_end_low, sems.at[3]),
            pltpu.make_async_copy(sums.at[end_rows], end_sums, sems.at[4]),
        ]
        run_all(loads)
        slot = jnp.where(z == 0, 1, 2)
        some = pl.ds(pl.multiple_of(slot * lanes, lanes), lanes)
        value = forward[...].reshape(total, lanes)
        answer = respond(value, same_side[:, some], cross_side[:, some])
        result[...] = partial[...] + transform(answer, tab_high, tab_low)
        wrapped = wrapped_ends(value, tab_end_high, tab_end_low, end_sums, taps)
        at = pl.ds(pl.multiple_of(jnp.where(z == 0, 0, quarter - lanes), lanes), lanes)
        result[:, at] = result[:, at] - wrapped
        keep[...] = result[: total // 2].reshape(keep.shape)
        send[...] = result[total // 2 :].reshape(send.shape)

    @pl.when(jnp.logical_not(at_end))
    def _():
        keep[...] = partial[: total // 2].reshape(keep.shape)
        send[...] = partial[total // 2 :].reshape(send.shape)


def unpack_kernel(most, *rest):
    slots, out = rest[:-1], rest[-1]
    d = lax.axis_index("shot")
    chip, core = d // 2, d % 2
    for q in range(len(slots) // 2):
        own, other = slots[2 * q][...], slots[2 * q + 1][...]
        first, second = jnp.where(core == 0, own, other), jnp.where(core == 0, other, own)
        rows = pl.ds(pl.multiple_of((chip ^ q) * (2 * most), 8), 2 * most)
        for b in range(out.shape[0]):
            some = slice(b * most, (b + 1) * most)
            out[b, rows, :] = jnp.concatenate([first[some], second[some]], axis=0)


def f32(*shape):
    return jax.ShapeDtypeStruct(shape, jnp.float32)


def kernel_call(body, out_shape, in_specs, out_specs, scratch, flops=0, moved=0, vmem=None):
    return pl.pallas_call(
        body,
        name=getattr(body, "func", body).__name__,
        out_shape=out_shape,
        in_specs=in_specs,
        out_specs=out_specs,
        scratch_shapes=scratch,
        compiler_params=pltpu.CompilerParams(vmem_limit_bytes=vmem),
        cost_estimate=pl.CostEstimate(flops=flops, bytes_accessed=moved, transcendentals=0),
    )


def plane_device(traces, live_mask, offset_bin, surface, block_owner, point_column, filters):
    shots, receivers, quarter = traces.shape
    devices = lax.axis_size("shot")
    points = STEPS * POINTS_BLK
    rows = shots * receivers
    bins_total = filters.shape[0] * devices
    most = max(2, 3 * rows // (2 * bins_total))
    lanes = surface.shape[2]
    half = receivers // 2
    chunk = receivers // devices
    core = lax.axis_index("shot") & 1
    high, low = (jnp.asarray(x) for x in wave_constant(lax.axis_size("freq")))
    dma = pltpu.SemaphoreType.DMA

    to_sibling = kernel_call(
        sibling_kernel, f32(POINTS_BLK, half, lanes), [ANY], VMEM, [dma], moved=2 << 20, vmem=8 << 20
    )(surface)
    sibling = swap(to_sibling, "shot", devices, 1)

    bins = offset_bin.reshape(shots, receivers)
    bands = kernel_call(
        spectra_kernel,
        [f32(shots * points + 8, lanes)] * 4,
        [SMEM, SMEM, VMEM, VMEM, VMEM, ANY, ANY],
        [VMEM] * 4,
        [
            pltpu.VMEM((shots * points, quarter), jnp.float32),
            pltpu.VMEM((quarter, 2 * NF), jnp.bfloat16),
            pltpu.VMEM((quarter, 2 * NF), jnp.bfloat16),
            pltpu.VMEM((shots * points, 2 * NF), jnp.float32),
            dma((2,)),
        ],
        moved=1 << 21,
        vmem=16 << 20,
    )(point_column, live_mask, traces, bins, filters, high, low)
    def scatter(step):
        pieces = kernel_call(
            functools.partial(pieces_kernel, step),
            [f32(POINTS_BLK, chunk, lanes)] * 3,
            [SMEM, VMEM, VMEM],
            [VMEM] * 3,
            [],
            moved=4 << 20,
            vmem=24 << 20,
        )(block_owner, surface, sibling)
        return [swap(piece, "shot", devices, 2 * (k + 1)) for k, piece in enumerate(pieces)]

    sides = [pltpu.VMEM((8, shots * points, lanes), jnp.float32)] * 2
    cost = shots * chunk * points * lanes * 8

    def others(*sent):
        return kernel_call(
            functools.partial(others_kernel, len(sent) > 3),
            [f32(2 * shots, chunk, lanes)] * 3 + [f32(STEPS, POINTS_BLK, chunk, lanes)],
            [SMEM] + [ANY] * (2 + len(sent)) + [VMEM] * 2,
            [VMEM] * 4,
            sides + [dma((STEPS,))],
            flops=3 * cost,
            moved=1 << 20,
            vmem=16 << 20,
        )(block_owner, surface, sibling, *sent, *every)

    sent = scatter(0)

    spectra = bands[0]
    for k in (3, 2, 1):
        spectra = spectra + swap(bands[k], "freq", 4, k)
    far, second, first = [swap(spectra, "shot", devices, 2 * q) for q in (3, 2, 1)]
    every = jnp.stack([spectra, first, second, far])
    sent[2:], every = lax.optimization_barrier((sent[2:], every))
    every = [every, swap(every, "shot", devices, 1)]

    places = kernel_call(
        functools.partial(slots_kernel, most),
        jax.ShapeDtypeStruct((bins_total * most, rows), jnp.bfloat16),
        [VMEM] * 2,
        VMEM,
        [],
        flops=rows * rows * 100,
        moved=1 << 21,
        vmem=24 << 20,
    )(offset_bin.reshape(1, rows), live_mask.reshape(1, rows))

    waves = jnp.asarray(tap_constant(lax.axis_size("freq"), lanes))
    end_high, end_low, picks, sums = (jnp.asarray(x) for x in end_constants(lax.axis_size("freq"), lanes))
    taps, same_side, cross_side = kernel_call(
        functools.partial(response_kernel, filters.shape[0]),
        [f32(rows, RIM * RIM), f32(rows, 4 * lanes), f32(rows, 4 * lanes)],
        [VMEM] * 5,
        [VMEM] * 3,
        [pltpu.VMEM((devices, 8, lanes), jnp.float32)],
        flops=rows * 64 * 4 * 1152,
        moved=1 << 22,
        vmem=24 << 20,
    )(bins, waves, picks, *every)

    both = (block_owner[0] ^ block_owner[1]) == 1
    sent, every = lax.optimization_barrier((sent, every))
    *outs, chosen = lax.cond(both, lambda *sent: others(*sent, *scatter(1)), others, *sent)
    turned = {q: swap(outs[q - 1], "shot", devices, 2 * q) for q in (3, 2, 1)}
    own = kernel_call(
        own_kernel,
        f32(2 * shots, chunk, lanes),
        [VMEM] * 3,
        VMEM,
        sides,
        flops=cost,
        moved=1 << 20,
        vmem=16 << 20,
    )(chosen, *every)
    own = kernel_call(
        arrange_kernel,
        f32(2 * shots, 4, chunk, lanes),
        [VMEM] * 4,
        VMEM,
        [],
        moved=1 << 19,
        vmem=8 << 20,
    )(own, turned[1], turned[2], turned[3])
    across = swap(own, "freq", 4, 2)
    right = lax.ppermute(own, "freq", [(0, 1), (1, 2), (2, 3)])
    left = lax.ppermute(own, "freq", [(1, 0), (2, 1), (3, 2)])
    forward = lax.ppermute(across, "freq", [(2, 3), (1, 0)])

    tables = (high, low, end_high, end_low, sums, taps, same_side, cross_side)
    bf16 = functools.partial(pltpu.VMEM, dtype=jnp.bfloat16)
    partial = kernel_call(
        inverse_kernel,
        f32(rows, quarter),
        [ANY] * 5 + [VMEM] * 3 + [ANY] * 4,
        VMEM,
        [
            pltpu.VMEM((2 * shots, 4, chunk, 4 * lanes), jnp.float32),
            bf16((quarter, 4 * lanes)),
            bf16((quarter, 4 * lanes)),
            bf16((RIM * RIM, 4 * lanes)),
            bf16((RIM * RIM, 4 * lanes)),
            bf16((RIM * RIM, lanes)),
            dma((4,)),
            dma((17,)),
        ],
        flops=6 * rows * 4 * lanes * quarter,
        moved=4 << 20,
        vmem=32 << 20,
    )(*tables, own, right, left, across)
    keep, send = kernel_call(
        forward_kernel,
        [f32(shots, half, quarter)] * 2,
        [ANY] * 5 + [VMEM] * 5,
        [VMEM] * 2,
        [
            bf16((quarter, lanes)),
            bf16((quarter, lanes)),
            bf16((RIM * RIM, lanes)),
            bf16((RIM * RIM, lanes)),
            bf16((RIM * RIM, lanes)),
            pltpu.VMEM((rows, quarter), jnp.float32),
            dma((5,)),
        ],
        flops=6 * rows * lanes * quarter,
        moved=2 << 20,
        vmem=32 << 20,
    )(*tables, partial, forward)
    got = swap(send, "shot", devices, 1)

    bin_slots = filters.shape[0] * most
    slots = kernel_call(
        clean_kernel,
        [f32(bin_slots, quarter)] * devices,
        [VMEM] * 4,
        [VMEM] * devices,
        [pltpu.VMEM((rows, quarter), jnp.bfloat16)] * 2 + [pltpu.VMEM((devices * bin_slots, quarter), jnp.float32)],
        flops=4 * rows * bins_total * most * quarter,
        moved=6 << 20,
        vmem=32 << 20,
    )(keep, got, traces, places)
    slots = [slots[0]] + [swap(slots[k], "shot", devices, k) for k in range(1, devices)]
    return kernel_call(
        functools.partial(unpack_kernel, most),
        f32(filters.shape[0], devices * most, quarter),
        [VMEM] * devices,
        VMEM,
        [],
        moved=3 << 20,
        vmem=16 << 20,
    )(*slots)


def with_halo(cells, sides, width):
    for axis, dim in sides:
        count = lax.axis_size(axis)
        ends = count - 1
        head = lax.slice_in_dim(cells, 0, width, axis=dim)
        tail = lax.slice_in_dim(cells, cells.shape[dim] - width, cells.shape[dim], axis=dim)
        cells = jnp.concatenate(
            [
                lax.ppermute(tail, axis, [(i, (i + 1) % count) for i in range(ends)]),
                cells,
                lax.ppermute(head, axis, [((i + 1) % count, i) for i in range(ends)]),
            ],
            axis=dim,
        )
    return cells


def broadcast(value, axis, source):
    kept = jnp.where(lax.axis_index(axis) == source, value, 0).astype(value.dtype)
    return lax.psum(kept, axis)


def wave_table(time_ids, comp_ids, band_width, period):
    mode_ids = comp_ids // (2 * band_width) * band_width + comp_ids % band_width
    phase_ids = (mode_ids[None, :] + 1) * time_ids[:, None] % period
    angles = phase_ids.astype(jnp.float32) * (2.0 * math.pi / period)
    real_part = comp_ids % (2 * band_width) < band_width
    return jnp.where(real_part[None, :], jnp.cos(angles), -jnp.sin(angles))


def cross_mix(left_side, right_side):
    return jnp.einsum("bsj,jrb->srb", left_side, right_side, precision=FULL_PRECISION)


def shifted_sum(widened, tap_table, out_width):
    half_span = (tap_table.shape[-1] - 1) // 2
    summed = jnp.zeros(widened.shape[:-1] + (out_width,), jnp.float32)
    for tap_index in range(tap_table.shape[-1]):
        offset_start = 2 * half_span - tap_index
        window = lax.slice_in_dim(
            widened, offset_start, offset_start + out_width, axis=widened.ndim - 1
        )
        summed = summed + tap_table[..., tap_index : tap_index + 1] * window
    return summed


def widened_rims(values):
    half_span = (TAPS - 1) // 2
    return with_halo(values, (("freq", 2),), half_span)


def pack_rows(values, slot_ids, total_slots):
    return jnp.zeros((total_slots, values.shape[-1]), jnp.float32).at[slot_ids].set(values)


def any_device(traces, live_mask, offset_bin, surface, block_owner, point_column, filters):
    shots_here, receivers, quarter = traces.shape
    freq_count = lax.axis_size("freq")
    shot_count = lax.axis_size("shot")
    band_width = NF // freq_count
    rows_here = shots_here * receivers
    bins_total = filters.shape[0] * shot_count
    most_slots = max(2, 3 * rows_here // (2 * bins_total))
    total_slots = bins_total * most_slots
    live_rows = live_mask.astype(jnp.float32)[:, :, None]
    live_traces = traces * live_rows
    columns = point_column.reshape(-1)
    picked = jnp.take(live_traces, columns, axis=1).reshape(shots_here * columns.shape[0], quarter)
    freq_index = lax.axis_index("freq")
    time_ids = freq_index * quarter + jnp.arange(quarter)
    band_ids = freq_index * 2 * band_width + jnp.arange(2 * band_width)
    wave_rows = wave_table(
        time_ids, jnp.arange(2 * band_width * lax.axis_size("freq")), band_width, NT
    )
    spectra = lax.psum_scatter(
        lax.dot_general(wave_rows, picked, (((0,), (1,)), ((), ())), precision=FULL_PRECISION),
        "freq",
        scatter_dimension=0,
        tiled=True,
    )
    spectra = spectra.reshape(2 * band_width, shots_here, columns.shape[0])
    real_sum = jnp.zeros((shots_here, receivers, band_width), jnp.float32)
    imag_sum = jnp.zeros((shots_here, receivers, band_width), jnp.float32)
    for step_index in range(STEPS):
        surface_part = broadcast(surface, "shot", block_owner[step_index])
        point_spectra = spectra[:, :, step_index * POINTS_BLK : (step_index + 1) * POINTS_BLK]
        data_real = point_spectra[:band_width]
        data_imag = point_spectra[band_width:]
        surf_real = surface_part[:, :, :band_width]
        surf_imag = surface_part[:, :, band_width:]
        real_sum = real_sum + (cross_mix(data_real, surf_real) - cross_mix(data_imag, surf_imag))
        imag_sum = imag_sum + (cross_mix(data_real, surf_imag) + cross_mix(data_imag, surf_real))
    prediction = jnp.concatenate([real_sum, imag_sum], axis=2).reshape(rows_here, 2 * band_width)
    inverse = wave_table(jnp.arange(NT), band_ids, band_width, NT).T * (2.0 / NT)
    partial_value = jnp.dot(prediction, inverse, precision=FULL_PRECISION)
    multiples = lax.psum_scatter(partial_value, "freq", scatter_dimension=1, tiled=True)
    multiples = multiples.reshape(shots_here, receivers, quarter) * live_rows
    bins_flat = offset_bin.reshape(rows_here)
    order_ids = jnp.arange(rows_here)
    earlier = (bins_flat[:, None] == bins_flat[None, :]) & (order_ids[None, :] < order_ids[:, None])
    rank_ids = jnp.sum(earlier.astype(jnp.int32), axis=1)
    slot_ids = bins_flat * most_slots + rank_ids
    every_filter = lax.all_gather(filters, "shot", axis=0, tiled=True)
    trace_taps = jnp.take(every_filter, bins_flat, axis=0).reshape(
        shots_here, receivers, every_filter.shape[1]
    )
    widened = widened_rims(multiples)
    cleaned = live_traces - shifted_sum(widened, trace_taps, quarter)
    cleaned_slots = pack_rows(cleaned.reshape(rows_here, quarter), slot_ids, total_slots)
    cleaned_slots = cleaned_slots.reshape(bins_total, most_slots, quarter)
    return lax.all_to_all(cleaned_slots, "shot", split_axis=0, concat_axis=1, tiled=True)


def on_device(traces, live_mask, offset_bin, surface, block_owner, point_column, filters):
    devices = lax.axis_size("shot")
    in_plane = devices == 8 and lax.axis_size("freq") == 4
    whole_tiles = traces.shape[1] % (8 * devices) == 0 and filters.shape[0] <= 8
    plan = plane_device if in_plane and whole_tiles else any_device
    return plan(traces, live_mask, offset_bin, surface, block_owner, point_column, filters)


def solution(mesh):
    return jax.shard_map(
        on_device,
        mesh=mesh,
        in_specs=(
            P("shot", None, "freq"),
            P("shot", None),
            P("shot", None, None),
            P("shot", None, "freq"),
            P(),
            P(),
            P("shot", None),
        ),
        out_specs=P("shot", None, "freq"),
        check_vma=False,
    )
```

```python
import functools
import math

import jax
import jax.numpy as jnp
import numpy as np
from jax import lax
from jax.experimental import pallas as pl
from jax.experimental.pallas import tpu as pltpu
from jax.sharding import PartitionSpec as P

NT = 1024
NF = 256
TAPS = 31
POINTS_BLK = 16
STEPS = 2
RIM = 16
FAR_FIRST = (3, 1, 2)

FULL_PRECISION = lax.Precision.HIGHEST
VMEM = pl.BlockSpec(memory_space=pltpu.VMEM)
SMEM = pl.BlockSpec(memory_space=pltpu.SMEM)
ANY = pl.BlockSpec(memory_space=pl.ANY)


def wave_constant(bands):
    width = NF // bands
    comps = np.arange(2 * NF)
    modes = comps // (2 * width) * width + comps % width
    phases = (modes[None, :] + 1) * np.arange(NT)[:, None] % NT
    angles = phases * (2.0 * math.pi / NT)
    table = np.where((comps % (2 * width) < width)[None, :], np.cos(angles), -np.sin(angles))
    table = np.pad(table, ((RIM, RIM), (0, 0))).astype(np.float32)
    high = table.astype(jnp.bfloat16)
    low = (table - high.astype(np.float32)).astype(jnp.bfloat16)
    return high, low


def tap_constant(bands, lanes):
    high, low = wave_constant(bands)
    table = high.astype(np.float32) + low.astype(np.float32)
    shifts = (np.arange(TAPS) - (TAPS - 1) // 2) % NT
    return np.pad(table[RIM + shifts], ((0, lanes - TAPS), (0, 0)))


def end_constants(bands, lanes):
    high, low = wave_constant(bands)
    k, t = np.divmod(np.arange(RIM * RIM), RIM)
    waves = [np.stack([part[NT + k], part[RIM + k]]).reshape(2 * RIM * RIM, -1) for part in (high, low)]
    half_span = (TAPS - 1) // 2
    picks = np.zeros((2, lanes, RIM * RIM), np.float32)
    sums = np.zeros((2, RIM * RIM, lanes), np.float32)
    for side, tap, lane in ((0, t + RIM - k + half_span, t), (1, t - 1 - k, lanes - RIM + t)):
        fits = (tap >= 0) & (tap < TAPS)
        picks[side, tap[fits], np.arange(RIM * RIM)[fits]] = 1
        sums[side, np.arange(RIM * RIM), lane] = 1
    return *waves, picks, sums.reshape(2 * RIM * RIM, lanes).astype(jnp.bfloat16)


def split_two(value):
    high = value.astype(jnp.bfloat16)
    return high, (value - high.astype(jnp.float32)).astype(jnp.bfloat16)


def dot_nn(left, right):
    return lax.dot_general(left, right, (((1,), (0,)), ((), ())), preferred_element_type=jnp.float32)


def dot_nt(left, right):
    return lax.dot_general(left, right, (((1,), (1,)), ((), ())), preferred_element_type=jnp.float32)


def run_all(copies):
    for copy in copies:
        copy.start()
    for copy in copies:
        copy.wait()


def swap(value, axis, count, bit):
    return lax.ppermute(value, axis, [(i, i ^ bit) for i in range(count)])


def spectra_kernel(cols, live, traces, bins, filters, high, low, *rest):
    outs, (picked, tab_high, tab_low, part, sems) = rest[:4], rest[4:]
    shots, _, quarter = traces.shape
    z = lax.axis_index("freq")
    rows = pl.ds(pl.multiple_of(RIM + z * quarter, 16), quarter)
    loads = [
        pltpu.make_async_copy(high.at[rows], tab_high, sems.at[0]),
        pltpu.make_async_copy(low.at[rows], tab_low, sems.at[1]),
    ]
    for load in loads:
        load.start()
    per_block = cols.shape[1]
    points = cols.shape[0] * per_block
    for j in range(points):
        col = cols[j // per_block, j % per_block]
        for s in range(shots):
            row = traces[s, pl.ds(col, 1), :]
            picked[s * points + j : s * points + j + 1, :] = row * live[s, col].astype(jnp.float32)
    for load in loads:
        load.wait()
    left_high, left_low = split_two(picked[...])
    part[...] = (
        dot_nn(left_high, tab_high[...]) + dot_nn(left_low, tab_high[...]) + dot_nn(left_high, tab_low[...])
    )
    lines, lanes = outs[0].shape
    rows = shots * points
    for k, out in enumerate(outs):
        out[:rows] = part[:, pl.ds(pl.multiple_of((z ^ k) * lanes, lanes), lanes)]
        out[rows:] = jnp.zeros((lines - rows, lanes), jnp.float32)
    own = filters.shape[0]
    outs[0][rows : rows + own, : filters.shape[1]] = filters[...]
    half = bins.shape[1] // 2
    other = 1 - lax.axis_index("shot") % 2
    there = bins[:, pl.ds(pl.multiple_of(other * half, half), half)]
    outs[0][rows + own : rows + own + shots, :half] = there.astype(jnp.float32)


def sibling_kernel(surface, out, sem):
    half = out.shape[1]
    core = lax.axis_index("shot") % 2
    copy = pltpu.make_async_copy(surface.at[:, pl.ds(pl.multiple_of((1 - core) * half, 8), half)], out, sem)
    copy.start()
    copy.wait()


def pieces_kernel(step, owners, surface, sibling, *outs):
    d = lax.axis_index("shot")
    chip, core = d // 2, d % 2
    half = sibling.shape[1]
    chunk = outs[0].shape[1]
    first_owner, other_owner = owners[step], owners[1 - step]
    owner_core = jnp.where(first_owner // 2 == chip, first_owner % 2, other_owner % 2)
    for source, base, wanted in ((surface, core * half, owner_core == core), (sibling, 0, owner_core != core)):

        @pl.when(wanted)
        def _(source=source, base=base):
            for k, out in enumerate(outs):
                first = base + (chip ^ (k + 1)) * chunk
                out[...] = source[:, pl.ds(pl.multiple_of(first, 8), chunk), :]


def predict(chosen, spectra, real_side, imag_side, outs):
    points = STEPS * POINTS_BLK
    rows = real_side.shape[1]
    shots = rows // points
    size, lanes = chosen.shape[2:]
    lane = lax.broadcasted_iota(jnp.int32, (rows, lanes), 1)
    for q in outs:
        for c in range(2):
            value = spectra[c][q, :rows, :]
            turned = pltpu.roll(value, lanes // 2, 1)
            real_side[2 * q + c] = jnp.where(lane < lanes // 2, value, turned)
            imag_side[2 * q + c] = jnp.where(lane < lanes // 2, turned, -value)
    yield
    for q, out in outs.items():

        @pl.loop(0, 2)
        def _(rel, q=q, out=out):
            at = 2 * q + rel
            first_sum = [jnp.zeros((size, lanes), jnp.float32)] * shots
            second_sum = [jnp.zeros((size, lanes), jnp.float32)] * shots
            for j in range(points):
                block = chosen[j // POINTS_BLK, j % POINTS_BLK]
                for s in range(shots):
                    row = s * points + j
                    first_sum[s] = first_sum[s] + real_side[at, row : row + 1, :] * block
                    second_sum[s] = second_sum[s] + imag_side[at, row : row + 1, :] * block
            for s in range(shots):
                out[rel * shots + s] = first_sum[s] + pltpu.roll(second_sum[s], lanes // 2, 1)


def others_kernel(extra, owners, surface, sibling, *rest):
    sent, spectra, outs, (chosen, real_side, imag_side, sems) = rest[:-9], rest[-9:-7], rest[-7:-4], rest[-4:]
    d = lax.axis_index("shot")
    chip, core = d // 2, d % 2
    half = sibling.shape[1]
    chunk = chosen.shape[2]
    for b in range(STEPS):
        owner = owners[b]
        step, owner_core = (owner // 2) ^ chip, owner % 2

        @pl.when((step == 0) & (owner_core == core))
        def _():
            rows = pl.ds(pl.multiple_of(core * half + chip * chunk, 8), chunk)
            pltpu.make_async_copy(surface.at[:, rows], chosen.at[b], sems.at[b]).start()

        @pl.when((step == 0) & (owner_core != core))
        def _():
            rows = pl.ds(pl.multiple_of(chip * chunk, 8), chunk)
            pltpu.make_async_copy(sibling.at[:, rows], chosen.at[b], sems.at[b]).start()

        for k in range(3):

            @pl.when(step == k + 1)
            def _():
                source = sent[3 + k] if extra and b == 1 else sent[k]
                pltpu.make_async_copy(source, chosen.at[b], sems.at[b]).start()

    steps = predict(chosen, spectra, real_side, imag_side, dict(zip((1, 2, 3), outs)))
    next(steps)
    for b in range(STEPS):
        pltpu.make_async_copy(sibling.at[:, pl.ds(0, chunk)], chosen.at[b], sems.at[b]).wait()
    for _ in steps:
        pass


def own_kernel(chosen, own, other, out, real_side, imag_side):
    for _ in predict(chosen, (own, other), real_side, imag_side, {0: out}):
        pass


def arrange_kernel(order, *rest):
    pieces, out = rest[:-1], rest[-1]
    chip = lax.axis_index("shot") // 2
    for q, piece in zip(order, pieces):
        out[:, chip ^ q] = piece[...]


def slots_kernel(most, bins, live, places):
    total = bins.shape[1]
    bins_total = places.shape[0] // most
    member = (lax.broadcasted_iota(jnp.int32, (bins_total, total), 0) == bins[...]).astype(jnp.float32)
    before = lax.broadcasted_iota(jnp.int32, (total, total), 0) < lax.broadcasted_iota(jnp.int32, (total, total), 1)
    counts = dot_nn(member.astype(jnp.bfloat16), before.astype(jnp.float32).astype(jnp.bfloat16))
    rank = jnp.sum(counts * member, axis=0, keepdims=True)
    slot = bins[...] * most + rank.astype(jnp.int32)
    slot = jnp.where(live[...] != 0, slot, -1)
    at = lax.broadcasted_iota(jnp.int32, places.shape, 0)
    places[...] = (at == slot).astype(jnp.float32).astype(jnp.bfloat16)


def response_kernel(own_bins, bins, waves, picks, *rest):
    spectra, (taps, same_side, cross_side, filters) = rest[:2], rest[2:]
    d = lax.axis_index("shot")
    z = lax.axis_index("freq")
    lines = spectra[0].shape[1]
    for q in range(4):
        for c in range(2):
            filters[d ^ (2 * q + c)] = spectra[c][q, lines - 8 :, :]
    devices, padded, lanes = filters.shape
    shots, receivers = bins.shape
    half = receivers // 2
    here = bins[:, pl.ds(pl.multiple_of(d % 2 * half, half), half)]
    first = lines - 8 + own_bins
    there = spectra[1][0, first : first + shots, :half].astype(jnp.int32)
    lists = [some[s : s + 1] for some in (here, there) for s in range(shots)]
    bin_row = jnp.concatenate(lists, axis=1)
    shape = (devices * padded, shots * receivers)
    row = lax.broadcasted_iota(jnp.int32, shape, 0)
    bin_of_row = jnp.where(row % padded < own_bins, row // padded * own_bins + row % padded, -1)
    member = (bin_of_row == bin_row).astype(jnp.float32).astype(jnp.bfloat16)

    def per_trace(table):
        high, low = split_two(table)
        dims = (((0,), (0,)), ((), ()))
        return lax.dot_general(member, high, dims, preferred_element_type=jnp.float32) + lax.dot_general(
            member, low, dims, preferred_element_type=jnp.float32
        )

    table = filters[...].reshape(devices * padded, lanes)
    side = picks[(z + 1) // 4]
    taps[...] = per_trace(jnp.dot(table, side, precision=FULL_PRECISION, preferred_element_type=jnp.float32))
    lane = lax.broadcasted_iota(jnp.int32, (devices * padded, lanes), 1)
    for slot in range(4):
        cols = pl.ds(pl.multiple_of((z ^ slot) * lanes, lanes), lanes)
        answer = jnp.dot(table, waves[:, cols], precision=FULL_PRECISION, preferred_element_type=jnp.float32)
        turned = pltpu.roll(answer, lanes // 2, 1)
        into = slice(slot * lanes, (slot + 1) * lanes)
        same_side[:, into] = per_trace(jnp.where(lane < lanes // 2, answer, turned))
        cross_side[:, into] = per_trace(jnp.where(lane < lanes // 2, -turned, answer))


def clean_kernel(keep, got, traces, places, *rest):
    outs, (high, low, packed) = rest[:-3], rest[-3:]
    d = lax.axis_index("shot")
    core = d % 2
    shots, receivers, _ = traces.shape
    half = keep.shape[1]
    for source, side in ((keep, core), (got, 1 - core)):
        for s in range(shots):
            first = pl.multiple_of(side * half, half)
            flat = pl.ds(pl.multiple_of(s * receivers + first, half), half)
            clean_high, clean_low = split_two(traces[s, pl.ds(first, half), :] - source[s])
            high[flat, :] = clean_high
            low[flat, :] = clean_low
    packed[...] = dot_nn(places[...], high[...]) + dot_nn(places[...], low[...])
    count = outs[0].shape[0]
    for k, out in enumerate(outs):
        out[...] = packed[pl.ds(pl.multiple_of((d ^ k) * count, 8), count), :]


def transform(value, into_high, into_low):
    left_high, left_low = split_two(value)
    full = dot_nt(left_high, into_high[...]) + dot_nt(left_low, into_high[...]) + dot_nt(left_high, into_low[...])
    return full * (2.0 / NT)


def transform_band(value, into_high, into_low):
    left_high, left_low = split_two(value)
    both = jnp.concatenate([left_high, left_low], axis=1)
    twice = jnp.concatenate([into_high[...], into_high[...]], axis=1)
    return (dot_nt(both, twice) + dot_nt(left_high, into_low[...])) * (2.0 / NT)


def respond(value, same_side, cross_side):
    lanes = 2 * NF // 4
    bands = [value[:, i : i + lanes] for i in range(0, value.shape[1], lanes)]
    turned = jnp.concatenate([pltpu.roll(band, lanes // 2, 1) for band in bands], axis=1)
    return value * same_side + turned * cross_side


def wrapped_ends(beyond, end_sums, taps):
    beyond_high, beyond_low = split_two(beyond * taps[...])
    return dot_nn(beyond_high, end_sums[...]) + dot_nn(beyond_low, end_sums[...])


def inverse_kernel(high, low, end_high, end_low, sums, taps, same_side, cross_side, *rest):
    own, near, across, middle, out, gathered, tab_high, tab_low, tab_end_high, tab_end_low, end_sums, sems, tab_sems = rest
    z = lax.axis_index("freq")
    lanes = own.shape[3]
    quarter = tab_high.shape[0]
    at_end = (z == 0) | (z == 3)
    rows = pl.ds(pl.multiple_of(RIM + z * quarter, 16), quarter)
    end_size = RIM * RIM
    end_rows = pl.ds(pl.multiple_of((z + 1) // 4 * end_size, 16), end_size)
    loads = []
    end_loads = [pltpu.make_async_copy(sums.at[end_rows], end_sums, tab_sems.at[16])]
    for slot in range(4):
        cols = pl.ds(pl.multiple_of((z ^ slot) * lanes, lanes), lanes)
        into = pl.ds(slot * lanes, lanes)
        for i, (table, scratch) in enumerate(((high, tab_high), (low, tab_low))):
            loads.append(pltpu.make_async_copy(table.at[rows, cols], scratch.at[:, into], tab_sems.at[4 * slot + i]))
        for i, (table, scratch) in enumerate(((end_high, tab_end_high), (end_low, tab_end_low))):
            copy = pltpu.make_async_copy(table.at[end_rows, cols], scratch.at[:, into], tab_sems.at[4 * slot + 2 + i])
            end_loads.append(copy)
    for load in loads:
        load.start()

    @pl.when(at_end)
    def _():
        for load in end_loads:
            load.start()

    def fetch(source, slot):
        return pltpu.make_async_copy(source, gathered.at[:, :, :, pl.ds(slot * lanes, lanes)], sems.at[slot])

    straight = [fetch(band, slot) for slot, band in enumerate((own, near, across))]
    for copy in straight:
        copy.start()

    @pl.when(at_end)
    def _():
        gathered[:, :, :, 3 * lanes :] = jnp.zeros(own.shape, jnp.float32)

    @pl.when(jnp.logical_not(at_end))
    def _():
        fetch(middle, 3).start()
        fetch(middle, 3).wait()

    for copy in loads + straight:
        copy.wait()
    total = math.prod(own.shape[:3])
    value = gathered[...].reshape(total, 4 * lanes)
    out[...] = transform(respond(value, same_side[...], cross_side[...]), tab_high, tab_low)

    @pl.when(at_end)
    def _():
        for load in end_loads:
            load.wait()
        beyond = transform(gathered[...].reshape(total, 4 * lanes), tab_end_high, tab_end_low)
        wrapped = wrapped_ends(beyond, end_sums, taps)
        cols = pl.ds(pl.multiple_of(jnp.where(z == 0, 0, quarter - lanes), lanes), lanes)
        out[:, cols] = out[:, cols] - wrapped


def forward_kernel(high, low, end_high, end_low, sums, taps, same_side, cross_side, partial, forward, *rest):
    keep, send, tab_high, tab_low, tab_end_high, tab_end_low, end_sums, result, sems = rest
    z = lax.axis_index("freq")
    lanes = forward.shape[3]
    total, quarter = partial.shape
    at_end = (z == 0) | (z == 3)

    @pl.when(at_end)
    def _():
        rows = pl.ds(pl.multiple_of(RIM + z * quarter, 16), quarter)
        end_size = RIM * RIM
        end_rows = pl.ds(pl.multiple_of((z + 1) // 4 * end_size, 16), end_size)
        cols = pl.ds(pl.multiple_of((3 - z) * lanes, lanes), lanes)
        loads = [
            pltpu.make_async_copy(high.at[rows, cols], tab_high, sems.at[0]),
            pltpu.make_async_copy(low.at[rows, cols], tab_low, sems.at[1]),
            pltpu.make_async_copy(end_high.at[end_rows, cols], tab_end_high, sems.at[2]),
            pltpu.make_async_copy(end_low.at[end_rows, cols], tab_end_low, sems.at[3]),
            pltpu.make_async_copy(sums.at[end_rows], end_sums, sems.at[4]),
        ]
        run_all(loads)
        some = slice(3 * lanes, 4 * lanes)
        value = forward[...].reshape(total, lanes)
        answer = respond(value, same_side[:, some], cross_side[:, some])
        result[...] = partial[...] + transform_band(answer, tab_high, tab_low)
        wrapped = wrapped_ends(transform_band(value, tab_end_high, tab_end_low), end_sums, taps)
        at = pl.ds(pl.multiple_of(jnp.where(z == 0, 0, quarter - lanes), lanes), lanes)
        result[:, at] = result[:, at] - wrapped
        keep[...] = result[: total // 2].reshape(keep.shape)
        send[...] = result[total // 2 :].reshape(send.shape)

    @pl.when(jnp.logical_not(at_end))
    def _():
        keep[...] = partial[: total // 2].reshape(keep.shape)
        send[...] = partial[total // 2 :].reshape(send.shape)


def unpack_kernel(most, order, *rest):
    slots, out = dict(zip(order, rest[:-1])), rest[-1]
    d = lax.axis_index("shot")
    chip, core = d // 2, d % 2
    for q in range(len(slots) // 2):
        own, other = slots[2 * q][...], slots[2 * q + 1][...]
        first, second = jnp.where(core == 0, own, other), jnp.where(core == 0, other, own)
        rows = pl.ds(pl.multiple_of((chip ^ q) * (2 * most), 8), 2 * most)
        for b in range(out.shape[0]):
            some = slice(b * most, (b + 1) * most)
            out[b, rows, :] = jnp.concatenate([first[some], second[some]], axis=0)


def f32(*shape):
    return jax.ShapeDtypeStruct(shape, jnp.float32)


def kernel_call(body, out_shape, in_specs, out_specs, scratch, flops=0, moved=0, vmem=None):
    return pl.pallas_call(
        body,
        name=getattr(body, "func", body).__name__,
        out_shape=out_shape,
        in_specs=in_specs,
        out_specs=out_specs,
        scratch_shapes=scratch,
        compiler_params=pltpu.CompilerParams(vmem_limit_bytes=vmem),
        cost_estimate=pl.CostEstimate(flops=flops, bytes_accessed=moved, transcendentals=0),
    )


def plane_device(traces, live_mask, offset_bin, surface, block_owner, point_column, filters):
    shots, receivers, quarter = traces.shape
    devices = lax.axis_size("shot")
    points = STEPS * POINTS_BLK
    rows = shots * receivers
    bins_total = filters.shape[0] * devices
    most = max(2, 3 * rows // (2 * bins_total))
    lanes = surface.shape[2]
    half = receivers // 2
    chunk = receivers // devices
    core = lax.axis_index("shot") & 1
    high, low = (jnp.asarray(x) for x in wave_constant(lax.axis_size("freq")))
    dma = pltpu.SemaphoreType.DMA

    to_sibling = kernel_call(
        sibling_kernel, f32(POINTS_BLK, half, lanes), [ANY], VMEM, [dma], moved=2 << 20, vmem=8 << 20
    )(surface)
    sibling = swap(to_sibling, "shot", devices, 1)

    bins = offset_bin.reshape(shots, receivers)
    bands = kernel_call(
        spectra_kernel,
        [f32(shots * points + 8, lanes)] * 4,
        [SMEM, SMEM, VMEM, VMEM, VMEM, ANY, ANY],
        [VMEM] * 4,
        [
            pltpu.VMEM((shots * points, quarter), jnp.float32),
            pltpu.VMEM((quarter, 2 * NF), jnp.bfloat16),
            pltpu.VMEM((quarter, 2 * NF), jnp.bfloat16),
            pltpu.VMEM((shots * points, 2 * NF), jnp.float32),
            dma((2,)),
        ],
        moved=1 << 21,
        vmem=16 << 20,
    )(point_column, live_mask, traces, bins, filters, high, low)
    def scatter(step):
        pieces = kernel_call(
            functools.partial(pieces_kernel, step),
            [f32(POINTS_BLK, chunk, lanes)] * 3,
            [SMEM, VMEM, VMEM],
            [VMEM] * 3,
            [],
            moved=4 << 20,
            vmem=24 << 20,
        )(block_owner, surface, sibling)
        return [swap(piece, "shot", devices, 2 * (k + 1)) for k, piece in enumerate(pieces)]

    sides = [pltpu.VMEM((8, shots * points, lanes), jnp.float32)] * 2
    cost = shots * chunk * points * lanes * 8

    def others(*sent):
        return kernel_call(
            functools.partial(others_kernel, len(sent) > 3),
            [f32(2 * shots, chunk, lanes)] * 3 + [f32(STEPS, POINTS_BLK, chunk, lanes)],
            [SMEM] + [ANY] * (2 + len(sent)) + [VMEM] * 2,
            [VMEM] * 4,
            sides + [dma((STEPS,))],
            flops=3 * cost,
            moved=1 << 20,
            vmem=16 << 20,
        )(block_owner, surface, sibling, *sent, *every)

    sent = scatter(0)

    spectra = bands[0]
    for k in (3, 2, 1):
        spectra = spectra + swap(bands[k], "freq", 4, k)
    far, second, first = [swap(spectra, "shot", devices, 2 * q) for q in (3, 2, 1)]
    every = jnp.stack([spectra, first, second, far])
    sent[2:], every = lax.optimization_barrier((sent[2:], every))
    every = [every, swap(every, "shot", devices, 1)]

    places = kernel_call(
        functools.partial(slots_kernel, most),
        jax.ShapeDtypeStruct((bins_total * most, rows), jnp.bfloat16),
        [VMEM] * 2,
        VMEM,
        [],
        flops=rows * rows * 100,
        moved=1 << 21,
        vmem=24 << 20,
    )(offset_bin.reshape(1, rows), live_mask.reshape(1, rows))

    waves = jnp.asarray(tap_constant(lax.axis_size("freq"), lanes))
    end_high, end_low, picks, sums = (jnp.asarray(x) for x in end_constants(lax.axis_size("freq"), lanes))
    taps, same_side, cross_side = kernel_call(
        functools.partial(response_kernel, filters.shape[0]),
        [f32(rows, RIM * RIM), f32(rows, 4 * lanes), f32(rows, 4 * lanes)],
        [VMEM] * 5,
        [VMEM] * 3,
        [pltpu.VMEM((devices, 8, lanes), jnp.float32)],
        flops=rows * 64 * 4 * 1152,
        moved=1 << 22,
        vmem=24 << 20,
    )(bins, waves, picks, *every)

    both = (block_owner[0] ^ block_owner[1]) == 1
    sent, every = lax.optimization_barrier((sent, every))
    *outs, chosen = lax.cond(both, lambda *sent: others(*sent, *scatter(1)), others, *sent)
    turned = {q: swap(outs[q - 1], "shot", devices, 2 * q) for q in FAR_FIRST}
    own = kernel_call(
        own_kernel,
        f32(2 * shots, chunk, lanes),
        [VMEM] * 3,
        VMEM,
        sides,
        flops=cost,
        moved=1 << 20,
        vmem=16 << 20,
    )(chosen, *every)
    own = kernel_call(
        functools.partial(arrange_kernel, FAR_FIRST + (0,)),
        f32(2 * shots, 4, chunk, lanes),
        [VMEM] * 4,
        VMEM,
        [],
        moved=1 << 19,
        vmem=8 << 20,
    )(*[turned[q] for q in FAR_FIRST], own)
    across = swap(own, "freq", 4, 2)
    near = swap(own, "freq", 4, 1)
    middle = lax.ppermute(own, "freq", [(1, 2), (2, 1)])
    forward = lax.ppermute(across, "freq", [(2, 3), (1, 0)])

    tables = (high, low, end_high, end_low, sums, taps, same_side, cross_side)
    bf16 = functools.partial(pltpu.VMEM, dtype=jnp.bfloat16)
    partial = kernel_call(
        inverse_kernel,
        f32(rows, quarter),
        [ANY] * 5 + [VMEM] * 3 + [ANY] * 4,
        VMEM,
        [
            pltpu.VMEM((2 * shots, 4, chunk, 4 * lanes), jnp.float32),
            bf16((quarter, 4 * lanes)),
            bf16((quarter, 4 * lanes)),
            bf16((RIM * RIM, 4 * lanes)),
            bf16((RIM * RIM, 4 * lanes)),
            bf16((RIM * RIM, lanes)),
            dma((4,)),
            dma((17,)),
        ],
        flops=6 * rows * 4 * lanes * quarter,
        moved=4 << 20,
        vmem=32 << 20,
    )(*tables, own, near, across, middle)
    keep, send = kernel_call(
        forward_kernel,
        [f32(shots, half, quarter)] * 2,
        [ANY] * 5 + [VMEM] * 5,
        [VMEM] * 2,
        [
            bf16((quarter, lanes)),
            bf16((quarter, lanes)),
            bf16((RIM * RIM, lanes)),
            bf16((RIM * RIM, lanes)),
            bf16((RIM * RIM, lanes)),
            pltpu.VMEM((rows, quarter), jnp.float32),
            dma((5,)),
        ],
        flops=6 * rows * lanes * quarter,
        moved=2 << 20,
        vmem=32 << 20,
    )(*tables, partial, forward)
    got = swap(send, "shot", devices, 1)

    bin_slots = filters.shape[0] * most
    slots = kernel_call(
        clean_kernel,
        [f32(bin_slots, quarter)] * devices,
        [VMEM] * 4,
        [VMEM] * devices,
        [pltpu.VMEM((rows, quarter), jnp.bfloat16)] * 2 + [pltpu.VMEM((devices * bin_slots, quarter), jnp.float32)],
        flops=4 * rows * bins_total * most * quarter,
        moved=6 << 20,
        vmem=32 << 20,
    )(keep, got, traces, places)
    order = [2 * q + c for q in FAR_FIRST for c in range(2)] + [1, 0]
    slots = [swap(slots[k], "shot", devices, k) if k else slots[k] for k in order]
    return kernel_call(
        functools.partial(unpack_kernel, most, order),
        f32(filters.shape[0], devices * most, quarter),
        [VMEM] * devices,
        VMEM,
        [],
        moved=3 << 20,
        vmem=16 << 20,
    )(*slots)


def with_halo(cells, sides, width):
    for axis, dim in sides:
        count = lax.axis_size(axis)
        ends = count - 1
        head = lax.slice_in_dim(cells, 0, width, axis=dim)
        tail = lax.slice_in_dim(cells, cells.shape[dim] - width, cells.shape[dim], axis=dim)
        cells = jnp.concatenate(
            [
                lax.ppermute(tail, axis, [(i, (i + 1) % count) for i in range(ends)]),
                cells,
                lax.ppermute(head, axis, [((i + 1) % count, i) for i in range(ends)]),
            ],
            axis=dim,
        )
    return cells


def broadcast(value, axis, source):
    kept = jnp.where(lax.axis_index(axis) == source, value, 0).astype(value.dtype)
    return lax.psum(kept, axis)


def wave_table(time_ids, comp_ids, band_width, period):
    mode_ids = comp_ids // (2 * band_width) * band_width + comp_ids % band_width
    phase_ids = (mode_ids[None, :] + 1) * time_ids[:, None] % period
    angles = phase_ids.astype(jnp.float32) * (2.0 * math.pi / period)
    real_part = comp_ids % (2 * band_width) < band_width
    return jnp.where(real_part[None, :], jnp.cos(angles), -jnp.sin(angles))


def cross_mix(left_side, right_side):
    return jnp.einsum("bsj,jrb->srb", left_side, right_side, precision=FULL_PRECISION)


def shifted_sum(widened, tap_table, out_width):
    half_span = (tap_table.shape[-1] - 1) // 2
    summed = jnp.zeros(widened.shape[:-1] + (out_width,), jnp.float32)
    for tap_index in range(tap_table.shape[-1]):
        offset_start = 2 * half_span - tap_index
        window = lax.slice_in_dim(
            widened, offset_start, offset_start + out_width, axis=widened.ndim - 1
        )
        summed = summed + tap_table[..., tap_index : tap_index + 1] * window
    return summed


def widened_rims(values):
    half_span = (TAPS - 1) // 2
    return with_halo(values, (("freq", 2),), half_span)


def pack_rows(values, slot_ids, total_slots):
    return jnp.zeros((total_slots, values.shape[-1]), jnp.float32).at[slot_ids].set(values)


def any_device(traces, live_mask, offset_bin, surface, block_owner, point_column, filters):
    shots_here, receivers, quarter = traces.shape
    freq_count = lax.axis_size("freq")
    shot_count = lax.axis_size("shot")
    band_width = NF // freq_count
    rows_here = shots_here * receivers
    bins_total = filters.shape[0] * shot_count
    most_slots = max(2, 3 * rows_here // (2 * bins_total))
    total_slots = bins_total * most_slots
    live_rows = live_mask.astype(jnp.float32)[:, :, None]
    live_traces = traces * live_rows
    columns = point_column.reshape(-1)
    picked = jnp.take(live_traces, columns, axis=1).reshape(shots_here * columns.shape[0], quarter)
    freq_index = lax.axis_index("freq")
    time_ids = freq_index * quarter + jnp.arange(quarter)
    band_ids = freq_index * 2 * band_width + jnp.arange(2 * band_width)
    wave_rows = wave_table(
        time_ids, jnp.arange(2 * band_width * lax.axis_size("freq")), band_width, NT
    )
    spectra = lax.psum_scatter(
        lax.dot_general(wave_rows, picked, (((0,), (1,)), ((), ())), precision=FULL_PRECISION),
        "freq",
        scatter_dimension=0,
        tiled=True,
    )
    spectra = spectra.reshape(2 * band_width, shots_here, columns.shape[0])
    real_sum = jnp.zeros((shots_here, receivers, band_width), jnp.float32)
    imag_sum = jnp.zeros((shots_here, receivers, band_width), jnp.float32)
    for step_index in range(STEPS):
        surface_part = broadcast(surface, "shot", block_owner[step_index])
        point_spectra = spectra[:, :, step_index * POINTS_BLK : (step_index + 1) * POINTS_BLK]
        data_real = point_spectra[:band_width]
        data_imag = point_spectra[band_width:]
        surf_real = surface_part[:, :, :band_width]
        surf_imag = surface_part[:, :, band_width:]
        real_sum = real_sum + (cross_mix(data_real, surf_real) - cross_mix(data_imag, surf_imag))
        imag_sum = imag_sum + (cross_mix(data_real, surf_imag) + cross_mix(data_imag, surf_real))
    prediction = jnp.concatenate([real_sum, imag_sum], axis=2).reshape(rows_here, 2 * band_width)
    inverse = wave_table(jnp.arange(NT), band_ids, band_width, NT).T * (2.0 / NT)
    partial_value = jnp.dot(prediction, inverse, precision=FULL_PRECISION)
    multiples = lax.psum_scatter(partial_value, "freq", scatter_dimension=1, tiled=True)
    multiples = multiples.reshape(shots_here, receivers, quarter) * live_rows
    bins_flat = offset_bin.reshape(rows_here)
    order_ids = jnp.arange(rows_here)
    earlier = (bins_flat[:, None] == bins_flat[None, :]) & (order_ids[None, :] < order_ids[:, None])
    rank_ids = jnp.sum(earlier.astype(jnp.int32), axis=1)
    slot_ids = bins_flat * most_slots + rank_ids
    every_filter = lax.all_gather(filters, "shot", axis=0, tiled=True)
    trace_taps = jnp.take(every_filter, bins_flat, axis=0).reshape(
        shots_here, receivers, every_filter.shape[1]
    )
    widened = widened_rims(multiples)
    cleaned = live_traces - shifted_sum(widened, trace_taps, quarter)
    cleaned_slots = pack_rows(cleaned.reshape(rows_here, quarter), slot_ids, total_slots)
    cleaned_slots = cleaned_slots.reshape(bins_total, most_slots, quarter)
    return lax.all_to_all(cleaned_slots, "shot", split_axis=0, concat_axis=1, tiled=True)


def on_device(traces, live_mask, offset_bin, surface, block_owner, point_column, filters):
    devices = lax.axis_size("shot")
    in_plane = devices == 8 and lax.axis_size("freq") == 4
    whole_tiles = traces.shape[1] % (8 * devices) == 0 and filters.shape[0] <= 8
    plan = plane_device if in_plane and whole_tiles else any_device
    return plan(traces, live_mask, offset_bin, surface, block_owner, point_column, filters)


def solution(mesh):
    return jax.shard_map(
        on_device,
        mesh=mesh,
        in_specs=(
            P("shot", None, "freq"),
            P("shot", None),
            P("shot", None, None),
            P("shot", None, "freq"),
            P(),
            P(),
            P("shot", None),
        ),
        out_specs=P("shot", None, "freq"),
        check_vma=False,
    )
```

```python
import functools
import math

import jax
import jax.numpy as jnp
import numpy as np
from jax import lax
from jax.experimental import pallas as pl
from jax.experimental.pallas import tpu as pltpu
from jax.sharding import PartitionSpec as P

NT = 1024
NF = 256
TAPS = 31
POINTS_BLK = 16
STEPS = 2
RIM = 16
FAR_FIRST = (3, 1, 2)

FULL_PRECISION = lax.Precision.HIGHEST
VMEM = pl.BlockSpec(memory_space=pltpu.VMEM)
SMEM = pl.BlockSpec(memory_space=pltpu.SMEM)
ANY = pl.BlockSpec(memory_space=pl.ANY)


def wave_constant(bands):
    width = NF // bands
    comps = np.arange(2 * NF)
    modes = comps // (2 * width) * width + comps % width
    phases = (modes[None, :] + 1) * np.arange(NT)[:, None] % NT
    angles = phases * (2.0 * math.pi / NT)
    table = np.where((comps % (2 * width) < width)[None, :], np.cos(angles), -np.sin(angles))
    table = np.pad(table, ((RIM, RIM), (0, 0))).astype(np.float32)
    high = table.astype(jnp.bfloat16)
    low = (table - high.astype(np.float32)).astype(jnp.bfloat16)
    return high, low


def tap_constant(bands, lanes):
    high, low = wave_constant(bands)
    table = high.astype(np.float32) + low.astype(np.float32)
    shifts = (np.arange(TAPS) - (TAPS - 1) // 2) % NT
    return np.pad(table[RIM + shifts], ((0, lanes - TAPS), (0, 0)))


def end_constants(bands, lanes):
    high, low = wave_constant(bands)
    k, t = np.divmod(np.arange(RIM * RIM), RIM)
    waves = [np.stack([part[NT + k], part[RIM + k]]).reshape(2 * RIM * RIM, -1) for part in (high, low)]
    half_span = (TAPS - 1) // 2
    picks = np.zeros((2, lanes, RIM * RIM), np.float32)
    sums = np.zeros((2, RIM * RIM, lanes), np.float32)
    for side, tap, lane in ((0, t + RIM - k + half_span, t), (1, t - 1 - k, lanes - RIM + t)):
        fits = (tap >= 0) & (tap < TAPS)
        picks[side, tap[fits], np.arange(RIM * RIM)[fits]] = 1
        sums[side, np.arange(RIM * RIM), lane] = 1
    return *waves, picks, sums.reshape(2 * RIM * RIM, lanes).astype(jnp.bfloat16)


def split_two(value):
    high = value.astype(jnp.bfloat16)
    return high, (value - high.astype(jnp.float32)).astype(jnp.bfloat16)


def dot_nn(left, right):
    return lax.dot_general(left, right, (((1,), (0,)), ((), ())), preferred_element_type=jnp.float32)


def dot_nt(left, right):
    return lax.dot_general(left, right, (((1,), (1,)), ((), ())), preferred_element_type=jnp.float32)


def run_all(copies):
    for copy in copies:
        copy.start()
    for copy in copies:
        copy.wait()


def swap(value, axis, count, bit):
    return lax.ppermute(value, axis, [(i, i ^ bit) for i in range(count)])


def spectra_kernel(cols, live, traces, bins, filters, high, low, *rest):
    outs, (picked, tab_high, tab_low, part, sems) = rest[:4], rest[4:]
    shots, _, quarter = traces.shape
    z = lax.axis_index("freq")
    rows = pl.ds(pl.multiple_of(RIM + z * quarter, 16), quarter)
    loads = [
        pltpu.make_async_copy(high.at[rows], tab_high, sems.at[0]),
        pltpu.make_async_copy(low.at[rows], tab_low, sems.at[1]),
    ]
    for load in loads:
        load.start()
    per_block = cols.shape[1]
    points = cols.shape[0] * per_block
    for j in range(points):
        col = cols[j // per_block, j % per_block]
        for s in range(shots):
            row = traces[s, pl.ds(col, 1), :]
            picked[s * points + j : s * points + j + 1, :] = row * live[s, col].astype(jnp.float32)
    for load in loads:
        load.wait()
    left_high, left_low = split_two(picked[...])
    part[...] = (
        dot_nn(left_high, tab_high[...]) + dot_nn(left_low, tab_high[...]) + dot_nn(left_high, tab_low[...])
    )
    lines, lanes = outs[0].shape
    rows = shots * points
    for k, out in enumerate(outs):
        out[:rows] = part[:, pl.ds(pl.multiple_of((z ^ k) * lanes, lanes), lanes)]
        out[rows:] = jnp.zeros((lines - rows, lanes), jnp.float32)
    own = filters.shape[0]
    outs[0][rows : rows + own, : filters.shape[1]] = filters[...]
    half = bins.shape[1] // 2
    other = 1 - lax.axis_index("shot") % 2
    there = bins[:, pl.ds(pl.multiple_of(other * half, half), half)]
    outs[0][rows + own : rows + own + shots, :half] = there.astype(jnp.float32)


def sibling_kernel(surface, out, sem):
    half = out.shape[1]
    core = lax.axis_index("shot") % 2
    copy = pltpu.make_async_copy(surface.at[:, pl.ds(pl.multiple_of((1 - core) * half, 8), half)], out, sem)
    copy.start()
    copy.wait()


def pieces_kernel(step, owners, surface, sibling, *outs):
    d = lax.axis_index("shot")
    chip, core = d // 2, d % 2
    half = sibling.shape[1]
    chunk = outs[0].shape[1]
    first_owner, other_owner = owners[step], owners[1 - step]
    owner_core = jnp.where(first_owner // 2 == chip, first_owner % 2, other_owner % 2)
    for source, base, wanted in ((surface, core * half, owner_core == core), (sibling, 0, owner_core != core)):

        @pl.when(wanted)
        def _(source=source, base=base):
            for k, out in enumerate(outs):
                first = base + (chip ^ (k + 1)) * chunk
                out[...] = source[:, pl.ds(pl.multiple_of(first, 8), chunk), :]


def predict(chosen, spectra, real_side, imag_side, outs):
    points = STEPS * POINTS_BLK
    rows = real_side.shape[1]
    shots = rows // points
    size, lanes = chosen.shape[2:]
    lane = lax.broadcasted_iota(jnp.int32, (rows, lanes), 1)
    for q in outs:
        for c in range(2):
            value = spectra[c][q, :rows, :]
            turned = pltpu.roll(value, lanes // 2, 1)
            real_side[2 * q + c] = jnp.where(lane < lanes // 2, value, turned)
            imag_side[2 * q + c] = jnp.where(lane < lanes // 2, turned, -value)
    yield
    for q, out in outs.items():

        @pl.loop(0, 2)
        def _(rel, q=q, out=out):
            at = 2 * q + rel
            first_sum = [jnp.zeros((size, lanes), jnp.float32)] * shots
            second_sum = [jnp.zeros((size, lanes), jnp.float32)] * shots
            for j in range(points):
                block = chosen[j // POINTS_BLK, j % POINTS_BLK]
                for s in range(shots):
                    row = s * points + j
                    first_sum[s] = first_sum[s] + real_side[at, row : row + 1, :] * block
                    second_sum[s] = second_sum[s] + imag_side[at, row : row + 1, :] * block
            for s in range(shots):
                out[rel * shots + s] = first_sum[s] + pltpu.roll(second_sum[s], lanes // 2, 1)

        yield


def others_kernel(extra, owners, surface, sibling, *rest):
    sent, spectra, outs, kept = rest[:-13], rest[-13:-11], rest[-11:-8], rest[-8]
    results, (chosen, real_side, imag_side, sems) = rest[-7:-4], rest[-4:]
    d = lax.axis_index("shot")
    chip, core = d // 2, d % 2
    half = sibling.shape[1]
    chunk = chosen.shape[2]
    for b in range(STEPS):
        owner = owners[b]
        step, owner_core = (owner // 2) ^ chip, owner % 2

        @pl.when((step == 0) & (owner_core == core))
        def _():
            rows = pl.ds(pl.multiple_of(core * half + chip * chunk, 8), chunk)
            pltpu.make_async_copy(surface.at[:, rows], chosen.at[b], sems.at[b]).start()

        @pl.when((step == 0) & (owner_core != core))
        def _():
            rows = pl.ds(pl.multiple_of(chip * chunk, 8), chunk)
            pltpu.make_async_copy(sibling.at[:, rows], chosen.at[b], sems.at[b]).start()

        for k in range(3):

            @pl.when(step == k + 1)
            def _():
                source = sent[3 + k] if extra and b == 1 else sent[k]
                pltpu.make_async_copy(source, chosen.at[b], sems.at[b]).start()

    steps = predict(chosen, spectra, real_side, imag_side, dict(zip(FAR_FIRST, [results[q - 1] for q in FAR_FIRST])))
    next(steps)
    for b in range(STEPS):
        pltpu.make_async_copy(sibling.at[:, pl.ds(0, chunk)], chosen.at[b], sems.at[b]).wait()
    copies = [pltpu.make_async_copy(chosen, kept, sems.at[STEPS])]
    copies[0].start()
    for q, _ in zip(FAR_FIRST, steps):
        copies.append(pltpu.make_async_copy(results[q - 1], outs[q - 1], sems.at[STEPS + q]))
        copies[-1].start()
    for copy in copies:
        copy.wait()


def own_kernel(chosen, own, other, out, real_side, imag_side):
    for _ in predict(chosen, (own, other), real_side, imag_side, {0: out}):
        pass


def arrange_kernel(order, *rest):
    pieces, out = rest[:-1], rest[-1]
    chip = lax.axis_index("shot") // 2
    for q, piece in zip(order, pieces):
        out[:, chip ^ q] = piece[...]


def slots_kernel(most, bins, live, places):
    total = bins.shape[1]
    bins_total = places.shape[0] // most
    member = (lax.broadcasted_iota(jnp.int32, (bins_total, total), 0) == bins[...]).astype(jnp.float32)
    before = lax.broadcasted_iota(jnp.int32, (total, total), 0) < lax.broadcasted_iota(jnp.int32, (total, total), 1)
    counts = dot_nn(member.astype(jnp.bfloat16), before.astype(jnp.float32).astype(jnp.bfloat16))
    rank = jnp.sum(counts * member, axis=0, keepdims=True)
    slot = bins[...] * most + rank.astype(jnp.int32)
    slot = jnp.where(live[...] != 0, slot, -1)
    at = lax.broadcasted_iota(jnp.int32, places.shape, 0)
    places[...] = (at == slot).astype(jnp.float32).astype(jnp.bfloat16)


def response_kernel(own_bins, bins, waves, picks, *rest):
    spectra, (taps, same_side, cross_side, filters) = rest[:2], rest[2:]
    d = lax.axis_index("shot")
    z = lax.axis_index("freq")
    lines = spectra[0].shape[1]
    for q in range(4):
        for c in range(2):
            filters[d ^ (2 * q + c)] = spectra[c][q, lines - 8 :, :]
    devices, padded, lanes = filters.shape
    shots, receivers = bins.shape
    half = receivers // 2
    here = bins[:, pl.ds(pl.multiple_of(d % 2 * half, half), half)]
    first = lines - 8 + own_bins
    there = spectra[1][0, first : first + shots, :half].astype(jnp.int32)
    lists = [some[s : s + 1] for some in (here, there) for s in range(shots)]
    bin_row = jnp.concatenate(lists, axis=1)
    shape = (devices * padded, shots * receivers)
    row = lax.broadcasted_iota(jnp.int32, shape, 0)
    bin_of_row = jnp.where(row % padded < own_bins, row // padded * own_bins + row % padded, -1)
    member = (bin_of_row == bin_row).astype(jnp.float32).astype(jnp.bfloat16)

    def per_trace(table):
        high, low = split_two(table)
        dims = (((0,), (0,)), ((), ()))
        return lax.dot_general(member, high, dims, preferred_element_type=jnp.float32) + lax.dot_general(
            member, low, dims, preferred_element_type=jnp.float32
        )

    table = filters[...].reshape(devices * padded, lanes)
    side = picks[(z + 1) // 4]
    taps[...] = per_trace(jnp.dot(table, side, precision=FULL_PRECISION, preferred_element_type=jnp.float32))
    lane = lax.broadcasted_iota(jnp.int32, (devices * padded, lanes), 1)
    for slot in range(4):
        cols = pl.ds(pl.multiple_of((z ^ slot) * lanes, lanes), lanes)
        answer = jnp.dot(table, waves[:, cols], precision=FULL_PRECISION, preferred_element_type=jnp.float32)
        turned = pltpu.roll(answer, lanes // 2, 1)
        into = slice(slot * lanes, (slot + 1) * lanes)
        same_side[:, into] = per_trace(jnp.where(lane < lanes // 2, answer, turned))
        cross_side[:, into] = per_trace(jnp.where(lane < lanes // 2, -turned, answer))


def clean_kernel(keep, got, traces, places, *rest):
    outs, (high, low, packed) = rest[:-3], rest[-3:]
    d = lax.axis_index("shot")
    core = d % 2
    shots, receivers, _ = traces.shape
    half = keep.shape[1]
    for source, side in ((keep, core), (got, 1 - core)):
        for s in range(shots):
            first = pl.multiple_of(side * half, half)
            flat = pl.ds(pl.multiple_of(s * receivers + first, half), half)
            clean_high, clean_low = split_two(traces[s, pl.ds(first, half), :] - source[s])
            high[flat, :] = clean_high
            low[flat, :] = clean_low
    packed[...] = dot_nn(places[...], high[...]) + dot_nn(places[...], low[...])
    count = outs[0].shape[0]
    for k, out in enumerate(outs):
        out[...] = packed[pl.ds(pl.multiple_of((d ^ k) * count, 8), count), :]


def transform(value, into_high, into_low):
    left_high, left_low = split_two(value)
    full = dot_nt(left_high, into_high[...]) + dot_nt(left_low, into_high[...]) + dot_nt(left_high, into_low[...])
    return full * (2.0 / NT)


def transform_band(value, into_high, into_low):
    left_high, left_low = split_two(value)
    both = jnp.concatenate([left_high, left_low], axis=1)
    twice = jnp.concatenate([into_high[...], into_high[...]], axis=1)
    return (dot_nt(both, twice) + dot_nt(left_high, into_low[...])) * (2.0 / NT)


def respond(value, same_side, cross_side):
    lanes = 2 * NF // 4
    bands = [value[:, i : i + lanes] for i in range(0, value.shape[1], lanes)]
    turned = jnp.concatenate([pltpu.roll(band, lanes // 2, 1) for band in bands], axis=1)
    return value * same_side + turned * cross_side


def wrapped_ends(beyond, end_sums, taps):
    beyond_high, beyond_low = split_two(beyond * taps[...])
    return dot_nn(beyond_high, end_sums[...]) + dot_nn(beyond_low, end_sums[...])


def inverse_kernel(high, low, end_high, end_low, sums, taps, same_side, cross_side, *rest):
    own, near, across, middle, out, gathered, tab_high, tab_low, tab_end_high, tab_end_low, end_sums, sems, tab_sems = rest
    z = lax.axis_index("freq")
    lanes = own.shape[3]
    quarter = tab_high.shape[0]
    at_end = (z == 0) | (z == 3)
    rows = pl.ds(pl.multiple_of(RIM + z * quarter, 16), quarter)
    end_size = RIM * RIM
    end_rows = pl.ds(pl.multiple_of((z + 1) // 4 * end_size, 16), end_size)
    loads = []
    end_loads = [pltpu.make_async_copy(sums.at[end_rows], end_sums, tab_sems.at[16])]
    for slot in range(4):
        cols = pl.ds(pl.multiple_of((z ^ slot) * lanes, lanes), lanes)
        into = pl.ds(slot * lanes, lanes)
        for i, (table, scratch) in enumerate(((high, tab_high), (low, tab_low))):
            loads.append(pltpu.make_async_copy(table.at[rows, cols], scratch.at[:, into], tab_sems.at[4 * slot + i]))
        for i, (table, scratch) in enumerate(((end_high, tab_end_high), (end_low, tab_end_low))):
            copy = pltpu.make_async_copy(table.at[end_rows, cols], scratch.at[:, into], tab_sems.at[4 * slot + 2 + i])
            end_loads.append(copy)
    for load in loads:
        load.start()

    @pl.when(at_end)
    def _():
        for load in end_loads:
            load.start()

    def fetch(source, slot):
        return pltpu.make_async_copy(source, gathered.at[:, :, :, pl.ds(slot * lanes, lanes)], sems.at[slot])

    straight = [fetch(band, slot) for slot, band in enumerate((own, near, across))]
    for copy in straight:
        copy.start()

    @pl.when(at_end)
    def _():
        gathered[:, :, :, 3 * lanes :] = jnp.zeros(own.shape, jnp.float32)

    @pl.when(jnp.logical_not(at_end))
    def _():
        fetch(middle, 3).start()
        fetch(middle, 3).wait()

    for copy in loads + straight:
        copy.wait()
    total = math.prod(own.shape[:3])
    value = gathered[...].reshape(total, 4 * lanes)
    out[...] = transform(respond(value, same_side[...], cross_side[...]), tab_high, tab_low)

    @pl.when(at_end)
    def _():
        for load in end_loads:
            load.wait()
        beyond = transform(gathered[...].reshape(total, 4 * lanes), tab_end_high, tab_end_low)
        wrapped = wrapped_ends(beyond, end_sums, taps)
        cols = pl.ds(pl.multiple_of(jnp.where(z == 0, 0, quarter - lanes), lanes), lanes)
        out[:, cols] = out[:, cols] - wrapped


def forward_kernel(high, low, end_high, end_low, sums, taps, same_side, cross_side, partial, forward, *rest):
    keep, send, tab_high, tab_low, tab_end_high, tab_end_low, end_sums, result, sems = rest
    z = lax.axis_index("freq")
    lanes = forward.shape[3]
    total, quarter = partial.shape
    at_end = (z == 0) | (z == 3)

    @pl.when(at_end)
    def _():
        rows = pl.ds(pl.multiple_of(RIM + z * quarter, 16), quarter)
        end_size = RIM * RIM
        end_rows = pl.ds(pl.multiple_of((z + 1) // 4 * end_size, 16), end_size)
        cols = pl.ds(pl.multiple_of((3 - z) * lanes, lanes), lanes)
        loads = [
            pltpu.make_async_copy(high.at[rows, cols], tab_high, sems.at[0]),
            pltpu.make_async_copy(low.at[rows, cols], tab_low, sems.at[1]),
            pltpu.make_async_copy(end_high.at[end_rows, cols], tab_end_high, sems.at[2]),
            pltpu.make_async_copy(end_low.at[end_rows, cols], tab_end_low, sems.at[3]),
            pltpu.make_async_copy(sums.at[end_rows], end_sums, sems.at[4]),
        ]
        run_all(loads)
        some = slice(3 * lanes, 4 * lanes)
        value = forward[...].reshape(total, lanes)
        answer = respond(value, same_side[:, some], cross_side[:, some])
        result[...] = partial[...] + transform_band(answer, tab_high, tab_low)
        wrapped = wrapped_ends(transform_band(value, tab_end_high, tab_end_low), end_sums, taps)
        at = pl.ds(pl.multiple_of(jnp.where(z == 0, 0, quarter - lanes), lanes), lanes)
        result[:, at] = result[:, at] - wrapped
        keep[...] = result[: total // 2].reshape(keep.shape)
        send[...] = result[total // 2 :].reshape(send.shape)

    @pl.when(jnp.logical_not(at_end))
    def _():
        keep[...] = partial[: total // 2].reshape(keep.shape)
        send[...] = partial[total // 2 :].reshape(send.shape)


def unpack_kernel(most, order, *rest):
    slots, out = dict(zip(order, rest[:-1])), rest[-1]
    d = lax.axis_index("shot")
    chip, core = d // 2, d % 2
    for q in range(len(slots) // 2):
        own, other = slots[2 * q][...], slots[2 * q + 1][...]
        first, second = jnp.where(core == 0, own, other), jnp.where(core == 0, other, own)
        rows = pl.ds(pl.multiple_of((chip ^ q) * (2 * most), 8), 2 * most)
        for b in range(out.shape[0]):
            some = slice(b * most, (b + 1) * most)
            out[b, rows, :] = jnp.concatenate([first[some], second[some]], axis=0)


def f32(*shape):
    return jax.ShapeDtypeStruct(shape, jnp.float32)


def kernel_call(body, out_shape, in_specs, out_specs, scratch, flops=0, moved=0, vmem=None):
    return pl.pallas_call(
        body,
        name=getattr(body, "func", body).__name__,
        out_shape=out_shape,
        in_specs=in_specs,
        out_specs=out_specs,
        scratch_shapes=scratch,
        compiler_params=pltpu.CompilerParams(vmem_limit_bytes=vmem),
        cost_estimate=pl.CostEstimate(flops=flops, bytes_accessed=moved, transcendentals=0),
    )


def plane_device(traces, live_mask, offset_bin, surface, block_owner, point_column, filters):
    shots, receivers, quarter = traces.shape
    devices = lax.axis_size("shot")
    points = STEPS * POINTS_BLK
    rows = shots * receivers
    bins_total = filters.shape[0] * devices
    most = max(2, 3 * rows // (2 * bins_total))
    lanes = surface.shape[2]
    half = receivers // 2
    chunk = receivers // devices
    core = lax.axis_index("shot") & 1
    high, low = (jnp.asarray(x) for x in wave_constant(lax.axis_size("freq")))
    dma = pltpu.SemaphoreType.DMA

    to_sibling = kernel_call(
        sibling_kernel, f32(POINTS_BLK, half, lanes), [ANY], VMEM, [dma], moved=2 << 20, vmem=8 << 20
    )(surface)
    sibling = swap(to_sibling, "shot", devices, 1)

    bins = offset_bin.reshape(shots, receivers)
    bands = kernel_call(
        spectra_kernel,
        [f32(shots * points + 8, lanes)] * 4,
        [SMEM, SMEM, VMEM, VMEM, VMEM, ANY, ANY],
        [VMEM] * 4,
        [
            pltpu.VMEM((shots * points, quarter), jnp.float32),
            pltpu.VMEM((quarter, 2 * NF), jnp.bfloat16),
            pltpu.VMEM((quarter, 2 * NF), jnp.bfloat16),
            pltpu.VMEM((shots * points, 2 * NF), jnp.float32),
            dma((2,)),
        ],
        moved=1 << 21,
        vmem=16 << 20,
    )(point_column, live_mask, traces, bins, filters, high, low)
    def scatter(step):
        pieces = kernel_call(
            functools.partial(pieces_kernel, step),
            [f32(POINTS_BLK, chunk, lanes)] * 3,
            [SMEM, VMEM, VMEM],
            [VMEM] * 3,
            [],
            moved=4 << 20,
            vmem=24 << 20,
        )(block_owner, surface, sibling)
        return [swap(piece, "shot", devices, 2 * (k + 1)) for k, piece in enumerate(pieces)]

    sides = [pltpu.VMEM((8, shots * points, lanes), jnp.float32)] * 2
    cost = shots * chunk * points * lanes * 8

    def others(*sent):
        return kernel_call(
            functools.partial(others_kernel, len(sent) > 3),
            [f32(2 * shots, chunk, lanes)] * 3 + [f32(STEPS, POINTS_BLK, chunk, lanes)],
            [SMEM] + [ANY] * (2 + len(sent)) + [VMEM] * 2,
            [ANY] * 4,
            [pltpu.VMEM((2 * shots, chunk, lanes), jnp.float32)] * 3
            + [pltpu.VMEM((STEPS, POINTS_BLK, chunk, lanes), jnp.float32)]
            + sides
            + [dma((STEPS + 4,))],
            flops=3 * cost,
            moved=1 << 20,
            vmem=16 << 20,
        )(block_owner, surface, sibling, *sent, *every)

    sent = scatter(0)

    spectra = bands[0]
    for k in (3, 2, 1):
        spectra = spectra + swap(bands[k], "freq", 4, k)
    far, second, first = [swap(spectra, "shot", devices, 2 * q) for q in (3, 2, 1)]
    every = jnp.stack([spectra, first, second, far])
    sent[2:], every = lax.optimization_barrier((sent[2:], every))
    every = [every, swap(every, "shot", devices, 1)]

    places = kernel_call(
        functools.partial(slots_kernel, most),
        jax.ShapeDtypeStruct((bins_total * most, rows), jnp.bfloat16),
        [VMEM] * 2,
        VMEM,
        [],
        flops=rows * rows * 100,
        moved=1 << 21,
        vmem=24 << 20,
    )(offset_bin.reshape(1, rows), live_mask.reshape(1, rows))

    waves = jnp.asarray(tap_constant(lax.axis_size("freq"), lanes))
    end_high, end_low, picks, sums = (jnp.asarray(x) for x in end_constants(lax.axis_size("freq"), lanes))
    taps, same_side, cross_side = kernel_call(
        functools.partial(response_kernel, filters.shape[0]),
        [f32(rows, RIM * RIM), f32(rows, 4 * lanes), f32(rows, 4 * lanes)],
        [VMEM] * 5,
        [VMEM] * 3,
        [pltpu.VMEM((devices, 8, lanes), jnp.float32)],
        flops=rows * 64 * 4 * 1152,
        moved=1 << 22,
        vmem=24 << 20,
    )(bins, waves, picks, *every)

    both = (block_owner[0] ^ block_owner[1]) == 1
    sent, every = lax.optimization_barrier((sent, every))
    *outs, chosen = lax.cond(both, lambda *sent: others(*sent, *scatter(1)), others, *sent)
    turned = {q: swap(outs[q - 1], "shot", devices, 2 * q) for q in FAR_FIRST}
    own = kernel_call(
        own_kernel,
        f32(2 * shots, chunk, lanes),
        [VMEM] * 3,
        VMEM,
        sides,
        flops=cost,
        moved=1 << 20,
        vmem=16 << 20,
    )(chosen, *every)
    own = kernel_call(
        functools.partial(arrange_kernel, FAR_FIRST + (0,)),
        f32(2 * shots, 4, chunk, lanes),
        [VMEM] * 4,
        VMEM,
        [],
        moved=1 << 19,
        vmem=8 << 20,
    )(*[turned[q] for q in FAR_FIRST], own)
    across = swap(own, "freq", 4, 2)
    near = swap(own, "freq", 4, 1)
    middle = lax.ppermute(own, "freq", [(1, 2), (2, 1)])
    forward = lax.ppermute(across, "freq", [(2, 3), (1, 0)])

    tables = (high, low, end_high, end_low, sums, taps, same_side, cross_side)
    bf16 = functools.partial(pltpu.VMEM, dtype=jnp.bfloat16)
    partial = kernel_call(
        inverse_kernel,
        f32(rows, quarter),
        [ANY] * 5 + [VMEM] * 3 + [ANY] * 4,
        VMEM,
        [
            pltpu.VMEM((2 * shots, 4, chunk, 4 * lanes), jnp.float32),
            bf16((quarter, 4 * lanes)),
            bf16((quarter, 4 * lanes)),
            bf16((RIM * RIM, 4 * lanes)),
            bf16((RIM * RIM, 4 * lanes)),
            bf16((RIM * RIM, lanes)),
            dma((4,)),
            dma((17,)),
        ],
        flops=6 * rows * 4 * lanes * quarter,
        moved=4 << 20,
        vmem=32 << 20,
    )(*tables, own, near, across, middle)
    keep, send = kernel_call(
        forward_kernel,
        [f32(shots, half, quarter)] * 2,
        [ANY] * 5 + [VMEM] * 5,
        [VMEM] * 2,
        [
            bf16((quarter, lanes)),
            bf16((quarter, lanes)),
            bf16((RIM * RIM, lanes)),
            bf16((RIM * RIM, lanes)),
            bf16((RIM * RIM, lanes)),
            pltpu.VMEM((rows, quarter), jnp.float32),
            dma((5,)),
        ],
        flops=6 * rows * lanes * quarter,
        moved=2 << 20,
        vmem=32 << 20,
    )(*tables, partial, forward)
    got = swap(send, "shot", devices, 1)

    bin_slots = filters.shape[0] * most
    slots = kernel_call(
        clean_kernel,
        [f32(bin_slots, quarter)] * devices,
        [VMEM] * 4,
        [VMEM] * devices,
        [pltpu.VMEM((rows, quarter), jnp.bfloat16)] * 2 + [pltpu.VMEM((devices * bin_slots, quarter), jnp.float32)],
        flops=4 * rows * bins_total * most * quarter,
        moved=6 << 20,
        vmem=32 << 20,
    )(keep, got, traces, places)
    order = [2 * q + c for q in FAR_FIRST for c in range(2)] + [1, 0]
    slots = [swap(slots[k], "shot", devices, k) if k else slots[k] for k in order]
    return kernel_call(
        functools.partial(unpack_kernel, most, order),
        f32(filters.shape[0], devices * most, quarter),
        [VMEM] * devices,
        VMEM,
        [],
        moved=3 << 20,
        vmem=16 << 20,
    )(*slots)


def with_halo(cells, sides, width):
    for axis, dim in sides:
        count = lax.axis_size(axis)
        ends = count - 1
        head = lax.slice_in_dim(cells, 0, width, axis=dim)
        tail = lax.slice_in_dim(cells, cells.shape[dim] - width, cells.shape[dim], axis=dim)
        cells = jnp.concatenate(
            [
                lax.ppermute(tail, axis, [(i, (i + 1) % count) for i in range(ends)]),
                cells,
                lax.ppermute(head, axis, [((i + 1) % count, i) for i in range(ends)]),
            ],
            axis=dim,
        )
    return cells


def broadcast(value, axis, source):
    kept = jnp.where(lax.axis_index(axis) == source, value, 0).astype(value.dtype)
    return lax.psum(kept, axis)


def wave_table(time_ids, comp_ids, band_width, period):
    mode_ids = comp_ids // (2 * band_width) * band_width + comp_ids % band_width
    phase_ids = (mode_ids[None, :] + 1) * time_ids[:, None] % period
    angles = phase_ids.astype(jnp.float32) * (2.0 * math.pi / period)
    real_part = comp_ids % (2 * band_width) < band_width
    return jnp.where(real_part[None, :], jnp.cos(angles), -jnp.sin(angles))


def cross_mix(left_side, right_side):
    return jnp.einsum("bsj,jrb->srb", left_side, right_side, precision=FULL_PRECISION)


def shifted_sum(widened, tap_table, out_width):
    half_span = (tap_table.shape[-1] - 1) // 2
    summed = jnp.zeros(widened.shape[:-1] + (out_width,), jnp.float32)
    for tap_index in range(tap_table.shape[-1]):
        offset_start = 2 * half_span - tap_index
        window = lax.slice_in_dim(
            widened, offset_start, offset_start + out_width, axis=widened.ndim - 1
        )
        summed = summed + tap_table[..., tap_index : tap_index + 1] * window
    return summed


def widened_rims(values):
    half_span = (TAPS - 1) // 2
    return with_halo(values, (("freq", 2),), half_span)


def pack_rows(values, slot_ids, total_slots):
    return jnp.zeros((total_slots, values.shape[-1]), jnp.float32).at[slot_ids].set(values)


def any_device(traces, live_mask, offset_bin, surface, block_owner, point_column, filters):
    shots_here, receivers, quarter = traces.shape
    freq_count = lax.axis_size("freq")
    shot_count = lax.axis_size("shot")
    band_width = NF // freq_count
    rows_here = shots_here * receivers
    bins_total = filters.shape[0] * shot_count
    most_slots = max(2, 3 * rows_here // (2 * bins_total))
    total_slots = bins_total * most_slots
    live_rows = live_mask.astype(jnp.float32)[:, :, None]
    live_traces = traces * live_rows
    columns = point_column.reshape(-1)
    picked = jnp.take(live_traces, columns, axis=1).reshape(shots_here * columns.shape[0], quarter)
    freq_index = lax.axis_index("freq")
    time_ids = freq_index * quarter + jnp.arange(quarter)
    band_ids = freq_index * 2 * band_width + jnp.arange(2 * band_width)
    wave_rows = wave_table(
        time_ids, jnp.arange(2 * band_width * lax.axis_size("freq")), band_width, NT
    )
    spectra = lax.psum_scatter(
        lax.dot_general(wave_rows, picked, (((0,), (1,)), ((), ())), precision=FULL_PRECISION),
        "freq",
        scatter_dimension=0,
        tiled=True,
    )
    spectra = spectra.reshape(2 * band_width, shots_here, columns.shape[0])
    real_sum = jnp.zeros((shots_here, receivers, band_width), jnp.float32)
    imag_sum = jnp.zeros((shots_here, receivers, band_width), jnp.float32)
    for step_index in range(STEPS):
        surface_part = broadcast(surface, "shot", block_owner[step_index])
        point_spectra = spectra[:, :, step_index * POINTS_BLK : (step_index + 1) * POINTS_BLK]
        data_real = point_spectra[:band_width]
        data_imag = point_spectra[band_width:]
        surf_real = surface_part[:, :, :band_width]
        surf_imag = surface_part[:, :, band_width:]
        real_sum = real_sum + (cross_mix(data_real, surf_real) - cross_mix(data_imag, surf_imag))
        imag_sum = imag_sum + (cross_mix(data_real, surf_imag) + cross_mix(data_imag, surf_real))
    prediction = jnp.concatenate([real_sum, imag_sum], axis=2).reshape(rows_here, 2 * band_width)
    inverse = wave_table(jnp.arange(NT), band_ids, band_width, NT).T * (2.0 / NT)
    partial_value = jnp.dot(prediction, inverse, precision=FULL_PRECISION)
    multiples = lax.psum_scatter(partial_value, "freq", scatter_dimension=1, tiled=True)
    multiples = multiples.reshape(shots_here, receivers, quarter) * live_rows
    bins_flat = offset_bin.reshape(rows_here)
    order_ids = jnp.arange(rows_here)
    earlier = (bins_flat[:, None] == bins_flat[None, :]) & (order_ids[None, :] < order_ids[:, None])
    rank_ids = jnp.sum(earlier.astype(jnp.int32), axis=1)
    slot_ids = bins_flat * most_slots + rank_ids
    every_filter = lax.all_gather(filters, "shot", axis=0, tiled=True)
    trace_taps = jnp.take(every_filter, bins_flat, axis=0).reshape(
        shots_here, receivers, every_filter.shape[1]
    )
    widened = widened_rims(multiples)
    cleaned = live_traces - shifted_sum(widened, trace_taps, quarter)
    cleaned_slots = pack_rows(cleaned.reshape(rows_here, quarter), slot_ids, total_slots)
    cleaned_slots = cleaned_slots.reshape(bins_total, most_slots, quarter)
    return lax.all_to_all(cleaned_slots, "shot", split_axis=0, concat_axis=1, tiled=True)


def on_device(traces, live_mask, offset_bin, surface, block_owner, point_column, filters):
    devices = lax.axis_size("shot")
    in_plane = devices == 8 and lax.axis_size("freq") == 4
    whole_tiles = traces.shape[1] % (8 * devices) == 0 and filters.shape[0] + traces.shape[0] <= 8
    plan = plane_device if in_plane and whole_tiles else any_device
    return plan(traces, live_mask, offset_bin, surface, block_owner, point_column, filters)


def solution(mesh):
    return jax.shard_map(
        on_device,
        mesh=mesh,
        in_specs=(
            P("shot", None, "freq"),
            P("shot", None),
            P("shot", None, None),
            P("shot", None, "freq"),
            P(),
            P(),
            P("shot", None),
        ),
        out_specs=P("shot", None, "freq"),
        check_vma=False,
    )
```

```python
import functools
import math

import jax
import jax.numpy as jnp
import numpy as np
from jax import lax
from jax.experimental import pallas as pl
from jax.experimental.pallas import tpu as pltpu
from jax.sharding import PartitionSpec as P

NT = 1024
NF = 256
TAPS = 31
POINTS_BLK = 16
STEPS = 2
RIM = 16
FAR_FIRST = (3, 1, 2)
GATHERED = FAR_FIRST + (0,)

FULL_PRECISION = lax.Precision.HIGHEST
VMEM = pl.BlockSpec(memory_space=pltpu.VMEM)
SMEM = pl.BlockSpec(memory_space=pltpu.SMEM)
ANY = pl.BlockSpec(memory_space=pl.ANY)


def wave_constant(bands):
    width = NF // bands
    comps = np.arange(2 * NF)
    modes = comps // (2 * width) * width + comps % width
    phases = (modes[None, :] + 1) * np.arange(NT)[:, None] % NT
    angles = phases * (2.0 * math.pi / NT)
    table = np.where((comps % (2 * width) < width)[None, :], np.cos(angles), -np.sin(angles))
    table = np.pad(table, ((RIM, RIM), (0, 0))).astype(np.float32)
    high = table.astype(jnp.bfloat16)
    low = (table - high.astype(np.float32)).astype(jnp.bfloat16)
    return high, low


def tap_constant(bands, lanes):
    high, low = wave_constant(bands)
    table = high.astype(np.float32) + low.astype(np.float32)
    shifts = (np.arange(TAPS) - (TAPS - 1) // 2) % NT
    return np.pad(table[RIM + shifts], ((0, lanes - TAPS), (0, 0)))


def end_constants(bands, lanes):
    high, low = wave_constant(bands)
    k, t = np.divmod(np.arange(RIM * RIM), RIM)
    waves = [np.stack([part[NT + k], part[RIM + k]]).reshape(2 * RIM * RIM, -1) for part in (high, low)]
    half_span = (TAPS - 1) // 2
    picks = np.zeros((2, lanes, RIM * RIM), np.float32)
    sums = np.zeros((2, RIM * RIM, lanes), np.float32)
    for side, tap, lane in ((0, t + RIM - k + half_span, t), (1, t - 1 - k, lanes - RIM + t)):
        fits = (tap >= 0) & (tap < TAPS)
        picks[side, tap[fits], np.arange(RIM * RIM)[fits]] = 1
        sums[side, np.arange(RIM * RIM), lane] = 1
    return *waves, picks, sums.reshape(2 * RIM * RIM, lanes).astype(jnp.bfloat16)


def split_two(value):
    high = value.astype(jnp.bfloat16)
    return high, (value - high.astype(jnp.float32)).astype(jnp.bfloat16)


def dot_nn(left, right):
    return lax.dot_general(left, right, (((1,), (0,)), ((), ())), preferred_element_type=jnp.float32)


def dot_nt(left, right):
    return lax.dot_general(left, right, (((1,), (1,)), ((), ())), preferred_element_type=jnp.float32)


def run_all(copies):
    for copy in copies:
        copy.start()
    for copy in copies:
        copy.wait()


def swap(value, axis, count, bit):
    return lax.ppermute(value, axis, [(i, i ^ bit) for i in range(count)])


def spectra_kernel(cols, live, traces, bins, filters, high, low, *rest):
    outs, (picked, tab_high, tab_low, part, sems) = rest[:4], rest[4:]
    shots, _, quarter = traces.shape
    z = lax.axis_index("freq")
    rows = pl.ds(pl.multiple_of(RIM + z * quarter, 16), quarter)
    loads = [
        pltpu.make_async_copy(high.at[rows], tab_high, sems.at[0]),
        pltpu.make_async_copy(low.at[rows], tab_low, sems.at[1]),
    ]
    for load in loads:
        load.start()
    per_block = cols.shape[1]
    points = cols.shape[0] * per_block
    for j in range(points):
        col = cols[j // per_block, j % per_block]
        for s in range(shots):
            row = traces[s, pl.ds(col, 1), :]
            picked[s * points + j : s * points + j + 1, :] = row * live[s, col].astype(jnp.float32)
    for load in loads:
        load.wait()
    left_high, left_low = split_two(picked[...])
    part[...] = (
        dot_nn(left_high, tab_high[...]) + dot_nn(left_low, tab_high[...]) + dot_nn(left_high, tab_low[...])
    )
    lines, lanes = outs[0].shape
    rows = shots * points
    for k, out in enumerate(outs):
        out[:rows] = part[:, pl.ds(pl.multiple_of((z ^ k) * lanes, lanes), lanes)]
        out[rows:] = jnp.zeros((lines - rows, lanes), jnp.float32)
    own = filters.shape[0]
    outs[0][rows : rows + own, : filters.shape[1]] = filters[...]
    half = bins.shape[1] // 2
    other = 1 - lax.axis_index("shot") % 2
    there = bins[:, pl.ds(pl.multiple_of(other * half, half), half)]
    outs[0][rows + own : rows + own + shots, :half] = there.astype(jnp.float32)


def sibling_kernel(surface, out, sem):
    half = out.shape[1]
    core = lax.axis_index("shot") % 2
    copy = pltpu.make_async_copy(surface.at[:, pl.ds(pl.multiple_of((1 - core) * half, 8), half)], out, sem)
    copy.start()
    copy.wait()


def pieces_kernel(step, owners, surface, sibling, *outs):
    d = lax.axis_index("shot")
    chip, core = d // 2, d % 2
    half = sibling.shape[1]
    chunk = outs[0].shape[1]
    first_owner, other_owner = owners[step], owners[1 - step]
    owner_core = jnp.where(first_owner // 2 == chip, first_owner % 2, other_owner % 2)
    for source, base, wanted in ((surface, core * half, owner_core == core), (sibling, 0, owner_core != core)):

        @pl.when(wanted)
        def _(source=source, base=base):
            for k, out in enumerate(outs):
                first = base + (chip ^ (k + 1)) * chunk
                out[...] = source[:, pl.ds(pl.multiple_of(first, 8), chunk), :]


def predict(chosen, spectra, real_side, imag_side, outs):
    points = STEPS * POINTS_BLK
    rows = real_side.shape[1]
    shots = rows // points
    size, lanes = chosen.shape[2:]
    lane = lax.broadcasted_iota(jnp.int32, (rows, lanes), 1)
    for q in outs:
        for c in range(2):
            value = spectra[c][GATHERED.index(q), :rows, :]
            turned = pltpu.roll(value, lanes // 2, 1)
            real_side[2 * q + c] = jnp.where(lane < lanes // 2, value, turned)
            imag_side[2 * q + c] = jnp.where(lane < lanes // 2, turned, -value)
    yield
    for q, out in outs.items():

        @pl.loop(0, 2)
        def _(rel, q=q, out=out):
            at = 2 * q + rel
            first_sum = [jnp.zeros((size, lanes), jnp.float32)] * shots
            second_sum = [jnp.zeros((size, lanes), jnp.float32)] * shots
            for j in range(points):
                block = chosen[j // POINTS_BLK, j % POINTS_BLK]
                for s in range(shots):
                    row = s * points + j
                    first_sum[s] = first_sum[s] + real_side[at, row : row + 1, :] * block
                    second_sum[s] = second_sum[s] + imag_side[at, row : row + 1, :] * block
            for s in range(shots):
                out[rel * shots + s] = first_sum[s] + pltpu.roll(second_sum[s], lanes // 2, 1)

        yield


def others_kernel(extra, owners, surface, sibling, *rest):
    sent, spectra, outs, kept = rest[:-13], rest[-13:-11], rest[-11:-8], rest[-8]
    results, (chosen, real_side, imag_side, sems) = rest[-7:-4], rest[-4:]
    d = lax.axis_index("shot")
    chip, core = d // 2, d % 2
    half = sibling.shape[1]
    chunk = chosen.shape[2]
    for b in range(STEPS):
        owner = owners[b]
        step, owner_core = (owner // 2) ^ chip, owner % 2

        @pl.when((step == 0) & (owner_core == core))
        def _():
            rows = pl.ds(pl.multiple_of(core * half + chip * chunk, 8), chunk)
            pltpu.make_async_copy(surface.at[:, rows], chosen.at[b], sems.at[b]).start()

        @pl.when((step == 0) & (owner_core != core))
        def _():
            rows = pl.ds(pl.multiple_of(chip * chunk, 8), chunk)
            pltpu.make_async_copy(sibling.at[:, rows], chosen.at[b], sems.at[b]).start()

        for k in range(3):

            @pl.when(step == k + 1)
            def _():
                source = sent[3 + k] if extra and b == 1 else sent[k]
                pltpu.make_async_copy(source, chosen.at[b], sems.at[b]).start()

    steps = predict(chosen, spectra, real_side, imag_side, dict(zip(FAR_FIRST, [results[q - 1] for q in FAR_FIRST])))
    next(steps)
    for b in range(STEPS):
        pltpu.make_async_copy(sibling.at[:, pl.ds(0, chunk)], chosen.at[b], sems.at[b]).wait()
    copies = [pltpu.make_async_copy(chosen, kept, sems.at[STEPS])]
    copies[0].start()
    for q, _ in zip(FAR_FIRST, steps):
        copies.append(pltpu.make_async_copy(results[q - 1], outs[q - 1], sems.at[STEPS + q]))
        copies[-1].start()
    for copy in copies:
        copy.wait()


def own_kernel(chosen, own, other, out, real_side, imag_side):
    for _ in predict(chosen, (own, other), real_side, imag_side, {0: out}):
        pass


def arrange_kernel(order, *rest):
    pieces, out = rest[:-1], rest[-1]
    chip = lax.axis_index("shot") // 2
    for q, piece in zip(order, pieces):
        out[:, chip ^ q] = piece[...]


def slots_kernel(most, bins, live, places):
    total = bins.shape[1]
    bins_total = places.shape[0] // most
    member = (lax.broadcasted_iota(jnp.int32, (bins_total, total), 0) == bins[...]).astype(jnp.float32)
    before = lax.broadcasted_iota(jnp.int32, (total, total), 0) < lax.broadcasted_iota(jnp.int32, (total, total), 1)
    counts = dot_nn(member.astype(jnp.bfloat16), before.astype(jnp.float32).astype(jnp.bfloat16))
    rank = jnp.sum(counts * member, axis=0, keepdims=True)
    slot = bins[...] * most + rank.astype(jnp.int32)
    slot = jnp.where(live[...] != 0, slot, -1)
    at = lax.broadcasted_iota(jnp.int32, places.shape, 0)
    places[...] = (at == slot).astype(jnp.float32).astype(jnp.bfloat16)


def response_kernel(own_bins, bins, waves, picks, *rest):
    spectra, (taps, same_side, cross_side, filters) = rest[:2], rest[2:]
    d = lax.axis_index("shot")
    z = lax.axis_index("freq")
    lines = spectra[0].shape[1]
    for q in range(4):
        for c in range(2):
            filters[d ^ (2 * q + c)] = spectra[c][GATHERED.index(q), lines - 8 :, :]
    devices, padded, lanes = filters.shape
    shots, receivers = bins.shape
    half = receivers // 2
    here = bins[:, pl.ds(pl.multiple_of(d % 2 * half, half), half)]
    first = lines - 8 + own_bins
    there = spectra[1][GATHERED.index(0), first : first + shots, :half].astype(jnp.int32)
    lists = [some[s : s + 1] for some in (here, there) for s in range(shots)]
    bin_row = jnp.concatenate(lists, axis=1)
    shape = (devices * padded, shots * receivers)
    row = lax.broadcasted_iota(jnp.int32, shape, 0)
    bin_of_row = jnp.where(row % padded < own_bins, row // padded * own_bins + row % padded, -1)
    member = (bin_of_row == bin_row).astype(jnp.float32).astype(jnp.bfloat16)

    def per_trace(table):
        high, low = split_two(table)
        dims = (((0,), (0,)), ((), ()))
        return lax.dot_general(member, high, dims, preferred_element_type=jnp.float32) + lax.dot_general(
            member, low, dims, preferred_element_type=jnp.float32
        )

    table = filters[...].reshape(devices * padded, lanes)
    side = picks[(z + 1) // 4]
    taps[...] = per_trace(jnp.dot(table, side, precision=FULL_PRECISION, preferred_element_type=jnp.float32))
    lane = lax.broadcasted_iota(jnp.int32, (devices * padded, lanes), 1)
    for slot in range(4):
        cols = pl.ds(pl.multiple_of((z ^ slot) * lanes, lanes), lanes)
        answer = jnp.dot(table, waves[:, cols], precision=FULL_PRECISION, preferred_element_type=jnp.float32)
        turned = pltpu.roll(answer, lanes // 2, 1)
        into = slice(slot * lanes, (slot + 1) * lanes)
        same_side[:, into] = per_trace(jnp.where(lane < lanes // 2, answer, turned))
        cross_side[:, into] = per_trace(jnp.where(lane < lanes // 2, -turned, answer))


def clean_kernel(keep, got, traces, places, *rest):
    outs, (high, low, packed) = rest[:-3], rest[-3:]
    d = lax.axis_index("shot")
    core = d % 2
    shots, receivers, _ = traces.shape
    half = keep.shape[1]
    for source, side in ((keep, core), (got, 1 - core)):
        for s in range(shots):
            first = pl.multiple_of(side * half, half)
            flat = pl.ds(pl.multiple_of(s * receivers + first, half), half)
            clean_high, clean_low = split_two(traces[s, pl.ds(first, half), :] - source[s])
            high[flat, :] = clean_high
            low[flat, :] = clean_low
    packed[...] = dot_nn(places[...], high[...]) + dot_nn(places[...], low[...])
    count = outs[0].shape[0]
    for k, out in enumerate(outs):
        out[...] = packed[pl.ds(pl.multiple_of((d ^ k) * count, 8), count), :]


def transform(value, into_high, into_low):
    left_high, left_low = split_two(value)
    full = dot_nt(left_high, into_high[...]) + dot_nt(left_low, into_high[...]) + dot_nt(left_high, into_low[...])
    return full * (2.0 / NT)


def transform_band(value, into_high, into_low):
    left_high, left_low = split_two(value)
    both = jnp.concatenate([left_high, left_low], axis=1)
    twice = jnp.concatenate([into_high[...], into_high[...]], axis=1)
    return (dot_nt(both, twice) + dot_nt(left_high, into_low[...])) * (2.0 / NT)


def respond(value, same_side, cross_side):
    lanes = 2 * NF // 4
    bands = [value[:, i : i + lanes] for i in range(0, value.shape[1], lanes)]
    turned = jnp.concatenate([pltpu.roll(band, lanes // 2, 1) for band in bands], axis=1)
    return value * same_side + turned * cross_side


def wrapped_ends(beyond, end_sums, taps):
    beyond_high, beyond_low = split_two(beyond * taps[...])
    return dot_nn(beyond_high, end_sums[...]) + dot_nn(beyond_low, end_sums[...])


def inverse_kernel(high, low, end_high, end_low, sums, taps, same_side, cross_side, *rest):
    own, near, across, middle, out, gathered, tab_high, tab_low, tab_end_high, tab_end_low, end_sums, sems, tab_sems = rest
    z = lax.axis_index("freq")
    lanes = own.shape[3]
    quarter = tab_high.shape[0]
    at_end = (z == 0) | (z == 3)
    rows = pl.ds(pl.multiple_of(RIM + z * quarter, 16), quarter)
    end_size = RIM * RIM
    end_rows = pl.ds(pl.multiple_of((z + 1) // 4 * end_size, 16), end_size)
    loads = []
    end_loads = [pltpu.make_async_copy(sums.at[end_rows], end_sums, tab_sems.at[16])]
    for slot in range(4):
        cols = pl.ds(pl.multiple_of((z ^ slot) * lanes, lanes), lanes)
        into = pl.ds(slot * lanes, lanes)
        for i, (table, scratch) in enumerate(((high, tab_high), (low, tab_low))):
            loads.append(pltpu.make_async_copy(table.at[rows, cols], scratch.at[:, into], tab_sems.at[4 * slot + i]))
        for i, (table, scratch) in enumerate(((end_high, tab_end_high), (end_low, tab_end_low))):
            copy = pltpu.make_async_copy(table.at[end_rows, cols], scratch.at[:, into], tab_sems.at[4 * slot + 2 + i])
            end_loads.append(copy)
    for load in loads:
        load.start()

    @pl.when(at_end)
    def _():
        for load in end_loads:
            load.start()

    def fetch(source, slot):
        return pltpu.make_async_copy(source, gathered.at[:, :, :, pl.ds(slot * lanes, lanes)], sems.at[slot])

    straight = [fetch(band, slot) for slot, band in enumerate((own, near, across))]
    for copy in straight:
        copy.start()

    @pl.when(at_end)
    def _():
        gathered[:, :, :, 3 * lanes :] = jnp.zeros(own.shape, jnp.float32)

    @pl.when(jnp.logical_not(at_end))
    def _():
        fetch(middle, 3).start()
        fetch(middle, 3).wait()

    for copy in loads + straight:
        copy.wait()
    total = math.prod(own.shape[:3])
    value = gathered[...].reshape(total, 4 * lanes)
    out[...] = transform(respond(value, same_side[...], cross_side[...]), tab_high, tab_low)

    @pl.when(at_end)
    def _():
        for load in end_loads:
            load.wait()
        beyond = transform(gathered[...].reshape(total, 4 * lanes), tab_end_high, tab_end_low)
        wrapped = wrapped_ends(beyond, end_sums, taps)
        cols = pl.ds(pl.multiple_of(jnp.where(z == 0, 0, quarter - lanes), lanes), lanes)
        out[:, cols] = out[:, cols] - wrapped


def forward_kernel(high, low, end_high, end_low, sums, taps, same_side, cross_side, partial, forward, *rest):
    keep, send, tab_high, tab_low, tab_end_high, tab_end_low, end_sums, result, sems = rest
    z = lax.axis_index("freq")
    lanes = forward.shape[3]
    total, quarter = partial.shape
    at_end = (z == 0) | (z == 3)

    @pl.when(at_end)
    def _():
        rows = pl.ds(pl.multiple_of(RIM + z * quarter, 16), quarter)
        end_size = RIM * RIM
        end_rows = pl.ds(pl.multiple_of((z + 1) // 4 * end_size, 16), end_size)
        cols = pl.ds(pl.multiple_of((3 - z) * lanes, lanes), lanes)
        loads = [
            pltpu.make_async_copy(high.at[rows, cols], tab_high, sems.at[0]),
            pltpu.make_async_copy(low.at[rows, cols], tab_low, sems.at[1]),
            pltpu.make_async_copy(end_high.at[end_rows, cols], tab_end_high, sems.at[2]),
            pltpu.make_async_copy(end_low.at[end_rows, cols], tab_end_low, sems.at[3]),
            pltpu.make_async_copy(sums.at[end_rows], end_sums, sems.at[4]),
        ]
        run_all(loads)
        some = slice(3 * lanes, 4 * lanes)
        value = forward[...].reshape(total, lanes)
        answer = respond(value, same_side[:, some], cross_side[:, some])
        result[...] = partial[...] + transform_band(answer, tab_high, tab_low)
        wrapped = wrapped_ends(transform_band(value, tab_end_high, tab_end_low), end_sums, taps)
        at = pl.ds(pl.multiple_of(jnp.where(z == 0, 0, quarter - lanes), lanes), lanes)
        result[:, at] = result[:, at] - wrapped
        keep[...] = result[: total // 2].reshape(keep.shape)
        send[...] = result[total // 2 :].reshape(send.shape)

    @pl.when(jnp.logical_not(at_end))
    def _():
        keep[...] = partial[: total // 2].reshape(keep.shape)
        send[...] = partial[total // 2 :].reshape(send.shape)


def unpack_kernel(most, order, *rest):
    slots, out = dict(zip(order, rest[:-1])), rest[-1]
    d = lax.axis_index("shot")
    chip, core = d // 2, d % 2
    for q in range(len(slots) // 2):
        own, other = slots[2 * q][...], slots[2 * q + 1][...]
        first, second = jnp.where(core == 0, own, other), jnp.where(core == 0, other, own)
        rows = pl.ds(pl.multiple_of((chip ^ q) * (2 * most), 8), 2 * most)
        for b in range(out.shape[0]):
            some = slice(b * most, (b + 1) * most)
            out[b, rows, :] = jnp.concatenate([first[some], second[some]], axis=0)


def f32(*shape):
    return jax.ShapeDtypeStruct(shape, jnp.float32)


def kernel_call(body, out_shape, in_specs, out_specs, scratch, flops=0, moved=0, vmem=None):
    return pl.pallas_call(
        body,
        name=getattr(body, "func", body).__name__,
        out_shape=out_shape,
        in_specs=in_specs,
        out_specs=out_specs,
        scratch_shapes=scratch,
        compiler_params=pltpu.CompilerParams(vmem_limit_bytes=vmem),
        cost_estimate=pl.CostEstimate(flops=flops, bytes_accessed=moved, transcendentals=0),
    )


def plane_device(traces, live_mask, offset_bin, surface, block_owner, point_column, filters):
    shots, receivers, quarter = traces.shape
    devices = lax.axis_size("shot")
    points = STEPS * POINTS_BLK
    rows = shots * receivers
    bins_total = filters.shape[0] * devices
    most = max(2, 3 * rows // (2 * bins_total))
    lanes = surface.shape[2]
    half = receivers // 2
    chunk = receivers // devices
    core = lax.axis_index("shot") & 1
    high, low = (jnp.asarray(x) for x in wave_constant(lax.axis_size("freq")))
    dma = pltpu.SemaphoreType.DMA

    to_sibling = kernel_call(
        sibling_kernel, f32(POINTS_BLK, half, lanes), [ANY], VMEM, [dma], moved=2 << 20, vmem=8 << 20
    )(surface)
    sibling = swap(to_sibling, "shot", devices, 1)

    bins = offset_bin.reshape(shots, receivers)
    bands = kernel_call(
        spectra_kernel,
        [f32(shots * points + 8, lanes)] * 4,
        [SMEM, SMEM, VMEM, VMEM, VMEM, ANY, ANY],
        [VMEM] * 4,
        [
            pltpu.VMEM((shots * points, quarter), jnp.float32),
            pltpu.VMEM((quarter, 2 * NF), jnp.bfloat16),
            pltpu.VMEM((quarter, 2 * NF), jnp.bfloat16),
            pltpu.VMEM((shots * points, 2 * NF), jnp.float32),
            dma((2,)),
        ],
        moved=1 << 21,
        vmem=16 << 20,
    )(point_column, live_mask, traces, bins, filters, high, low)
    def scatter(step):
        pieces = kernel_call(
            functools.partial(pieces_kernel, step),
            [f32(POINTS_BLK, chunk, lanes)] * 3,
            [SMEM, VMEM, VMEM],
            [VMEM] * 3,
            [],
            moved=4 << 20,
            vmem=24 << 20,
        )(block_owner, surface, sibling)
        return [swap(piece, "shot", devices, 2 * (k + 1)) for k, piece in enumerate(pieces)]

    sides = [pltpu.VMEM((8, shots * points, lanes), jnp.float32)] * 2
    cost = shots * chunk * points * lanes * 8

    def others(*sent):
        return kernel_call(
            functools.partial(others_kernel, len(sent) > 3),
            [f32(2 * shots, chunk, lanes)] * 3 + [f32(STEPS, POINTS_BLK, chunk, lanes)],
            [SMEM] + [ANY] * (2 + len(sent)) + [VMEM] * 2,
            [ANY] * 4,
            [pltpu.VMEM((2 * shots, chunk, lanes), jnp.float32)] * 3
            + [pltpu.VMEM((STEPS, POINTS_BLK, chunk, lanes), jnp.float32)]
            + sides
            + [dma((STEPS + 4,))],
            flops=3 * cost,
            moved=1 << 20,
            vmem=16 << 20,
        )(block_owner, surface, sibling, *sent, *every)

    sent = scatter(0)

    spectra = bands[0]
    for k in (3, 2, 1):
        spectra = spectra + swap(bands[k], "freq", 4, k)
    far, second, first = [swap(spectra, "shot", devices, 2 * q) for q in (3, 2, 1)]
    every = jnp.stack([far, first, second, spectra])
    sent[2:], every = lax.optimization_barrier((sent[2:], every))
    every = [every, swap(every, "shot", devices, 1)]

    places = kernel_call(
        functools.partial(slots_kernel, most),
        jax.ShapeDtypeStruct((bins_total * most, rows), jnp.bfloat16),
        [VMEM] * 2,
        VMEM,
        [],
        flops=rows * rows * 100,
        moved=1 << 21,
        vmem=24 << 20,
    )(offset_bin.reshape(1, rows), live_mask.reshape(1, rows))

    waves = jnp.asarray(tap_constant(lax.axis_size("freq"), lanes))
    end_high, end_low, picks, sums = (jnp.asarray(x) for x in end_constants(lax.axis_size("freq"), lanes))
    taps, same_side, cross_side = kernel_call(
        functools.partial(response_kernel, filters.shape[0]),
        [f32(rows, RIM * RIM), f32(rows, 4 * lanes), f32(rows, 4 * lanes)],
        [VMEM] * 5,
        [VMEM] * 3,
        [pltpu.VMEM((devices, 8, lanes), jnp.float32)],
        flops=rows * 64 * 4 * 1152,
        moved=1 << 22,
        vmem=24 << 20,
    )(bins, waves, picks, *every)

    both = (block_owner[0] ^ block_owner[1]) == 1
    sent, every = lax.optimization_barrier((sent, every))
    *outs, chosen = lax.cond(both, lambda *sent: others(*sent, *scatter(1)), others, *sent)
    turned = {q: swap(outs[q - 1], "shot", devices, 2 * q) for q in FAR_FIRST}
    own = kernel_call(
        own_kernel,
        f32(2 * shots, chunk, lanes),
        [VMEM] * 3,
        VMEM,
        sides,
        flops=cost,
        moved=1 << 20,
        vmem=16 << 20,
    )(chosen, *every)
    own = kernel_call(
        functools.partial(arrange_kernel, FAR_FIRST + (0,)),
        f32(2 * shots, 4, chunk, lanes),
        [VMEM] * 4,
        VMEM,
        [],
        moved=1 << 19,
        vmem=8 << 20,
    )(*[turned[q] for q in FAR_FIRST], own)
    across = swap(own, "freq", 4, 2)
    near = swap(own, "freq", 4, 1)
    middle = lax.ppermute(own, "freq", [(1, 2), (2, 1)])
    forward = lax.ppermute(across, "freq", [(2, 3), (1, 0)])

    tables = (high, low, end_high, end_low, sums, taps, same_side, cross_side)
    bf16 = functools.partial(pltpu.VMEM, dtype=jnp.bfloat16)
    partial = kernel_call(
        inverse_kernel,
        f32(rows, quarter),
        [ANY] * 5 + [VMEM] * 3 + [ANY] * 4,
        VMEM,
        [
            pltpu.VMEM((2 * shots, 4, chunk, 4 * lanes), jnp.float32),
            bf16((quarter, 4 * lanes)),
            bf16((quarter, 4 * lanes)),
            bf16((RIM * RIM, 4 * lanes)),
            bf16((RIM * RIM, 4 * lanes)),
            bf16((RIM * RIM, lanes)),
            dma((4,)),
            dma((17,)),
        ],
        flops=6 * rows * 4 * lanes * quarter,
        moved=4 << 20,
        vmem=32 << 20,
    )(*tables, own, near, across, middle)
    keep, send = kernel_call(
        forward_kernel,
        [f32(shots, half, quarter)] * 2,
        [ANY] * 5 + [VMEM] * 5,
        [VMEM] * 2,
        [
            bf16((quarter, lanes)),
            bf16((quarter, lanes)),
            bf16((RIM * RIM, lanes)),
            bf16((RIM * RIM, lanes)),
            bf16((RIM * RIM, lanes)),
            pltpu.VMEM((rows, quarter), jnp.float32),
            dma((5,)),
        ],
        flops=6 * rows * lanes * quarter,
        moved=2 << 20,
        vmem=32 << 20,
    )(*tables, partial, forward)
    got = swap(send, "shot", devices, 1)

    bin_slots = filters.shape[0] * most
    slots = kernel_call(
        clean_kernel,
        [f32(bin_slots, quarter)] * devices,
        [VMEM] * 4,
        [VMEM] * devices,
        [pltpu.VMEM((rows, quarter), jnp.bfloat16)] * 2 + [pltpu.VMEM((devices * bin_slots, quarter), jnp.float32)],
        flops=4 * rows * bins_total * most * quarter,
        moved=6 << 20,
        vmem=32 << 20,
    )(keep, got, traces, places)
    order = [2 * q + c for q in FAR_FIRST for c in range(2)] + [1, 0]
    slots = [swap(slots[k], "shot", devices, k) if k else slots[k] for k in order]
    return kernel_call(
        functools.partial(unpack_kernel, most, order),
        f32(filters.shape[0], devices * most, quarter),
        [VMEM] * devices,
        VMEM,
        [],
        moved=3 << 20,
        vmem=16 << 20,
    )(*slots)


def with_halo(cells, sides, width):
    for axis, dim in sides:
        count = lax.axis_size(axis)
        ends = count - 1
        head = lax.slice_in_dim(cells, 0, width, axis=dim)
        tail = lax.slice_in_dim(cells, cells.shape[dim] - width, cells.shape[dim], axis=dim)
        cells = jnp.concatenate(
            [
                lax.ppermute(tail, axis, [(i, (i + 1) % count) for i in range(ends)]),
                cells,
                lax.ppermute(head, axis, [((i + 1) % count, i) for i in range(ends)]),
            ],
            axis=dim,
        )
    return cells


def broadcast(value, axis, source):
    kept = jnp.where(lax.axis_index(axis) == source, value, 0).astype(value.dtype)
    return lax.psum(kept, axis)


def wave_table(time_ids, comp_ids, band_width, period):
    mode_ids = comp_ids // (2 * band_width) * band_width + comp_ids % band_width
    phase_ids = (mode_ids[None, :] + 1) * time_ids[:, None] % period
    angles = phase_ids.astype(jnp.float32) * (2.0 * math.pi / period)
    real_part = comp_ids % (2 * band_width) < band_width
    return jnp.where(real_part[None, :], jnp.cos(angles), -jnp.sin(angles))


def cross_mix(left_side, right_side):
    return jnp.einsum("bsj,jrb->srb", left_side, right_side, precision=FULL_PRECISION)


def shifted_sum(widened, tap_table, out_width):
    half_span = (tap_table.shape[-1] - 1) // 2
    summed = jnp.zeros(widened.shape[:-1] + (out_width,), jnp.float32)
    for tap_index in range(tap_table.shape[-1]):
        offset_start = 2 * half_span - tap_index
        window = lax.slice_in_dim(
            widened, offset_start, offset_start + out_width, axis=widened.ndim - 1
        )
        summed = summed + tap_table[..., tap_index : tap_index + 1] * window
    return summed


def widened_rims(values):
    half_span = (TAPS - 1) // 2
    return with_halo(values, (("freq", 2),), half_span)


def pack_rows(values, slot_ids, total_slots):
    return jnp.zeros((total_slots, values.shape[-1]), jnp.float32).at[slot_ids].set(values)


def any_device(traces, live_mask, offset_bin, surface, block_owner, point_column, filters):
    shots_here, receivers, quarter = traces.shape
    freq_count = lax.axis_size("freq")
    shot_count = lax.axis_size("shot")
    band_width = NF // freq_count
    rows_here = shots_here * receivers
    bins_total = filters.shape[0] * shot_count
    most_slots = max(2, 3 * rows_here // (2 * bins_total))
    total_slots = bins_total * most_slots
    live_rows = live_mask.astype(jnp.float32)[:, :, None]
    live_traces = traces * live_rows
    columns = point_column.reshape(-1)
    picked = jnp.take(live_traces, columns, axis=1).reshape(shots_here * columns.shape[0], quarter)
    freq_index = lax.axis_index("freq")
    time_ids = freq_index * quarter + jnp.arange(quarter)
    band_ids = freq_index * 2 * band_width + jnp.arange(2 * band_width)
    wave_rows = wave_table(
        time_ids, jnp.arange(2 * band_width * lax.axis_size("freq")), band_width, NT
    )
    spectra = lax.psum_scatter(
        lax.dot_general(wave_rows, picked, (((0,), (1,)), ((), ())), precision=FULL_PRECISION),
        "freq",
        scatter_dimension=0,
        tiled=True,
    )
    spectra = spectra.reshape(2 * band_width, shots_here, columns.shape[0])
    real_sum = jnp.zeros((shots_here, receivers, band_width), jnp.float32)
    imag_sum = jnp.zeros((shots_here, receivers, band_width), jnp.float32)
    for step_index in range(STEPS):
        surface_part = broadcast(surface, "shot", block_owner[step_index])
        point_spectra = spectra[:, :, step_index * POINTS_BLK : (step_index + 1) * POINTS_BLK]
        data_real = point_spectra[:band_width]
        data_imag = point_spectra[band_width:]
        surf_real = surface_part[:, :, :band_width]
        surf_imag = surface_part[:, :, band_width:]
        real_sum = real_sum + (cross_mix(data_real, surf_real) - cross_mix(data_imag, surf_imag))
        imag_sum = imag_sum + (cross_mix(data_real, surf_imag) + cross_mix(data_imag, surf_real))
    prediction = jnp.concatenate([real_sum, imag_sum], axis=2).reshape(rows_here, 2 * band_width)
    inverse = wave_table(jnp.arange(NT), band_ids, band_width, NT).T * (2.0 / NT)
    partial_value = jnp.dot(prediction, inverse, precision=FULL_PRECISION)
    multiples = lax.psum_scatter(partial_value, "freq", scatter_dimension=1, tiled=True)
    multiples = multiples.reshape(shots_here, receivers, quarter) * live_rows
    bins_flat = offset_bin.reshape(rows_here)
    order_ids = jnp.arange(rows_here)
    earlier = (bins_flat[:, None] == bins_flat[None, :]) & (order_ids[None, :] < order_ids[:, None])
    rank_ids = jnp.sum(earlier.astype(jnp.int32), axis=1)
    slot_ids = bins_flat * most_slots + rank_ids
    every_filter = lax.all_gather(filters, "shot", axis=0, tiled=True)
    trace_taps = jnp.take(every_filter, bins_flat, axis=0).reshape(
        shots_here, receivers, every_filter.shape[1]
    )
    widened = widened_rims(multiples)
    cleaned = live_traces - shifted_sum(widened, trace_taps, quarter)
    cleaned_slots = pack_rows(cleaned.reshape(rows_here, quarter), slot_ids, total_slots)
    cleaned_slots = cleaned_slots.reshape(bins_total, most_slots, quarter)
    return lax.all_to_all(cleaned_slots, "shot", split_axis=0, concat_axis=1, tiled=True)


def on_device(traces, live_mask, offset_bin, surface, block_owner, point_column, filters):
    devices = lax.axis_size("shot")
    in_plane = devices == 8 and lax.axis_size("freq") == 4
    whole_tiles = traces.shape[1] % (8 * devices) == 0 and filters.shape[0] + traces.shape[0] <= 8
    plan = plane_device if in_plane and whole_tiles else any_device
    return plan(traces, live_mask, offset_bin, surface, block_owner, point_column, filters)


def solution(mesh):
    return jax.shard_map(
        on_device,
        mesh=mesh,
        in_specs=(
            P("shot", None, "freq"),
            P("shot", None),
            P("shot", None, None),
            P("shot", None, "freq"),
            P(),
            P(),
            P("shot", None),
        ),
        out_specs=P("shot", None, "freq"),
        check_vma=False,
    )
```
